256 devices in a mesh: clip: 64 (over y, x_hi, z), proj: 4 (over x_lo, core).
Axes of the slice: x: 4 (x_hi: 2, x_lo: 2; x = x_hi * 2 + x_lo), y: 4, z: 8, core: 2. Of those that a mesh axis runs over, the one named last changes fastest.
Arguments:
- clip_acts: bfloat16 [512, 64, 768], P(('clip', 'proj')), may hold values from -6 to 6
- clip_cotangents: bfloat16 [512, 64, 768], P(('clip', 'proj')), may hold values from -6 to 6
- weight_in: bfloat16 [768, 3072], replicated, may hold values from -0.21875 to 0.21875
- weight_out: bfloat16 [3072, 768], replicated, may hold values from -0.21875 to 0.21875
- proj_in: bfloat16 [768, 32], replicated, may hold values from -0.21875 to 0.21875
- proj_out: bfloat16 [3072, 32], replicated, may hold values from -0.109375 to 0.109375
- test_grads: bfloat16 [512, 1024], P(('clip', 'proj')), may hold values from -6 to 6
- clip_ids: int32 [512], P(('clip', 'proj')), may hold values from 0 to 1, as said below
Outputs:
- scores: float32 [512, 512], P(('clip', 'proj'))
The draws below stay inside these ranges and needn't reach their ends.
Inputs may be any that keep to these rules, and one draw needn't show every extreme that they name: `clip_ids`: in each aligned block of 2 entries (the clips of one device) every number from 0 to 1 stands once.
All inputs are finite; a program needn't handle non-finite values.
Results may differ from the reference program's by a relative error of at most 0.0065.
Values may be sent and summed in bfloat16 or wider, within the bound.
A program may use at most 128 MiB of HBM per device.

```python
import math
import jax
import jax.numpy as jnp
from jax import lax

D = 768
H = 3072
FRAMES = 64
RIN = 32
ROUT = 32
CPD = 2
R = 1024
NTRAIN = 512
NTEST = 512


def draw_clip_ids(key, part):
    key = jax.random.fold_in(key, 7)
    block_count = NTRAIN // CPD
    random_keys = jax.random.randint(key, (block_count, CPD), 0, 1 << 20)
    distinct = random_keys * CPD + jnp.arange(CPD, dtype=jnp.int32)[None, :]
    ordering = jnp.argsort(distinct, axis=1, stable=True).astype(jnp.int32)
    return ordering.reshape(-1)


def block_levels(key, shape, cuts, low, largest):
    loudness, own = 1.0, jax.random.fold_in(key, 6)
    for dim, parts in cuts:
        steps = jnp.exp(jax.random.uniform(jax.random.fold_in(own, dim), (parts,), jnp.float32, low / len(cuts), largest / len(cuts)))
        loudness = loudness * jnp.repeat(steps, shape[dim] // parts).reshape([-1 if axis == dim else 1 for axis in range(len(shape))])
    return loudness


def bell_draw(rng, dims, deviation, bound, split=(), kind=jnp.bfloat16):
    loudness = block_levels(rng, dims, split, -0.22, 0.18) if split else 1.0
    values = jax.random.normal(rng, dims, jnp.float32) * deviation * loudness
    return jnp.minimum(jnp.maximum(values, -bound), bound).astype(kind)


def setup_inputs(seed: int = 0) -> dict:
    arg_keys = jax.random.split(jax.random.key(seed), 9)
    return {
        "clip_acts": bell_draw(arg_keys[0], (NTRAIN, FRAMES, D), 1.0, 6.0, ((0, 256),)),
        "clip_cotangents": bell_draw(arg_keys[1], (NTRAIN, FRAMES, D), 1.0, 6.0, ((0, 256),)),
        "weight_in": bell_draw(arg_keys[2], (D, H), D ** -0.5, 0.21875),
        "weight_out": bell_draw(arg_keys[3], (H, D), D ** -0.5, 0.21875),
        "proj_in": bell_draw(arg_keys[4], (D, RIN), D ** -0.5, 0.21875),
        "proj_out": bell_draw(arg_keys[5], (H, ROUT), H ** -0.5, 0.109375),
        "test_grads": bell_draw(arg_keys[6], (NTEST, R), 1.0, 6.0, ((0, 256),)),
        "clip_ids": draw_clip_ids(jax.random.fold_in(arg_keys[8], 71), 0),
    }


damp_ratio = 0.1

def gelu_slope(values):
    normal_cdf = 0.5 * (1.0 + jax.scipy.special.erf(values / math.sqrt(2.0)))
    normal_pdf = jnp.exp(-0.5 * values * values) / math.sqrt(2.0 * math.pi)
    return normal_cdf + values * normal_pdf

def reference(clip_acts, clip_cotangents, weight_in, weight_out, proj_in, proj_out, test_grads, clip_ids):
    flattened = clip_acts.reshape(-1, D)
    preact = jnp.dot(flattened.astype(jnp.float32), weight_in.astype(jnp.float32), preferred_element_type=jnp.float32)
    backprop = lax.dot_general(clip_cotangents.reshape(-1, D).astype(jnp.float32), weight_out.astype(jnp.float32), (((1,), (1,)), ((), ())), preferred_element_type=jnp.float32)
    deltas = (backprop * gelu_slope(preact)).astype(jnp.bfloat16)
    left_side = jnp.dot(flattened.astype(jnp.float32), proj_in.astype(jnp.float32), preferred_element_type=jnp.float32).reshape(NTRAIN, FRAMES, RIN)
    right_side = jnp.dot(deltas.astype(jnp.float32), proj_out.astype(jnp.float32), preferred_element_type=jnp.float32).reshape(NTRAIN, FRAMES, ROUT)
    outer = jnp.einsum('ctr,cto->cro', left_side, right_side, precision=lax.Precision.HIGHEST)
    vectors = (outer / math.sqrt(FRAMES)).reshape(NTRAIN, RIN * ROUT).astype(jnp.bfloat16)
    widened = vectors.astype(jnp.float32)
    gram_matrix = jnp.dot(vectors.T.astype(jnp.float32), vectors.astype(jnp.float32), preferred_element_type=jnp.float32) / NTRAIN
    trace_value = jnp.sum(widened * widened) / NTRAIN
    damping = damp_ratio * trace_value / (RIN * ROUT)
    system = gram_matrix + damping * jnp.eye(RIN * ROUT, dtype=jnp.float32)
    factor = jnp.linalg.cholesky(system)
    solved = jax.scipy.linalg.cho_solve((factor, True), test_grads.astype(jnp.float32).T)
    raw = jnp.dot(widened.astype(jnp.float32), solved.astype(jnp.float32), precision=lax.Precision.HIGHEST, preferred_element_type=jnp.float32) / math.sqrt(RIN * ROUT)
    blocks = raw.reshape(NTRAIN // CPD, CPD, NTEST)
    picked = jnp.take_along_axis(blocks, clip_ids.reshape(NTRAIN // CPD, CPD, 1).astype(jnp.int32), axis=1)
    return picked.reshape(NTRAIN, NTEST)
```

```python
import functools
import math

import jax
import jax.numpy as jnp
from jax import lax
from jax.experimental import pallas as pl
from jax.experimental.pallas import tpu as pltpu
from jax.sharding import PartitionSpec as P

MESH = pl.DeviceIdType.MESH
F32, BF16 = jnp.float32, jnp.bfloat16
damp_ratio = 0.1

NY, NX, NZ, XLO = 4, 4, 8, 2
PLANE = NY * NX
TILE = 16
ROWS = 2 * NZ
TOLERANCE = 1e-6
MOST_STEPS = 4096


def gelu_slope(values):
    normal_cdf = 0.5 * (1.0 + jax.scipy.special.erf(values / math.sqrt(2.0)))
    normal_pdf = jnp.exp(-0.5 * values * values) / math.sqrt(2.0 * math.pi)
    return normal_cdf + values * normal_pdf


def my_place():
    clip, proj = lax.axis_index("clip"), lax.axis_index("proj")
    xh = NX // XLO
    y, z = clip // (xh * NZ), lax.rem(clip, NZ)
    x = lax.rem(clip // NZ, xh) * XLO + proj // 2
    return y, x, z, lax.rem(proj, 2)


def device_at(y, x, z, core):
    return {
        "clip": (y * (NX // XLO) + x // XLO) * NZ + z,
        "proj": lax.rem(x, XLO) * 2 + core,
    }


PLANE_STEPS = sorted(
    ((dy, dx) for dy in range(NY) for dx in range(NX) if (dy, dx) != (0, 0)),
    key=lambda s: min(s[0], NY - s[0]) + min(s[1], NX - s[1]),
)


def gather_kernel(
    v_ref, t_ref, v_all, t_all, line, wide, z_send, z_recv, p_send, p_recv, c_send, c_recv
):
    y, x, z, core = my_place()
    other = 1 - core
    chunks = v_all.shape[1] // 128
    half = PLANE * ROWS

    def along_z(d):
        return lax.rem(z + d, NZ)

    def in_plane(step):
        return lax.rem(y + step[0], NY), lax.rem(x + step[1], NX)

    barrier = pltpu.get_barrier_semaphore()
    targets = [device_at(y, x, along_z(d), core) for d in range(1, NZ)]
    targets += [device_at(*in_plane(s), z, core) for s in PLANE_STEPS]
    targets += [device_at(y, x, z, other)]
    for target in targets:
        pl.semaphore_signal(barrier, inc=1, device_id=target, device_id_type=MESH)
    pl.semaphore_wait(barrier, len(targets))

    def rows_of(place, of_core):
        start = of_core * half + (place[0] * NX + place[1]) * ROWS
        return pl.ds(pl.multiple_of(start, ROWS), ROWS)

    def z_copy(a, d, src, slot):
        return pltpu.make_async_remote_copy(
            src_ref=src,
            dst_ref=line.at[a, slot],
            send_sem=z_send.at[a, d - 1],
            recv_sem=z_recv.at[a, d - 1],
            device_id=targets[d - 1],
            device_id_type=MESH,
        )

    def p_copy(a, k, full, place):
        block = full.at[rows_of(place, core)]
        return pltpu.make_async_remote_copy(
            src_ref=block,
            dst_ref=block,
            send_sem=p_send.at[a, k],
            recv_sem=p_recv.at[a, k],
            device_id=targets[NZ - 1 + k],
            device_id_type=MESH,
        )

    def c_copy(a, k, full, place, of_core):
        block = full.at[rows_of(place, of_core)]
        return pltpu.make_async_remote_copy(
            src_ref=block,
            dst_ref=block,
            send_sem=c_send.at[a, k],
            recv_sem=c_recv.at[a, k],
            device_id=targets[-1],
            device_id_type=MESH,
        )

    fulls = (v_all, t_all)
    sources = (v_ref, t_ref)
    for a in range(2):
        for d in range(1, NZ):
            z_copy(a, d, sources[a], z).start()
        line[a, z] = sources[a][...]
    back = [(NY - s[0], NX - s[1]) for s in PLANE_STEPS]
    for a in range(2):
        full = fulls[a]
        for d in range(1, NZ):
            z_copy(a, d, sources[a], lax.rem(z + NZ - d, NZ)).wait_recv()
        wide[...] = line[a].reshape(NZ * TILE, 128).astype(F32)
        mine = rows_of((y, x), core)
        for c in range(chunks):
            full[mine, c * 128 : (c + 1) * 128] = wide[pl.ds(c, ROWS, stride=chunks), :].astype(
                BF16
            )
        for k in range(len(PLANE_STEPS)):
            p_copy(a, k, full, (y, x)).start()
        c_copy(a, 0, full, (y, x), core).start()
    for a in range(2):
        full = fulls[a]
        for k, s in enumerate(back):
            p_copy(a, k, full, in_plane(s)).wait_recv()
            c_copy(a, k + 1, full, in_plane(s), core).start()
    for a in range(2):
        full = fulls[a]
        for k, s in enumerate([(0, 0)] + back):
            c_copy(a, k, full, in_plane(s), other).wait_recv()
        for d in range(1, NZ):
            z_copy(a, d, sources[a], z).wait_send()
        for k, s in enumerate(PLANE_STEPS):
            p_copy(a, k, full, (y, x)).wait_send()
        for k, s in enumerate([(0, 0)] + back):
            c_copy(a, k, full, in_plane(s), core).wait_send()


def gather(v_tile, t_tile, width):
    everyone = 2 * PLANE * ROWS
    steps = len(PLANE_STEPS)
    full = jax.ShapeDtypeStruct((everyone, width), BF16)
    vmem = pl.BlockSpec(memory_space=pltpu.VMEM)
    dma = pltpu.SemaphoreType.DMA
    return pl.pallas_call(
        gather_kernel,
        out_shape=(full, full),
        in_specs=[vmem, vmem],
        out_specs=(vmem, vmem),
        scratch_shapes=[
            pltpu.VMEM((2, NZ, TILE, 128), BF16),
            pltpu.VMEM((NZ * TILE, 128), F32),
            dma((2, NZ - 1)),
            dma((2, NZ - 1)),
            dma((2, steps)),
            dma((2, steps)),
            dma((2, steps + 1)),
            dma((2, steps + 1)),
        ],
        compiler_params=pltpu.CompilerParams(
            collective_id=0, has_side_effects=True, vmem_limit_bytes=32 << 20
        ),
    )(v_tile, t_tile)


def pieces(values):
    first = values.astype(BF16).astype(F32)
    rest = values - first
    second = rest.astype(BF16).astype(F32)
    return first, second, rest - second


def stacked(values):
    first, second, third = pieces(values)
    return jnp.concatenate([first, second, third, jnp.zeros_like(first)], axis=0).astype(BF16)


def unstacked(product):
    return product[0:8] + product[8:16] + product[16:24]


def solve_kernel(ids_ref, v_ref, t_ref, out_ref, k_ref, split_ref):
    y, x, z, core = my_place()
    count, width = v_ref.shape
    gram = lax.dot_general(
        v_ref[...], v_ref[...], (((1,), (1,)), ((), ())), preferred_element_type=F32
    )
    gram = gram / count
    row = lax.broadcasted_iota(jnp.int32, (count, count), 0)
    column = lax.broadcasted_iota(jnp.int32, (count, count), 1)
    diagonal = jnp.sum(jnp.where(row == column, gram, 0.0), axis=0, keepdims=True)
    damping = damp_ratio * jnp.sum(diagonal, axis=1, keepdims=True) / width
    k_ref[...] = gram + jnp.where(row == column, damping, 0.0)
    diagonal = diagonal + damping
    first, second, third = pieces(k_ref[...])
    split_ref[:, 0:count] = first.astype(BF16)
    split_ref[:, count : 2 * count] = second.astype(BF16)
    split_ref[:, 2 * count : 3 * count] = third.astype(BF16)

    def times_system(p):
        product = unstacked(jnp.dot(stacked(p), split_ref[...], preferred_element_type=F32))
        return (
            product[:, 0:count]
            + product[:, count : 2 * count]
            + product[:, 2 * count : 3 * count]
        )

    def inner(a, b):
        return jnp.sum(a * b, axis=1, keepdims=True)

    def ratio(a, b):
        return jnp.where(b > 0.0, a / jnp.where(b > 0.0, b, 1.0), 0.0)

    base = core * (PLANE * ROWS) + (y * NX + x) * ROWS + z * 2
    lane = lax.broadcasted_iota(jnp.int32, (8, count), 1)
    sub = lax.broadcasted_iota(jnp.int32, (8, count), 0)
    wanted = jnp.where(sub == 0, base + ids_ref[0], base + ids_ref[1])
    rhs = jnp.where((lane == wanted) & (sub < 2), 1.0, 0.0)

    scale = 1.0 / diagonal
    zed = rhs * scale
    rz = inner(rhs, zed)
    goal = rz * (TOLERANCE * TOLERANCE)

    def unfinished(state):
        step, _, _, _, rz = state
        return (step < MOST_STEPS) & (jnp.max(rz - goal) > 0.0)

    def advance(state):
        step, sol, res, p, rz = state
        q = times_system(p)
        alpha = ratio(rz, inner(p, q))
        sol = sol + alpha * p
        res = res - alpha * q
        zed = res * scale
        new = inner(res, zed)
        p = zed + ratio(new, rz) * p
        return step + 1, sol, res, p, new

    state = (jnp.int32(0), jnp.zeros_like(rhs), rhs, zed, rz)
    sol = lax.while_loop(unfinished, advance, state)[1]

    mixed = unstacked(jnp.dot(stacked(sol), v_ref[...], preferred_element_type=F32))
    raw = unstacked(
        lax.dot_general(
            stacked(mixed), t_ref[...], (((1,), (1,)), ((), ())), preferred_element_type=F32
        )
    )
    raw = raw / math.sqrt(width)
    t_core, t_rest = row // (PLANE * ROWS), lax.rem(row, PLANE * ROWS)
    t_y, t_x = t_rest // (NX * ROWS), lax.rem(t_rest // ROWS, NX)
    t_z, t_k = lax.rem(t_rest, ROWS) // 2, lax.rem(t_rest, 2)
    goes = ((t_y * (NX // XLO) + t_x // XLO) * NZ + t_z) * (4 * XLO)
    goes = goes + (lax.rem(t_x, XLO) * 2 + t_core) * 2 + t_k
    order = jnp.where(goes == column, 1.0, 0.0).astype(BF16)
    raw = unstacked(jnp.dot(stacked(raw), order, preferred_element_type=F32))
    out_ref[...] = raw[0:2]


def solve(clip_ids, v_all, t_all):
    count = v_all.shape[0]
    vmem = pl.BlockSpec(memory_space=pltpu.VMEM)
    return pl.pallas_call(
        solve_kernel,
        out_shape=jax.ShapeDtypeStruct((2, count), F32),
        in_specs=[pl.BlockSpec(memory_space=pltpu.SMEM), vmem, vmem],
        out_specs=vmem,
        scratch_shapes=[
            pltpu.VMEM((count, count), F32),
            pltpu.VMEM((count, 3 * count), BF16),
        ],
        compiler_params=pltpu.CompilerParams(vmem_limit_bytes=48 << 20),
    )(clip_ids, v_all, t_all)


def body(
    clip_acts, clip_cotangents, weight_in, weight_out, proj_in, proj_out, test_grads, clip_ids
):
    clip_count, frame_count, feature_width = clip_acts.shape
    in_width = proj_in.shape[1]
    out_width = proj_out.shape[1]
    proj_width = in_width * out_width
    flattened = clip_acts.reshape(-1, feature_width)
    preact = jnp.dot(flattened, weight_in, preferred_element_type=F32)
    backprop = lax.dot_general(
        clip_cotangents.reshape(-1, feature_width),
        weight_out,
        (((1,), (1,)), ((), ())),
        preferred_element_type=F32,
    )
    deltas = (backprop * gelu_slope(preact)).astype(BF16)
    left_side = jnp.dot(flattened, proj_in, preferred_element_type=F32).reshape(
        clip_count, frame_count, in_width
    )
    right_side = jnp.dot(deltas, proj_out, preferred_element_type=F32).reshape(
        clip_count, frame_count, out_width
    )
    outer = jnp.einsum("ctr,cto->cro", left_side, right_side, precision=lax.Precision.HIGHEST)
    vectors = (outer / math.sqrt(frame_count)).astype(BF16)
    v_all, t_all = gather(
        vectors.reshape(TILE, 128), test_grads.reshape(TILE, 128), proj_width
    )
    return solve(clip_ids, v_all, t_all)


def solution(mesh):
    in_specs = (
        P(("clip", "proj"), None, None),
        P(("clip", "proj"), None, None),
        P(),
        P(),
        P(),
        P(),
        P(("clip", "proj"), None),
        P(("clip", "proj")),
    )
    out_specs = P(("clip", "proj"), None)
    return jax.shard_map(body, mesh=mesh, in_specs=in_specs, out_specs=out_specs, check_vma=False)
```

```python
import functools
import math

import jax
import jax.numpy as jnp
from jax import lax
from jax.experimental import pallas as pl
from jax.experimental.pallas import tpu as pltpu
from jax.sharding import PartitionSpec as P

MESH = pl.DeviceIdType.MESH
F32, BF16 = jnp.float32, jnp.bfloat16
damp_ratio = 0.1

NY, NX, NZ, XLO = 4, 4, 8, 2
PLANE = NY * NX
TILE = 16
ROWS = 2 * NZ
HALF = PLANE * ROWS
PARTS = 6
DOUBLINGS = 4
REFINEMENTS = 3
MOST_STEPS = 4096
LAST_BITS = 2.0**-22

PLANE_STEPS = sorted(
    ((dy, dx) for dy in range(NY) for dx in range(NX) if (dy, dx) != (0, 0)),
    key=lambda s: min(s[0], NY - s[0]) + min(s[1], NX - s[1]),
)
STEPS = len(PLANE_STEPS)
BACK = [(NY - s[0], NX - s[1]) for s in PLANE_STEPS]


def gelu_slope(values):
    normal_cdf = 0.5 * (1.0 + lax.erf(values * math.sqrt(0.5)))
    normal_pdf = jnp.exp(-0.5 * values * values) * (1.0 / math.sqrt(2.0 * math.pi))
    return normal_cdf + values * normal_pdf


def my_place():
    clip, proj = lax.axis_index("clip"), lax.axis_index("proj")
    xh = NX // XLO
    y, z = clip // (xh * NZ), lax.rem(clip, NZ)
    x = lax.rem(clip // NZ, xh) * XLO + proj // 2
    return y, x, z, lax.rem(proj, 2)


def device_at(y, x, z, core):
    return {
        "clip": (y * (NX // XLO) + x // XLO) * NZ + z,
        "proj": lax.rem(x, XLO) * 2 + core,
    }


def mm(a, b):
    return jnp.dot(a, b, preferred_element_type=F32)


def mm_t(a, b):
    return lax.dot_general(a, b, (((1,), (1,)), ((), ())), preferred_element_type=F32)


def pieces(values):
    first = values.astype(BF16).astype(F32)
    rest = values - first
    second = rest.astype(BF16).astype(F32)
    return first, second, rest - second


def stacked(values):
    first, second, third = pieces(values)
    return jnp.concatenate([first, second, third, jnp.zeros_like(first)], axis=0).astype(BF16)


def unstacked(product):
    return product[0:8] + product[8:16] + product[16:24]


def iota(shape, axis):
    return lax.broadcasted_iota(jnp.int32, shape, axis)


def inner(a, b):
    return jnp.sum(a * b, axis=1, keepdims=True)


def spread(ref, values):
    chunks = values.shape[1] // 128
    for c in range(chunks):
        ref[pl.ds(c, 2, stride=chunks), :] = values[:, c * 128 : (c + 1) * 128]
    return ref[...].astype(BF16)


def left_pieces(acts, proj_in):
    tokens, width = acts.shape[0], proj_in.shape[1]
    r, c = iota((width, 128), 0), iota((width, 128), 1)
    groups = 128 // width
    per = width // groups
    chosen = (c < width) & (r == lax.rem(c, per) * groups + c // per)
    ordered = mm(proj_in, jnp.where(chosen, 1.0, 0.0).astype(BF16)).astype(BF16)
    left = jnp.transpose(mm(acts, ordered))
    half = tokens // 2
    rows = []
    for k in range(2):
        lane = iota((per, tokens), 1)
        own = (lane >= k * half) & (lane < (k + 1) * half)
        row = [jnp.where(own, left[j * per : (j + 1) * per], 0.0) for j in range(groups)]
        rows.append(jnp.concatenate(row, axis=1))
    return jnp.concatenate(pieces(jnp.concatenate(rows, axis=0)), axis=0).astype(BF16)


def outer_tile(left, right, in_width):
    width = right.shape[1]
    groups = 128 // width
    wide = jnp.concatenate([right] * groups, axis=1)
    lane = iota(wide.shape, 1) // width
    stack = []
    for piece in pieces(wide):
        masked = [jnp.where(lane == j, piece, 0.0) for j in range(groups)]
        stack.append(jnp.concatenate(masked, axis=0).astype(BF16))
    product = mm(left, jnp.concatenate(stack, axis=1))
    total = None
    for i in (2, 1, 0):
        for j in (2, 1, 0):
            term = product[i * TILE : (i + 1) * TILE, j * 128 : (j + 1) * 128]
            total = term if total is None else total + term
    return total


def target_order(shape):
    j = iota((1, shape[1]), 1)
    k, core = lax.rem(j, 2), lax.rem(j // 2, 2)
    x_lo, z = lax.rem(j // 4, XLO), lax.rem(j // (4 * XLO), NZ)
    rest = j // (4 * XLO * NZ)
    x_hi, y = lax.rem(rest, NX // XLO), rest // (NX // XLO)
    source = core * HALF + (y * NX + x_hi * XLO + x_lo) * ROWS + z * 2 + k
    return jnp.where(iota(shape, 0) == source, 1.0, 0.0).astype(BF16)


def wanted_rows(ids_ref, count):
    y, x, z, core = my_place()
    base = core * HALF + (y * NX + x) * ROWS + z * 2
    lane, sub = iota((8, count), 1), iota((8, count), 0)
    wanted = jnp.where(sub == 0, base + ids_ref[0], base + ids_ref[1])
    return jnp.where((lane == wanted) & (sub < 2), 1.0, 0.0)


def form_system(v, split_ref):
    count, width = v.shape
    gram = mm_t(v, v) * (1.0 / count)
    eye = iota((count, count), 0) == iota((count, count), 1)
    diagonal = jnp.sum(jnp.where(eye, gram, 0.0), axis=0, keepdims=True)
    damping = damp_ratio * jnp.sum(diagonal, axis=1, keepdims=True) / width
    system = gram + jnp.where(eye, damping, 0.0)
    for i, piece in enumerate(pieces(system)):
        split_ref[:, i * count : (i + 1) * count] = piece.astype(BF16)
    return system, damping, diagonal + damping, eye


def times_system(p, split_ref):
    count = split_ref.shape[0]
    product = unstacked(mm(stacked(p), split_ref[...]))
    return (
        product[:, 0:count] + product[:, count : 2 * count] + product[:, 2 * count : 3 * count]
    )


def scores_of(sol, v, t):
    mixed = unstacked(mm(stacked(sol), v))
    raw = unstacked(mm_t(stacked(mixed), t)) * (1.0 / math.sqrt(v.shape[1]))
    return unstacked(mm(stacked(raw), target_order((t.shape[0], t.shape[0]))))


def refined(ids_ref, v, split_ref, m_ref):
    count = v.shape[0]
    system, low, _, eye = form_system(v, split_ref)
    high = split_ref[:, 0:count]
    square = mm(high, high)
    top = jnp.max(jnp.sum(jnp.abs(square), axis=0, keepdims=True), axis=1, keepdims=True)
    top = jnp.sqrt(top) * 1.02
    centre = 2.0 / (top + low)
    t = (top + low) / (top - low)
    t2 = 2.0 * t * t - 1.0
    c = 2.0 * t * t / t2 * centre
    m = jnp.where(eye, 2.0 * c, 0.0) - (c * centre) * system
    am = (2.0 * c) * system - (c * centre) * square
    for i in range(DOUBLINGS):
        t = t2
        t2 = 2.0 * t * t - 1.0
        c = 2.0 * t * t / t2
        rounded = m.astype(BF16)
        if i > 0:
            am = mm(high, rounded)
        m = c * (2.0 * m - mm(rounded, am.astype(BF16)))
    m_ref[...] = m.astype(BF16)

    rhs = wanted_rows(ids_ref, count)

    def precondition(r):
        return mm(jnp.concatenate([r, jnp.zeros_like(r)], axis=0).astype(BF16), m_ref[...])[0:8]

    sol = precondition(rhs)
    res = rhs - times_system(sol, split_ref)
    for _ in range(REFINEMENTS):
        sol = sol + precondition(res)
        res = rhs - times_system(sol, split_ref)
    excess = inner(res, res) - (LAST_BITS * top) * (LAST_BITS * top) * inner(sol, sol)
    return sol, excess


def main_kernel(
    ids_ref, acts_hbm, cot_hbm, w_in_hbm, w_out_hbm, proj_in_hbm, proj_out_hbm, t_ref,
    raw_ref, check_ref, v_out, t_out,
    acts, cot, w_in, w_out, proj_in, proj_out, v_all, t_all, tiles, line, wide, split_ref, m_ref,
    load_sem, in_sem, out_sem, store_sem, z_send, z_recv, p_send, p_recv, c_send, c_recv,
):
    y, x, z, core = my_place()
    other = 1 - core
    chunks = v_all.shape[1] // 128
    block = w_in.shape[1] // PARTS
    tokens = acts.shape[0] * acts.shape[1]

    small = [
        pltpu.make_async_copy(src, dst, load_sem.at[i])
        for i, (src, dst) in enumerate(
            ((acts_hbm, acts), (proj_in_hbm, proj_in), (cot_hbm, cot), (proj_out_hbm, proj_out))
        )
    ]
    loads_in, loads_out = [], []
    for i in range(PARTS):
        part = pl.ds(i * block, block)
        loads_in.append(
            pltpu.make_async_copy(w_in_hbm.at[:, part], w_in.at[:, part], in_sem.at[i])
        )
        loads_out.append(
            pltpu.make_async_copy(w_out_hbm.at[part], w_out.at[part], out_sem.at[i])
        )
    small[0].start()
    small[1].start()
    loads_in[0].start()
    small[2].start()
    loads_out[0].start()
    small[3].start()
    for i in range(1, PARTS):
        loads_in[i].start()
        loads_out[i].start()

    def along_z(d):
        return lax.rem(z + d, NZ)

    def in_plane(step):
        return lax.rem(y + step[0], NY), lax.rem(x + step[1], NX)

    barrier = pltpu.get_barrier_semaphore()
    targets = [device_at(y, x, along_z(d), core) for d in range(1, NZ)]
    targets += [device_at(*in_plane(s), z, core) for s in PLANE_STEPS]
    targets += [device_at(y, x, z, other)]
    for target in targets:
        pl.semaphore_signal(barrier, inc=1, device_id=target, device_id_type=MESH)

    def rows_of(place, of_core):
        start = of_core * HALF + (place[0] * NX + place[1]) * ROWS
        return pl.ds(pl.multiple_of(start, ROWS), ROWS)

    def z_copy(a, d, slot):
        return pltpu.make_async_remote_copy(
            src_ref=tiles.at[a],
            dst_ref=line.at[a, slot],
            send_sem=z_send.at[a, d - 1],
            recv_sem=z_recv.at[a, d - 1],
            device_id=targets[d - 1],
            device_id_type=MESH,
        )

    fulls = (v_all, t_all)

    def p_copy(a, k, place):
        rows = fulls[a].at[rows_of(place, core)]
        return pltpu.make_async_remote_copy(
            src_ref=rows,
            dst_ref=rows,
            send_sem=p_send.at[a, k],
            recv_sem=p_recv.at[a, k],
            device_id=targets[NZ - 1 + k],
            device_id_type=MESH,
        )

    def c_copy(a, k, place, of_core):
        rows = fulls[a].at[rows_of(place, of_core)]
        return pltpu.make_async_remote_copy(
            src_ref=rows,
            dst_ref=rows,
            send_sem=c_send.at[a, k],
            recv_sem=c_recv.at[a, k],
            device_id=targets[-1],
            device_id_type=MESH,
        )

    def start_line(a, tile):
        tiles[a] = tile
        for d in range(1, NZ):
            z_copy(a, d, z).start()
        line[a, z] = tile

    def start_plane(a):
        for d in range(1, NZ):
            z_copy(a, d, lax.rem(z + NZ - d, NZ)).wait_recv()
        wide[...] = line[a].reshape(NZ * TILE, 128).astype(F32)
        mine = rows_of((y, x), core)
        for c in range(chunks):
            fulls[a][mine, c * 128 : (c + 1) * 128] = wide[
                pl.ds(c, ROWS, stride=chunks), :
            ].astype(BF16)
        for k in range(STEPS):
            p_copy(a, k, (y, x)).start()
        c_copy(a, 0, (y, x), core).start()

    def forward(a):
        for k, s in enumerate(BACK):
            p_copy(a, k, in_plane(s)).wait_recv()
            c_copy(a, k + 1, in_plane(s), core).start()

    def finish(a):
        for k, s in enumerate([(0, 0)] + BACK):
            c_copy(a, k, in_plane(s), other).wait_recv()

    def settle(a):
        for d in range(1, NZ):
            z_copy(a, d, z).wait_send()
        for k in range(STEPS):
            p_copy(a, k, (y, x)).wait_send()
        for k, s in enumerate([(0, 0)] + BACK):
            c_copy(a, k, in_plane(s), core).wait_send()

    t_tile = spread(wide.at[pl.ds(0, TILE)], t_ref[...].astype(F32))
    pl.semaphore_wait(barrier, len(targets))
    start_line(1, t_tile)

    small[0].wait()
    small[1].wait()
    left = left_pieces(acts[...].reshape(tokens, -1), proj_in[...])
    small[2].wait()
    small[3].wait()
    right = None
    for i in range(PARTS):
        loads_in[i].wait()
        loads_out[i].wait()
        part = slice(i * block, (i + 1) * block)
        preact = mm(acts[...].reshape(tokens, -1), w_in[:, part])
        backprop = mm_t(cot[...].reshape(tokens, -1), w_out[part])
        deltas = (backprop * gelu_slope(preact)).astype(BF16)
        term = mm(deltas, proj_out[part])
        right = term if right is None else right + term
        if i == 1:
            start_plane(1)
    outer = outer_tile(left, right, proj_in.shape[1])
    start_line(0, (outer * (1.0 / math.sqrt(acts.shape[1]))).astype(BF16))
    forward(1)
    start_plane(0)
    finish(1)
    store_t = pltpu.make_async_copy(t_all, t_out, store_sem.at[1])
    store_t.start()
    forward(0)
    finish(0)
    store_v = pltpu.make_async_copy(v_all, v_out, store_sem.at[0])
    store_v.start()

    sol, excess = refined(ids_ref, v_all[...], split_ref, m_ref)
    raw_ref[...] = scores_of(sol, v_all[...], t_all[...])
    check_ref[...] = jnp.broadcast_to(excess, check_ref.shape)
    settle(1)
    settle(0)
    store_t.wait()
    store_v.wait()


def finish_kernel(ids_ref, raw_ref, check_ref, v_hbm, t_hbm, out_ref, v_ref, t_ref, split_ref, sem):
    out_ref[...] = raw_ref[0:2]
    excess = check_ref[...]
    fine = jnp.min(jnp.where(excess <= 0.0, 1.0, 0.0))

    @pl.when(fine < 1.0)
    def _():
        loads = [
            pltpu.make_async_copy(v_hbm, v_ref, sem.at[0]),
            pltpu.make_async_copy(t_hbm, t_ref, sem.at[1]),
        ]
        for load in loads:
            load.start()
        for load in loads:
            load.wait()
        count = v_ref.shape[0]
        _, _, diagonal, _ = form_system(v_ref[...], split_ref)
        rhs = wanted_rows(ids_ref, count)
        scale = 1.0 / diagonal

        def ratio(a, b):
            return jnp.where(b > 0.0, a / jnp.where(b > 0.0, b, 1.0), 0.0)

        def unfinished(state):
            step, _, _, _, rz = state
            return (step < MOST_STEPS) & (jnp.max(rz - goal) > 0.0)

        def advance(state):
            step, sol, res, p, rz = state
            q = times_system(p, split_ref)
            alpha = ratio(rz, inner(p, q))
            sol = sol + alpha * p
            res = res - alpha * q
            zed = res * scale
            new = inner(res, zed)
            p = zed + ratio(new, rz) * p
            return step + 1, sol, res, p, new

        zed = rhs * scale
        rz = inner(rhs, zed)
        goal = rz * 1e-12
        state = (jnp.int32(0), jnp.zeros_like(rhs), rhs, zed, rz)
        sol = lax.while_loop(unfinished, advance, state)[1]
        out_ref[...] = scores_of(sol, v_ref[...], t_ref[...])[0:2]


def body(
    clip_acts, clip_cotangents, weight_in, weight_out, proj_in, proj_out, test_grads, clip_ids
):
    width = proj_in.shape[1] * proj_out.shape[1]
    count = 2 * HALF
    full = jax.ShapeDtypeStruct((count, width), BF16)
    vmem = pl.BlockSpec(memory_space=pltpu.VMEM)
    smem = pl.BlockSpec(memory_space=pltpu.SMEM)
    hbm = pl.BlockSpec(memory_space=pl.ANY)
    dma = pltpu.SemaphoreType.DMA

    def like(array):
        return pltpu.VMEM(array.shape, array.dtype)

    raw, check, v_all, t_all = pl.pallas_call(
        main_kernel,
        out_shape=(
            jax.ShapeDtypeStruct((8, count), F32),
            jax.ShapeDtypeStruct((8, 128), F32),
            full,
            full,
        ),
        in_specs=[smem] + [hbm] * 6 + [vmem],
        out_specs=(vmem, vmem, hbm, hbm),
        scratch_shapes=[
            like(clip_acts),
            like(clip_cotangents),
            like(weight_in),
            like(weight_out),
            like(proj_in),
            like(proj_out),
            like(full),
            like(full),
            pltpu.VMEM((2, TILE, 128), BF16),
            pltpu.VMEM((2, NZ, TILE, 128), BF16),
            pltpu.VMEM((NZ * TILE, 128), F32),
            pltpu.VMEM((count, 3 * count), BF16),
            pltpu.VMEM((count, count), BF16),
            dma((4,)),
            dma((PARTS,)),
            dma((PARTS,)),
            dma((2,)),
            dma((2, NZ - 1)),
            dma((2, NZ - 1)),
            dma((2, STEPS)),
            dma((2, STEPS)),
            dma((2, STEPS + 1)),
            dma((2, STEPS + 1)),
        ],
        compiler_params=pltpu.CompilerParams(
            collective_id=0, has_side_effects=True, vmem_limit_bytes=56 << 20
        ),
    )(
        clip_ids,
        clip_acts,
        clip_cotangents,
        weight_in,
        weight_out,
        proj_in,
        proj_out,
        test_grads,
    )
    return pl.pallas_call(
        finish_kernel,
        out_shape=jax.ShapeDtypeStruct((2, count), F32),
        in_specs=[smem, vmem, vmem, hbm, hbm],
        out_specs=vmem,
        scratch_shapes=[
            like(full),
            like(full),
            pltpu.VMEM((count, 3 * count), BF16),
            dma((2,)),
        ],
        compiler_params=pltpu.CompilerParams(vmem_limit_bytes=56 << 20),
    )(clip_ids, raw, check, v_all, t_all)


def solution(mesh):
    in_specs = (
        P(("clip", "proj"), None, None),
        P(("clip", "proj"), None, None),
        P(),
        P(),
        P(),
        P(),
        P(("clip", "proj"), None),
        P(("clip", "proj")),
    )
    out_specs = P(("clip", "proj"), None)
    return jax.shard_map(body, mesh=mesh, in_specs=in_specs, out_specs=out_specs, check_vma=False)
```

```python
import functools
import math

import jax
import jax.numpy as jnp
from jax import lax
from jax.experimental import pallas as pl
from jax.experimental.pallas import tpu as pltpu
from jax.sharding import PartitionSpec as P

MESH = pl.DeviceIdType.MESH
F32, BF16 = jnp.float32, jnp.bfloat16
damp_ratio = 0.1

NY, NX, NZ, XLO = 4, 4, 8, 2
PLANE = NY * NX
TILE = 16
ROWS = 2 * NZ
HALF = PLANE * ROWS
PARTS = 2
DOUBLINGS = 4
REFINEMENTS = 3
MOST_STEPS = 4096
LAST_BITS = 2.0**-22

PLANE_STEPS = sorted(
    ((dy, dx) for dy in range(NY) for dx in range(NX) if (dy, dx) != (0, 0)),
    key=lambda s: min(s[0], NY - s[0]) + min(s[1], NX - s[1]),
)
STEPS = len(PLANE_STEPS)


def gelu_slope(values):
    normal_cdf = 0.5 * (1.0 + lax.erf(values * math.sqrt(0.5)))
    normal_pdf = jnp.exp(-0.5 * values * values) * (1.0 / math.sqrt(2.0 * math.pi))
    return normal_cdf + values * normal_pdf


def my_place():
    clip, proj = lax.axis_index("clip"), lax.axis_index("proj")
    xh = NX // XLO
    y, z = clip // (xh * NZ), lax.rem(clip, NZ)
    x = lax.rem(clip // NZ, xh) * XLO + proj // 2
    return y, x, z, lax.rem(proj, 2)


def device_at(y, x, z, core):
    return {
        "clip": (y * (NX // XLO) + x // XLO) * NZ + z,
        "proj": lax.rem(x, XLO) * 2 + core,
    }


def mm(a, b):
    return jnp.dot(a, b, preferred_element_type=F32)


def mm_t(a, b):
    return lax.dot_general(a, b, (((1,), (1,)), ((), ())), preferred_element_type=F32)


def pieces(values):
    first = values.astype(BF16).astype(F32)
    rest = values - first
    second = rest.astype(BF16).astype(F32)
    return first, second, rest - second


def stacked(values):
    first, second, third = pieces(values)
    return jnp.concatenate([first, second, third, jnp.zeros_like(first)], axis=0).astype(BF16)


def unstacked(product):
    return product[0:8] + product[8:16] + product[16:24]


def iota(shape, axis):
    return lax.broadcasted_iota(jnp.int32, shape, axis)


def inner(a, b):
    return jnp.sum(a * b, axis=1, keepdims=True)


def spread(ref, values):
    chunks = values.shape[1] // 128
    for c in range(chunks):
        ref[pl.ds(c, 2, stride=chunks), :] = values[:, c * 128 : (c + 1) * 128]
    return ref[...].astype(BF16)


def left_pieces(acts, proj_in):
    tokens, width = acts.shape[0], proj_in.shape[0]
    groups = 128 // width
    per = width // groups
    r, c = iota((128, width), 1), iota((128, width), 0)
    chosen = (c < width) & (r == lax.rem(c, per) * groups + c // per)
    ordered = mm(jnp.where(chosen, 1.0, 0.0).astype(BF16), proj_in).astype(BF16)
    left = mm_t(ordered, acts)
    half = tokens // 2
    rows = []
    for k in range(2):
        lane = iota((per, tokens), 1)
        own = (lane >= k * half) & (lane < (k + 1) * half)
        row = [jnp.where(own, left[j * per : (j + 1) * per], 0.0) for j in range(groups)]
        rows.append(jnp.concatenate(row, axis=1))
    return jnp.concatenate(pieces(jnp.concatenate(rows, axis=0)), axis=0).astype(BF16)


def outer_tile(left, right, in_width):
    width = right.shape[1]
    groups = 128 // width
    wide = jnp.concatenate([right] * groups, axis=1)
    lane = iota(wide.shape, 1) // width
    stack = []
    for piece in pieces(wide):
        masked = [jnp.where(lane == j, piece, 0.0) for j in range(groups)]
        stack.append(jnp.concatenate(masked, axis=0).astype(BF16))
    product = mm(left, jnp.concatenate(stack, axis=1))
    total = None
    for i in (2, 1, 0):
        for j in (2, 1, 0):
            term = product[i * TILE : (i + 1) * TILE, j * 128 : (j + 1) * 128]
            total = term if total is None else total + term
    return total


def target_order(shape):
    j = iota((1, shape[1]), 1)
    k, core = lax.rem(j, 2), lax.rem(j // 2, 2)
    x_lo, z = lax.rem(j // 4, XLO), lax.rem(j // (4 * XLO), NZ)
    rest = j // (4 * XLO * NZ)
    x_hi, y = lax.rem(rest, NX // XLO), rest // (NX // XLO)
    source = core * HALF + (y * NX + x_hi * XLO + x_lo) * ROWS + z * 2 + k
    return jnp.where(iota(shape, 0) == source, 1.0, 0.0).astype(BF16)


def wanted_rows(ids_ref, count):
    y, x, z, core = my_place()
    base = core * HALF + (y * NX + x) * ROWS + z * 2
    lane, sub = iota((8, count), 1), iota((8, count), 0)
    wanted = jnp.where(sub == 0, base + ids_ref[0], base + ids_ref[1])
    return jnp.where((lane == wanted) & (sub < 2), 1.0, 0.0)


def form_system(v, split_ref):
    count, width = v.shape
    gram = mm_t(v, v) * (1.0 / count)
    eye = iota((count, count), 0) == iota((count, count), 1)
    diagonal = jnp.sum(jnp.where(eye, gram, 0.0), axis=0, keepdims=True)
    damping = damp_ratio * jnp.sum(diagonal, axis=1, keepdims=True) / width
    system = gram + jnp.where(eye, damping, 0.0)
    for i, piece in enumerate(pieces(system)):
        split_ref[:, i * count : (i + 1) * count] = piece.astype(BF16)
    return system, damping, diagonal + damping, eye


def times_system(p, split_ref):
    count = split_ref.shape[0]
    product = unstacked(mm(stacked(p), split_ref[...]))
    return (
        product[:, 0:count] + product[:, count : 2 * count] + product[:, 2 * count : 3 * count]
    )


def scores_of(sol, v, t):
    mixed = unstacked(mm(stacked(sol), v))
    raw = unstacked(mm_t(stacked(mixed), t)) * (1.0 / math.sqrt(v.shape[1]))
    return unstacked(mm(stacked(raw), target_order((t.shape[0], t.shape[0]))))


def refined(ids_ref, v, split_ref, m_ref):
    count = v.shape[0]
    system, low, _, eye = form_system(v, split_ref)
    high = split_ref[:, 0:count]
    square = mm(high, high)
    top = jnp.max(jnp.sum(jnp.abs(square), axis=0, keepdims=True), axis=1, keepdims=True)
    top = jnp.sqrt(top) * 1.02
    centre = 2.0 / (top + low)
    t = (top + low) / (top - low)
    t2 = 2.0 * t * t - 1.0
    c = 2.0 * t * t / t2 * centre
    m = jnp.where(eye, 2.0 * c, 0.0) - (c * centre) * system
    am = (2.0 * c) * system - (c * centre) * square
    for i in range(DOUBLINGS):
        t = t2
        t2 = 2.0 * t * t - 1.0
        c = 2.0 * t * t / t2
        rounded = m.astype(BF16)
        if i > 0:
            am = mm(high, rounded)
        m = c * (2.0 * m - mm(rounded, am.astype(BF16)))
    m_ref[...] = m.astype(BF16)

    rhs = wanted_rows(ids_ref, count)

    def precondition(r):
        return mm(jnp.concatenate([r, jnp.zeros_like(r)], axis=0).astype(BF16), m_ref[...])[0:8]

    sol = precondition(rhs)
    res = rhs - times_system(sol, split_ref)
    for _ in range(REFINEMENTS):
        sol = sol + precondition(res)
        res = rhs - times_system(sol, split_ref)
    excess = inner(res, res) - (LAST_BITS * top) * (LAST_BITS * top) * inner(sol, sol)
    return sol, excess


def main_kernel(
    ids_ref, acts_hbm, cot_hbm, w_in_hbm, w_out_hbm, proj_in_hbm, proj_out_hbm, t_ref,
    raw_ref, check_ref, v_out, t_out,
    acts, cot, w_in, w_out, proj_in, proj_out, v_all, t_all, tiles, line, wide, split_ref, m_ref,
    load_sem, in_sem, out_sem, store_sem, z_send, z_recv, p_send, p_recv, c_send, c_recv,
):
    y, x, z, core = my_place()
    other = 1 - core
    chunks = v_all.shape[-1] // 128
    block = w_in.shape[1] // PARTS
    tokens = acts.shape[0] * acts.shape[1]

    small = [
        pltpu.make_async_copy(src, dst, load_sem.at[i])
        for i, (src, dst) in enumerate(
            ((acts_hbm, acts), (proj_in_hbm, proj_in), (cot_hbm, cot), (proj_out_hbm, proj_out))
        )
    ]
    loads_in, loads_out = [], []
    for i in range(PARTS):
        part = pl.ds(i * block, block)
        loads_in.append(
            pltpu.make_async_copy(w_in_hbm.at[:, part], w_in.at[:, part], in_sem.at[i])
        )
        loads_out.append(
            pltpu.make_async_copy(w_out_hbm.at[part], w_out.at[part], out_sem.at[i])
        )
    small[0].start()
    small[1].start()
    loads_in[0].start()
    small[2].start()
    loads_out[0].start()
    small[3].start()
    for i in range(1, PARTS):
        loads_in[i].start()
        loads_out[i].start()

    def along_z(d):
        return lax.rem(z + d, NZ)

    def in_plane(step):
        return lax.rem(y + step[0], NY), lax.rem(x + step[1], NX)

    barrier = pltpu.get_barrier_semaphore()
    targets = [device_at(y, x, along_z(d), core) for d in range(1, NZ)]
    targets += [device_at(*in_plane(s), z, core) for s in PLANE_STEPS]
    targets += [device_at(y, x, z, other)]
    for target in targets:
        pl.semaphore_signal(barrier, inc=1, device_id=target, device_id_type=MESH)

    fulls = (v_all, t_all)
    mine = y * NX + x

    def z_copy(a, d):
        return pltpu.make_async_remote_copy(
            src_ref=tiles.at[a],
            dst_ref=line.at[a, z],
            send_sem=z_send.at[a],
            recv_sem=z_recv.at[a],
            device_id=targets[d - 1],
            device_id_type=MESH,
        )

    def p_copy(a, k):
        step = PLANE_STEPS[k]
        rows = fulls[a].at[core, mine]
        group = step[0] if a == 0 else NY
        return pltpu.make_async_remote_copy(
            src_ref=rows,
            dst_ref=rows,
            send_sem=p_send.at[a],
            recv_sem=p_recv.at[group],
            device_id=targets[NZ - 1 + k],
            device_id_type=MESH,
        )

    def c_copy(i, src, dst):
        return pltpu.make_async_remote_copy(
            src_ref=src,
            dst_ref=dst,
            send_sem=c_send.at[i],
            recv_sem=c_recv.at[i],
            device_id=targets[-1],
            device_id_type=MESH,
        )

    def arrived(ref, sem):
        pltpu.make_async_copy(ref, ref, sem).wait()

    def start_line(a, tile):
        tiles[a] = tile
        for d in range(1, NZ):
            z_copy(a, d).start()
        line[a, z] = tile

    def start_plane(a):
        arrived(line.at[a, pl.ds(0, NZ - 1)], z_recv.at[a])
        wide[...] = line[a].reshape(NZ * TILE, 128).astype(F32)
        for c in range(chunks):
            fulls[a][core, mine, :, c * 128 : (c + 1) * 128] = wide[
                pl.ds(c, ROWS, stride=chunks), :
            ].astype(BF16)
        for k in range(STEPS):
            p_copy(a, k).start()

    t_tile = spread(wide.at[pl.ds(0, TILE)], t_ref[...].astype(F32))
    pl.semaphore_wait(barrier, len(targets))
    start_line(1, t_tile)

    small[0].wait()
    small[1].wait()
    left = left_pieces(acts[...].reshape(tokens, -1), proj_in[...])
    small[2].wait()
    small[3].wait()
    right = None
    for i in range(PARTS):
        loads_in[i].wait()
        loads_out[i].wait()
        part = slice(i * block, (i + 1) * block)
        preact = mm(acts[...].reshape(tokens, -1), w_in[:, part])
        backprop = mm_t(cot[...].reshape(tokens, -1), w_out[part])
        deltas = (backprop * gelu_slope(preact)).astype(BF16)
        term = mm_t(deltas, proj_out[:, part])
        right = term if right is None else right + term
        if i == 0:
            start_plane(1)
    outer = outer_tile(left, right, proj_in.shape[0])
    start_line(0, (outer * (1.0 / math.sqrt(acts.shape[1]))).astype(BF16))
    start_plane(0)

    arrived(t_all.at[core, pl.ds(0, STEPS)], p_recv.at[NY])
    t_copy = c_copy(NY, t_all.at[core], t_all.at[core])
    t_copy.start()
    v_copies = []
    for i in range(NY):
        first = lax.rem(y + NY - i, NY) * NX
        arrived(v_all.at[core, pl.ds(first, NX - (i == 0))], p_recv.at[i])
        rows = v_all.at[core, pl.ds(first, NX)]
        v_copies.append(c_copy(i, rows, rows))
        v_copies[-1].start()
    t_copy.wait_recv()
    store_t = pltpu.make_async_copy(t_all, t_out, store_sem.at[1])
    store_t.start()
    for copy in v_copies:
        copy.wait_recv()
    store_v = pltpu.make_async_copy(v_all, v_out, store_sem.at[0])
    store_v.start()

    v = v_all[...].reshape(2 * HALF, -1)
    sol, excess = refined(ids_ref, v, split_ref, m_ref)
    raw_ref[...] = scores_of(sol, v, t_all[...].reshape(2 * HALF, -1))
    check_ref[...] = jnp.broadcast_to(excess, check_ref.shape)
    for a in range(2):
        arrived(line.at[a, pl.ds(0, NZ - 1)], z_send.at[a])
        arrived(fulls[a].at[core, pl.ds(0, STEPS)], p_send.at[a])
    t_copy.wait_send()
    for copy in v_copies:
        copy.wait_send()
    store_t.wait()
    store_v.wait()


def finish_kernel(ids_ref, raw_ref, check_ref, v_hbm, t_hbm, out_ref, v_ref, t_ref, split_ref, sem):
    out_ref[...] = raw_ref[0:2]
    excess = check_ref[...]
    fine = jnp.min(jnp.where(excess <= 0.0, 1.0, 0.0))

    @pl.when(fine < 1.0)
    def _():
        loads = [
            pltpu.make_async_copy(v_hbm, v_ref, sem.at[0]),
            pltpu.make_async_copy(t_hbm, t_ref, sem.at[1]),
        ]
        for load in loads:
            load.start()
        for load in loads:
            load.wait()
        count = 2 * HALF
        v, t = v_ref[...].reshape(count, -1), t_ref[...].reshape(count, -1)
        _, _, diagonal, _ = form_system(v, split_ref)
        rhs = wanted_rows(ids_ref, count)
        scale = 1.0 / diagonal

        def ratio(a, b):
            return jnp.where(b > 0.0, a / jnp.where(b > 0.0, b, 1.0), 0.0)

        def unfinished(state):
            step, _, _, _, rz = state
            return (step < MOST_STEPS) & (jnp.max(rz - goal) > 0.0)

        def advance(state):
            step, sol, res, p, rz = state
            q = times_system(p, split_ref)
            alpha = ratio(rz, inner(p, q))
            sol = sol + alpha * p
            res = res - alpha * q
            zed = res * scale
            new = inner(res, zed)
            p = zed + ratio(new, rz) * p
            return step + 1, sol, res, p, new

        zed = rhs * scale
        rz = inner(rhs, zed)
        goal = rz * 1e-12
        state = (jnp.int32(0), jnp.zeros_like(rhs), rhs, zed, rz)
        sol = lax.while_loop(unfinished, advance, state)[1]
        out_ref[...] = scores_of(sol, v, t)[0:2]


def body(
    clip_acts, clip_cotangents, weight_in, weight_out, proj_in, proj_out, test_grads, clip_ids
):
    width = proj_in.shape[1] * proj_out.shape[1]
    proj_in, proj_out = proj_in.T, proj_out.T
    count = 2 * HALF
    full = jax.ShapeDtypeStruct((2, PLANE, ROWS, width), BF16)
    vmem = pl.BlockSpec(memory_space=pltpu.VMEM)
    smem = pl.BlockSpec(memory_space=pltpu.SMEM)
    hbm = pl.BlockSpec(memory_space=pl.ANY)
    dma = pltpu.SemaphoreType.DMA

    def like(array):
        return pltpu.VMEM(array.shape, array.dtype)

    raw, check, v_all, t_all = pl.pallas_call(
        main_kernel,
        out_shape=(
            jax.ShapeDtypeStruct((8, count), F32),
            jax.ShapeDtypeStruct((8, 128), F32),
            full,
            full,
        ),
        in_specs=[smem] + [hbm] * 6 + [vmem],
        out_specs=(vmem, vmem, hbm, hbm),
        scratch_shapes=[
            like(clip_acts),
            like(clip_cotangents),
            like(weight_in),
            like(weight_out),
            like(proj_in),
            like(proj_out),
            like(full),
            like(full),
            pltpu.VMEM((2, TILE, 128), BF16),
            pltpu.VMEM((2, NZ, TILE, 128), BF16),
            pltpu.VMEM((NZ * TILE, 128), F32),
            pltpu.VMEM((count, 3 * count), BF16),
            pltpu.VMEM((count, count), BF16),
            dma((4,)),
            dma((PARTS,)),
            dma((PARTS,)),
            dma((2,)),
            dma((2,)),
            dma((2,)),
            dma((2,)),
            dma((NY + 1,)),
            dma((NY + 1,)),
            dma((NY + 1,)),
        ],
        compiler_params=pltpu.CompilerParams(
            collective_id=0, has_side_effects=True, vmem_limit_bytes=56 << 20
        ),
    )(
        clip_ids,
        clip_acts,
        clip_cotangents,
        weight_in,
        weight_out,
        proj_in,
        proj_out,
        test_grads,
    )
    return pl.pallas_call(
        finish_kernel,
        out_shape=jax.ShapeDtypeStruct((2, count), F32),
        in_specs=[smem, vmem, vmem, hbm, hbm],
        out_specs=vmem,
        scratch_shapes=[
            like(full),
            like(full),
            pltpu.VMEM((count, 3 * count), BF16),
            dma((2,)),
        ],
        compiler_params=pltpu.CompilerParams(vmem_limit_bytes=56 << 20),
    )(clip_ids, raw, check, v_all, t_all)


def solution(mesh):
    in_specs = (
        P(("clip", "proj"), None, None),
        P(("clip", "proj"), None, None),
        P(),
        P(),
        P(),
        P(),
        P(("clip", "proj"), None),
        P(("clip", "proj")),
    )
    out_specs = P(("clip", "proj"), None)
    return jax.shard_map(body, mesh=mesh, in_specs=in_specs, out_specs=out_specs, check_vma=False)
```

```python
import functools
import math

import jax
import jax.numpy as jnp
from jax import lax
from jax.experimental import pallas as pl
from jax.experimental.pallas import tpu as pltpu
from jax.sharding import PartitionSpec as P

MESH = pl.DeviceIdType.MESH
F32, BF16 = jnp.float32, jnp.bfloat16
damp_ratio = 0.1

NY, NX, NZ, XLO = 4, 4, 8, 2
PLANE = NY * NX
TILE = 16
ROWS = 2 * NZ
HALF = PLANE * ROWS
PARTS = 2
DOUBLINGS = 4
REFINEMENTS = 3
MOST_STEPS = 4096
LAST_BITS = 2.0**-22

PLANE_STEPS = sorted(
    ((dy, dx) for dy in range(NY) for dx in range(NX) if (dy, dx) != (0, 0)),
    key=lambda s: -(min(s[0], NY - s[0]) + min(s[1], NX - s[1])),
)
STEPS = len(PLANE_STEPS)
LINE_STEPS = sorted(range(1, NZ), key=lambda d: -min(d, NZ - d))
CHUNKS = 8
ACROSS = 6
SPLIT = ACROSS * 128


def gelu_slope(values):
    normal_cdf = 0.5 * (1.0 + lax.erf(values * math.sqrt(0.5)))
    normal_pdf = jnp.exp(-0.5 * values * values) * (1.0 / math.sqrt(2.0 * math.pi))
    return normal_cdf + values * normal_pdf


def my_place():
    clip, proj = lax.axis_index("clip"), lax.axis_index("proj")
    xh = NX // XLO
    y, z = clip // (xh * NZ), lax.rem(clip, NZ)
    x = lax.rem(clip // NZ, xh) * XLO + proj // 2
    return y, x, z, lax.rem(proj, 2)


def device_at(y, x, z, core):
    return {
        "clip": (y * (NX // XLO) + x // XLO) * NZ + z,
        "proj": lax.rem(x, XLO) * 2 + core,
    }


def mm(a, b):
    return jnp.dot(a, b, preferred_element_type=F32)


def mm_t(a, b):
    return lax.dot_general(a, b, (((1,), (1,)), ((), ())), preferred_element_type=F32)


def pieces(values):
    first = values.astype(BF16).astype(F32)
    rest = values - first
    second = rest.astype(BF16).astype(F32)
    return first, second, rest - second


def stacked(values):
    first, second, third = pieces(values)
    return jnp.concatenate([first, second, third, jnp.zeros_like(first)], axis=0).astype(BF16)


def unstacked(product):
    return product[0:8] + product[8:16] + product[16:24]


def iota(shape, axis):
    return lax.broadcasted_iota(jnp.int32, shape, axis)


def inner(a, b):
    return jnp.sum(a * b, axis=1, keepdims=True)


def spread(ref, values):
    chunks = values.shape[1] // 128
    for c in range(chunks):
        ref[pl.ds(c, 2, stride=chunks), :] = values[:, c * 128 : (c + 1) * 128]
    return ref[...].astype(BF16)


def left_pieces(acts, proj_in):
    tokens, width = acts.shape[0], proj_in.shape[0]
    groups = 128 // width
    per = width // groups
    r, c = iota((128, width), 1), iota((128, width), 0)
    chosen = (c < width) & (r == lax.rem(c, per) * groups + c // per)
    ordered = mm(jnp.where(chosen, 1.0, 0.0).astype(BF16), proj_in).astype(BF16)
    left = mm_t(ordered, acts)
    half = tokens // 2
    rows = []
    for k in range(2):
        lane = iota((per, tokens), 1)
        own = (lane >= k * half) & (lane < (k + 1) * half)
        row = [jnp.where(own, left[j * per : (j + 1) * per], 0.0) for j in range(groups)]
        rows.append(jnp.concatenate(row, axis=1))
    return jnp.concatenate(pieces(jnp.concatenate(rows, axis=0)), axis=0).astype(BF16)


def outer_tile(left, right, in_width):
    width = right.shape[1]
    groups = 128 // width
    wide = jnp.concatenate([right] * groups, axis=1)
    lane = iota(wide.shape, 1) // width
    stack = []
    for piece in pieces(wide):
        masked = [jnp.where(lane == j, piece, 0.0) for j in range(groups)]
        stack.append(jnp.concatenate(masked, axis=0).astype(BF16))
    product = mm(left, jnp.concatenate(stack, axis=1))
    total = None
    for i in (2, 1, 0):
        for j in (2, 1, 0):
            term = product[i * TILE : (i + 1) * TILE, j * 128 : (j + 1) * 128]
            total = term if total is None else total + term
    return total


def target_order(shape):
    j = iota((1, shape[1]), 1)
    k, core = lax.rem(j, 2), lax.rem(j // 2, 2)
    x_lo, z = lax.rem(j // 4, XLO), lax.rem(j // (4 * XLO), NZ)
    rest = j // (4 * XLO * NZ)
    x_hi, y = lax.rem(rest, NX // XLO), rest // (NX // XLO)
    source = core * HALF + (y * NX + x_hi * XLO + x_lo) * ROWS + k * NZ + z
    return jnp.where(iota(shape, 0) == source, 1.0, 0.0).astype(BF16)


def wanted_rows(ids_ref, count):
    y, x, z, core = my_place()
    base = core * HALF + (y * NX + x) * ROWS + z
    lane, sub = iota((8, count), 1), iota((8, count), 0)
    wanted = base + NZ * jnp.where(sub == 0, ids_ref[0], ids_ref[1])
    return jnp.where((lane == wanted) & (sub < 2), 1.0, 0.0)


def form_system(v, split_ref):
    count, width = v.shape
    gram = mm_t(v, v) * (1.0 / count)
    eye = iota((count, count), 0) == iota((count, count), 1)
    diagonal = jnp.sum(jnp.where(eye, gram, 0.0), axis=0, keepdims=True)
    damping = damp_ratio * jnp.sum(diagonal, axis=1, keepdims=True) / width
    system = gram + jnp.where(eye, damping, 0.0)
    for i, piece in enumerate(pieces(system)):
        split_ref[:, i * count : (i + 1) * count] = piece.astype(BF16)
    return system, damping, diagonal + damping, eye


def times_system(p, split_ref):
    count = split_ref.shape[0]
    product = unstacked(mm(stacked(p), split_ref[...]))
    return (
        product[:, 0:count] + product[:, count : 2 * count] + product[:, 2 * count : 3 * count]
    )


def scores_of(sol, v, t):
    mixed = unstacked(mm(stacked(sol), v))
    raw = unstacked(mm_t(stacked(mixed), t)) * (1.0 / math.sqrt(v.shape[1]))
    return unstacked(mm(stacked(raw), target_order((t.shape[0], t.shape[0]))))


def refined(ids_ref, v, split_ref, m_ref):
    count = v.shape[0]
    system, low, _, eye = form_system(v, split_ref)
    high = split_ref[:, 0:count]
    square = mm(high, high)
    top = jnp.max(jnp.sum(jnp.abs(square), axis=0, keepdims=True), axis=1, keepdims=True)
    top = jnp.sqrt(top) * 1.02
    centre = 2.0 / (top + low)
    t = (top + low) / (top - low)
    t2 = 2.0 * t * t - 1.0
    c = 2.0 * t * t / t2 * centre
    m = jnp.where(eye, 2.0 * c, 0.0) - (c * centre) * system
    am = (2.0 * c) * system - (c * centre) * square
    for i in range(DOUBLINGS):
        t = t2
        t2 = 2.0 * t * t - 1.0
        c = 2.0 * t * t / t2
        rounded = m.astype(BF16)
        if i > 0:
            am = mm(high, rounded)
        m = c * (2.0 * m - mm(rounded, am.astype(BF16)))
    m_ref[...] = m.astype(BF16)

    rhs = wanted_rows(ids_ref, count)

    def precondition(r):
        return mm(jnp.concatenate([r, jnp.zeros_like(r)], axis=0).astype(BF16), m_ref[...])[0:8]

    sol = precondition(rhs)
    res = rhs - times_system(sol, split_ref)
    for _ in range(REFINEMENTS):
        sol = sol + precondition(res)
        res = rhs - times_system(sol, split_ref)
    excess = inner(res, res) - (LAST_BITS * top) * (LAST_BITS * top) * inner(sol, sol)
    return sol, excess


def main_kernel(
    ids_hbm, acts_hbm, cot_hbm, w_in_hbm, w_out_hbm, proj_in_hbm, proj_out_hbm, test_hbm,
    raw_ref, check_ref, v_out, t_out,
    ids_ref, acts, cot, w_in, w_out, proj_in, proj_out, test, v_all, t_all,
    tiles, line, plane, cross, wide, split_ref, m_ref,
    load_sem, in_sem, out_sem, store_sem,
    line_send, line_recv, plane_send, plane_recv,
    rows_send, rows_recv, cross_send, cross_recv, core_send, core_recv,
):
    y, x, z, core = my_place()
    block = w_in.shape[1] // PARTS
    tokens = acts.shape[0] * acts.shape[1]

    small = [
        pltpu.make_async_copy(src, dst, load_sem.at[i])
        for i, (src, dst) in enumerate(
            (
                (acts_hbm, acts),
                (proj_in_hbm, proj_in),
                (cot_hbm, cot),
                (proj_out_hbm, proj_out),
                (test_hbm, test),
                (ids_hbm, ids_ref),
            )
        )
    ]
    loads_in, loads_out = [], []
    for i in range(PARTS):
        part = pl.ds(i * block, block)
        loads_in.append(
            pltpu.make_async_copy(w_in_hbm.at[:, part], w_in.at[:, part], in_sem.at[i])
        )
        loads_out.append(
            pltpu.make_async_copy(w_out_hbm.at[part], w_out.at[part], out_sem.at[i])
        )
    small[4].start()
    small[0].start()
    small[1].start()
    loads_in[0].start()
    small[2].start()
    loads_out[0].start()
    small[3].start()
    for i in range(1, PARTS):
        loads_in[i].start()
        loads_out[i].start()
    small[5].start()

    barrier = pltpu.get_barrier_semaphore()
    on_line = [device_at(y, x, lax.rem(z + d, NZ), core) for d in LINE_STEPS]
    on_plane = [
        device_at(lax.rem(y + dy, NY), lax.rem(x + dx, NX), z, core) for dy, dx in PLANE_STEPS
    ]
    partner = device_at(y, x, z, 1 - core)
    targets = on_line + on_plane + [partner]
    for target in targets:
        pl.semaphore_signal(barrier, inc=1, device_id=target, device_id_type=MESH)

    fulls = (v_all, t_all)
    mine = y * NX + x

    def send(src, dst, send_sem, recv_sem, target):
        pltpu.make_async_remote_copy(
            src_ref=src,
            dst_ref=dst,
            send_sem=send_sem,
            recv_sem=recv_sem,
            device_id=target,
            device_id_type=MESH,
        ).start()

    def await_bytes(ref, sem):
        pltpu.make_async_copy(ref, ref, sem).wait()

    def start_tiles(a, tile):
        tiles[a] = tile
        for target in on_line:
            send(tiles.at[a], line.at[a, z], line_send.at[a], line_recv.at[a], target)
        for target in on_plane:
            send(tiles.at[a], plane.at[a, mine], plane_send.at[a], plane_recv.at[a], target)
        line[a, z] = tile
        plane[a, mine] = tile

    def start_blocks(a):
        full = fulls[a]
        await_bytes(line.at[a, pl.ds(0, NZ - 1)], line_recv.at[a])
        wide[0 : NZ * TILE, :] = line[a].reshape(NZ * TILE, 128).astype(F32)
        for c in range(ACROSS):
            both = [wide[pl.ds(k * CHUNKS + c, NZ, stride=TILE), :] for k in range(2)]
            full[core, mine, :, c * 128 : (c + 1) * 128] = jnp.concatenate(both, axis=0).astype(
                BF16
            )
        rows = full.at[core, mine, :, pl.ds(0, SPLIT)]
        for (dy, _), target in zip(PLANE_STEPS, on_plane):
            send(rows, rows, rows_send.at[a], rows_recv.at[dy if a == 0 else NY], target)
        await_bytes(plane.at[a, pl.ds(0, STEPS)], plane_recv.at[a])
        wide[...] = plane[a].reshape(PLANE * TILE, 128).astype(F32)
        for c in range(ACROSS, CHUNKS):
            both = [wide[pl.ds(k * CHUNKS + c, PLANE, stride=TILE), :] for k in range(2)]
            cross[a, z, :, (c - ACROSS) * 128 : (c - ACROSS + 1) * 128] = jnp.concatenate(
                both, axis=0
            ).astype(BF16)
        rows = cross.at[a, z]
        for target in on_line:
            send(rows, rows, cross_send.at[a], cross_recv.at[a], target)

    def place_cross(a):
        await_bytes(cross.at[a, pl.ds(0, NZ - 1)], cross_recv.at[a])
        for c in range(CHUNKS - ACROSS):
            wide[...] = cross[a, :, :, c * 128 : (c + 1) * 128].reshape(NZ * 2 * PLANE, 128).astype(F32)
            for p in range(PLANE):
                both = [wide[pl.ds(k * PLANE + p, NZ, stride=2 * PLANE), :] for k in range(2)]
                fulls[a][core, p, :, SPLIT + c * 128 : SPLIT + (c + 1) * 128] = jnp.concatenate(
                    both, axis=0
                ).astype(BF16)

    def core_copy(i, rows):
        return pltpu.make_async_remote_copy(
            src_ref=rows,
            dst_ref=rows,
            send_sem=core_send.at[i],
            recv_sem=core_recv.at[i],
            device_id=partner,
            device_id_type=MESH,
        )

    small[4].wait()
    t_tile = spread(wide.at[pl.ds(0, TILE)], test[...].astype(F32))
    pl.semaphore_wait(barrier, len(targets))
    start_tiles(1, t_tile)

    small[0].wait()
    small[1].wait()
    left = left_pieces(acts[...].reshape(tokens, -1), proj_in[...])
    small[2].wait()
    small[3].wait()
    right = None
    for i in range(PARTS):
        loads_in[i].wait()
        loads_out[i].wait()
        part = slice(i * block, (i + 1) * block)
        preact = mm(acts[...].reshape(tokens, -1), w_in[:, part])
        backprop = mm_t(cot[...].reshape(tokens, -1), w_out[part])
        deltas = (backprop * gelu_slope(preact)).astype(BF16)
        term = mm_t(deltas, proj_out[:, part])
        right = term if right is None else right + term
    outer = outer_tile(left, right, proj_in.shape[0])
    start_tiles(0, (outer * (1.0 / math.sqrt(acts.shape[1]))).astype(BF16))
    start_blocks(1)
    start_blocks(0)

    place_cross(0)
    v_copies = []
    for dy in (0, 1, 3, 2):
        first = lax.rem(y + NY - dy, NY) * NX
        count = NX - (dy == 0)
        await_bytes(v_all.at[core, pl.ds(first, count), :, pl.ds(0, SPLIT)], rows_recv.at[dy])
        v_copies.append(core_copy(dy, v_all.at[core, pl.ds(first, NX)]))
        v_copies[-1].start()
    place_cross(1)
    await_bytes(t_all.at[core, pl.ds(0, STEPS), :, pl.ds(0, SPLIT)], rows_recv.at[NY])
    t_copy = core_copy(NY, t_all.at[core])
    t_copy.start()
    for copy in v_copies:
        copy.wait_recv()
    store_v = pltpu.make_async_copy(v_all, v_out, store_sem.at[0])
    store_v.start()

    small[5].wait()
    v = v_all[...].reshape(2 * HALF, -1)
    sol, excess = refined(ids_ref, v, split_ref, m_ref)
    t_copy.wait_recv()
    store_t = pltpu.make_async_copy(t_all, t_out, store_sem.at[1])
    store_t.start()
    raw_ref[...] = scores_of(sol, v, t_all[...].reshape(2 * HALF, -1))
    check_ref[...] = jnp.broadcast_to(excess, check_ref.shape)
    for a in range(2):
        await_bytes(line.at[a, pl.ds(0, NZ - 1)], line_send.at[a])
        await_bytes(plane.at[a, pl.ds(0, STEPS)], plane_send.at[a])
        await_bytes(fulls[a].at[core, pl.ds(0, STEPS), :, pl.ds(0, SPLIT)], rows_send.at[a])
        await_bytes(cross.at[a, pl.ds(0, NZ - 1)], cross_send.at[a])
    t_copy.wait_send()
    for copy in v_copies:
        copy.wait_send()
    store_v.wait()
    store_t.wait()


def finish_kernel(ids_ref, raw_ref, check_ref, v_hbm, t_hbm, out_ref, v_ref, t_ref, split_ref, sem):
    out_ref[...] = raw_ref[0:2]
    excess = check_ref[...]
    fine = jnp.min(jnp.where(excess <= 0.0, 1.0, 0.0))

    @pl.when(fine < 1.0)
    def _():
        loads = [
            pltpu.make_async_copy(v_hbm, v_ref, sem.at[0]),
            pltpu.make_async_copy(t_hbm, t_ref, sem.at[1]),
        ]
        for load in loads:
            load.start()
        for load in loads:
            load.wait()
        count = 2 * HALF
        v, t = v_ref[...].reshape(count, -1), t_ref[...].reshape(count, -1)
        _, _, diagonal, _ = form_system(v, split_ref)
        rhs = wanted_rows(ids_ref, count)
        scale = 1.0 / diagonal

        def ratio(a, b):
            return jnp.where(b > 0.0, a / jnp.where(b > 0.0, b, 1.0), 0.0)

        def unfinished(state):
            step, _, _, _, rz = state
            return (step < MOST_STEPS) & (jnp.max(rz - goal) > 0.0)

        def advance(state):
            step, sol, res, p, rz = state
            q = times_system(p, split_ref)
            alpha = ratio(rz, inner(p, q))
            sol = sol + alpha * p
            res = res - alpha * q
            zed = res * scale
            new = inner(res, zed)
            p = zed + ratio(new, rz) * p
            return step + 1, sol, res, p, new

        zed = rhs * scale
        rz = inner(rhs, zed)
        goal = rz * 1e-12
        state = (jnp.int32(0), jnp.zeros_like(rhs), rhs, zed, rz)
        sol = lax.while_loop(unfinished, advance, state)[1]
        out_ref[...] = scores_of(sol, v, t)[0:2]


def body(
    clip_acts, clip_cotangents, weight_in, weight_out, proj_in, proj_out, test_grads, clip_ids
):
    width = proj_in.shape[1] * proj_out.shape[1]
    proj_in, proj_out = proj_in.T, proj_out.T
    count = 2 * HALF
    full = jax.ShapeDtypeStruct((2, PLANE, ROWS, width), BF16)
    vmem = pl.BlockSpec(memory_space=pltpu.VMEM)
    smem = pl.BlockSpec(memory_space=pltpu.SMEM)
    hbm = pl.BlockSpec(memory_space=pl.ANY)
    dma = pltpu.SemaphoreType.DMA

    def like(array):
        return pltpu.VMEM(array.shape, array.dtype)

    raw, check, v_all, t_all = pl.pallas_call(
        main_kernel,
        out_shape=(
            jax.ShapeDtypeStruct((8, count), F32),
            jax.ShapeDtypeStruct((8, 128), F32),
            full,
            full,
        ),
        in_specs=[hbm] * 8,
        out_specs=(vmem, vmem, hbm, hbm),
        scratch_shapes=[
            pltpu.SMEM(clip_ids.shape, clip_ids.dtype),
            like(clip_acts),
            like(clip_cotangents),
            like(weight_in),
            like(weight_out),
            like(proj_in),
            like(proj_out),
            like(test_grads),
            like(full),
            like(full),
            pltpu.VMEM((2, TILE, 128), BF16),
            pltpu.VMEM((2, NZ, TILE, 128), BF16),
            pltpu.VMEM((2, PLANE, TILE, 128), BF16),
            pltpu.VMEM((2, NZ, 2 * PLANE, (CHUNKS - ACROSS) * 128), BF16),
            pltpu.VMEM((PLANE * TILE, 128), F32),
            pltpu.VMEM((count, 3 * count), BF16),
            pltpu.VMEM((count, count), BF16),
            dma((6,)),
            dma((PARTS,)),
            dma((PARTS,)),
            dma((2,)),
            dma((2,)),
            dma((2,)),
            dma((2,)),
            dma((2,)),
            dma((2,)),
            dma((NY + 1,)),
            dma((2,)),
            dma((2,)),
            dma((NY + 1,)),
            dma((NY + 1,)),
        ],
        compiler_params=pltpu.CompilerParams(
            collective_id=0, has_side_effects=True, vmem_limit_bytes=56 << 20
        ),
    )(
        clip_ids,
        clip_acts,
        clip_cotangents,
        weight_in,
        weight_out,
        proj_in,
        proj_out,
        test_grads,
    )
    return pl.pallas_call(
        finish_kernel,
        out_shape=jax.ShapeDtypeStruct((2, count), F32),
        in_specs=[smem, vmem, vmem, hbm, hbm],
        out_specs=vmem,
        scratch_shapes=[
            like(full),
            like(full),
            pltpu.VMEM((count, 3 * count), BF16),
            dma((2,)),
        ],
        compiler_params=pltpu.CompilerParams(vmem_limit_bytes=56 << 20),
    )(clip_ids, raw, check, v_all, t_all)


def solution(mesh):
    in_specs = (
        P(("clip", "proj"), None, None),
        P(("clip", "proj"), None, None),
        P(),
        P(),
        P(),
        P(),
        P(("clip", "proj"), None),
        P(("clip", "proj")),
    )
    out_specs = P(("clip", "proj"), None)
    return jax.shard_map(body, mesh=mesh, in_specs=in_specs, out_specs=out_specs, check_vma=False)
```

```python
import functools
import math

import jax
import jax.numpy as jnp
from jax import lax
from jax.experimental import pallas as pl
from jax.experimental.pallas import tpu as pltpu
from jax.sharding import PartitionSpec as P

MESH = pl.DeviceIdType.MESH
F32, BF16 = jnp.float32, jnp.bfloat16
damp_ratio = 0.1

NY, NX, NZ, XLO = 4, 4, 8, 2
PLANE = NY * NX
TILE = 16
ROWS = 2 * NZ
HALF = PLANE * ROWS
PARTS = 2
DOUBLINGS = 4
REFINEMENTS = 3
MOST_STEPS = 4096
LAST_BITS = 2.0**-22

PLANE_STEPS = sorted(
    ((dy, dx) for dy in range(NY) for dx in range(NX) if (dy, dx) != (0, 0)),
    key=lambda s: -(min(s[0], NY - s[0]) + min(s[1], NX - s[1])),
)
STEPS = len(PLANE_STEPS)
LINE_STEPS = sorted(range(1, NZ), key=lambda d: -min(d, NZ - d))
CHUNKS = 8
ACROSS = 6
SPLIT = ACROSS * 128


def gelu_slope(values):
    normal_cdf = 0.5 * (1.0 + lax.erf(values * math.sqrt(0.5)))
    normal_pdf = jnp.exp(-0.5 * values * values) * (1.0 / math.sqrt(2.0 * math.pi))
    return normal_cdf + values * normal_pdf


def my_place():
    clip, proj = lax.axis_index("clip"), lax.axis_index("proj")
    xh = NX // XLO
    y, z = clip // (xh * NZ), lax.rem(clip, NZ)
    x = lax.rem(clip // NZ, xh) * XLO + proj // 2
    return y, x, z, lax.rem(proj, 2)


def device_at(y, x, z, core):
    return {
        "clip": (y * (NX // XLO) + x // XLO) * NZ + z,
        "proj": lax.rem(x, XLO) * 2 + core,
    }


def mm(a, b):
    return jnp.dot(a, b, preferred_element_type=F32)


def mm_t(a, b):
    return lax.dot_general(a, b, (((1,), (1,)), ((), ())), preferred_element_type=F32)


def pieces(values):
    first = values.astype(BF16).astype(F32)
    rest = values - first
    second = rest.astype(BF16).astype(F32)
    return first, second, rest - second


def stacked(values):
    first, second, third = pieces(values)
    return jnp.concatenate([first, second, third, jnp.zeros_like(first)], axis=0).astype(BF16)


def unstacked(product):
    return product[0:8] + product[8:16] + product[16:24]


def iota(shape, axis):
    return lax.broadcasted_iota(jnp.int32, shape, axis)


def inner(a, b):
    return jnp.sum(a * b, axis=1, keepdims=True)


def spread(ref, values):
    chunks = values.shape[1] // 128
    for c in range(chunks):
        ref[pl.ds(c, 2, stride=chunks), :] = values[:, c * 128 : (c + 1) * 128]
    return ref[...].astype(BF16)


def left_pieces(acts, proj_in):
    tokens, width = acts.shape[0], proj_in.shape[0]
    groups = 128 // width
    per = width // groups
    r, c = iota((128, width), 1), iota((128, width), 0)
    chosen = (c < width) & (r == lax.rem(c, per) * groups + c // per)
    ordered = mm(jnp.where(chosen, 1.0, 0.0).astype(BF16), proj_in).astype(BF16)
    left = mm_t(ordered, acts)
    half = tokens // 2
    rows = []
    for k in range(2):
        lane = iota((per, tokens), 1)
        own = (lane >= k * half) & (lane < (k + 1) * half)
        row = [jnp.where(own, left[j * per : (j + 1) * per], 0.0) for j in range(groups)]
        rows.append(jnp.concatenate(row, axis=1))
    return jnp.concatenate(pieces(jnp.concatenate(rows, axis=0)), axis=0).astype(BF16)


def outer_tile(left, right, in_width):
    width = right.shape[1]
    groups = 128 // width
    wide = jnp.concatenate([right] * groups, axis=1)
    lane = iota(wide.shape, 1) // width
    stack = []
    for piece in pieces(wide):
        masked = [jnp.where(lane == j, piece, 0.0) for j in range(groups)]
        stack.append(jnp.concatenate(masked, axis=0).astype(BF16))
    product = mm(left, jnp.concatenate(stack, axis=1))
    total = None
    for i in (2, 1, 0):
        for j in (2, 1, 0):
            term = product[i * TILE : (i + 1) * TILE, j * 128 : (j + 1) * 128]
            total = term if total is None else total + term
    return total


def target_order(shape):
    j = iota((1, shape[1]), 1)
    k, core = lax.rem(j, 2), lax.rem(j // 2, 2)
    x_lo, z = lax.rem(j // 4, XLO), lax.rem(j // (4 * XLO), NZ)
    rest = j // (4 * XLO * NZ)
    x_hi, y = lax.rem(rest, NX // XLO), rest // (NX // XLO)
    source = core * HALF + (y * NX + x_hi * XLO + x_lo) * ROWS + k * NZ + z
    return jnp.where(iota(shape, 0) == source, 1.0, 0.0).astype(BF16)


def wanted_rows(ids_ref, count):
    y, x, z, core = my_place()
    base = core * HALF + (y * NX + x) * ROWS + z
    lane, sub = iota((8, count), 1), iota((8, count), 0)
    wanted = base + NZ * jnp.where(sub == 0, ids_ref[0], ids_ref[1])
    return jnp.where((lane == wanted) & (sub < 2), 1.0, 0.0)


def form_system(v, split_ref):
    count, width = v.shape
    gram = mm_t(v, v) * (1.0 / count)
    eye = iota((count, count), 0) == iota((count, count), 1)
    diagonal = jnp.sum(jnp.where(eye, gram, 0.0), axis=0, keepdims=True)
    damping = damp_ratio * jnp.sum(diagonal, axis=1, keepdims=True) / width
    system = gram + jnp.where(eye, damping, 0.0)
    for i, piece in enumerate(pieces(system)):
        split_ref[:, i * count : (i + 1) * count] = piece.astype(BF16)
    return system, damping, diagonal + damping, eye


def times_system(p, split_ref):
    count = split_ref.shape[0]
    product = unstacked(mm(stacked(p), split_ref[...]))
    return (
        product[:, 0:count] + product[:, count : 2 * count] + product[:, 2 * count : 3 * count]
    )


def scores_of(sol, v, t):
    mixed = unstacked(mm(stacked(sol), v))
    raw = unstacked(mm_t(stacked(mixed), t)) * (1.0 / math.sqrt(v.shape[1]))
    return unstacked(mm(stacked(raw), target_order((t.shape[0], t.shape[0]))))


def approximate_inverse(v, split_ref, m_ref):
    count = v.shape[0]
    system, low, _, eye = form_system(v, split_ref)
    high = split_ref[:, 0:count]
    square = mm(high, high)
    top = jnp.max(jnp.sum(jnp.abs(square), axis=0, keepdims=True), axis=1, keepdims=True)
    top = jnp.sqrt(top) * 1.02
    centre = 2.0 / (top + low)
    t = (top + low) / (top - low)
    t2 = 2.0 * t * t - 1.0
    c = 2.0 * t * t / t2 * centre
    m = jnp.where(eye, 2.0 * c, 0.0) - (c * centre) * system
    am = (2.0 * c) * system - (c * centre) * square
    for i in range(DOUBLINGS):
        t = t2
        t2 = 2.0 * t * t - 1.0
        c = 2.0 * t * t / t2
        rounded = m.astype(BF16)
        if i > 0:
            am = mm(high, rounded)
        m = c * (2.0 * m - mm(rounded, am.astype(BF16)))
    m_ref[...] = m.astype(BF16)
    return top


def refined(rhs, top, split_ref, m_ref):
    def precondition(r):
        return mm(jnp.concatenate([r, jnp.zeros_like(r)], axis=0).astype(BF16), m_ref[...])[0:8]

    sol = precondition(rhs)
    res = rhs - times_system(sol, split_ref)
    for _ in range(REFINEMENTS):
        sol = sol + precondition(res)
        res = rhs - times_system(sol, split_ref)
    excess = inner(res, res) - (LAST_BITS * top) * (LAST_BITS * top) * inner(sol, sol)
    return sol, excess


def main_kernel(
    ids_hbm, acts_hbm, cot_hbm, w_in_hbm, w_out_hbm, proj_in_hbm, proj_out_hbm, test_hbm,
    raw_ref, check_ref, v_all, t_all,
    ids_ref, acts, cot, w_in, w_out, proj_in, proj_out, test,
    tiles, line, plane, cross, wide, split_ref, m_ref,
    load_sem, in_sem, out_sem,
    line_send, line_recv, plane_send, plane_recv,
    rows_send, rows_recv, cross_send, cross_recv, core_send, core_recv,
):
    y, x, z, core = my_place()
    block = w_in.shape[1] // PARTS
    tokens = acts.shape[0] * acts.shape[1]

    small = [
        pltpu.make_async_copy(src, dst, load_sem.at[i])
        for i, (src, dst) in enumerate(
            (
                (acts_hbm, acts),
                (proj_in_hbm, proj_in),
                (cot_hbm, cot),
                (proj_out_hbm, proj_out),
                (test_hbm, test),
                (ids_hbm, ids_ref),
            )
        )
    ]
    loads_in, loads_out = [], []
    for i in range(PARTS):
        part = pl.ds(i * block, block)
        loads_in.append(
            pltpu.make_async_copy(w_in_hbm.at[:, part], w_in.at[:, part], in_sem.at[i])
        )
        loads_out.append(
            pltpu.make_async_copy(w_out_hbm.at[part], w_out.at[part], out_sem.at[i])
        )
    small[4].start()
    small[0].start()
    small[1].start()
    loads_in[0].start()
    small[2].start()
    loads_out[0].start()
    small[3].start()
    for i in range(1, PARTS):
        loads_in[i].start()
        loads_out[i].start()
    small[5].start()

    barrier = pltpu.get_barrier_semaphore()
    on_line = [device_at(y, x, lax.rem(z + d, NZ), core) for d in LINE_STEPS]
    on_plane = [
        device_at(lax.rem(y + dy, NY), lax.rem(x + dx, NX), z, core) for dy, dx in PLANE_STEPS
    ]
    partner = device_at(y, x, z, 1 - core)
    targets = on_line + on_plane + [partner]
    for target in targets:
        pl.semaphore_signal(barrier, inc=1, device_id=target, device_id_type=MESH)

    fulls = (v_all, t_all)
    mine = y * NX + x

    def send(src, dst, send_sem, recv_sem, target):
        pltpu.make_async_remote_copy(
            src_ref=src,
            dst_ref=dst,
            send_sem=send_sem,
            recv_sem=recv_sem,
            device_id=target,
            device_id_type=MESH,
        ).start()

    def await_bytes(ref, sem):
        pltpu.make_async_copy(ref, ref, sem).wait()

    def start_tiles(a, tile):
        tiles[a] = tile
        for target in on_line:
            send(tiles.at[a], line.at[a, z], line_send.at[a], line_recv.at[a], target)
        for target in on_plane:
            send(tiles.at[a], plane.at[a, mine], plane_send.at[a], plane_recv.at[a], target)
        line[a, z] = tile
        plane[a, mine] = tile

    def start_blocks(a):
        full = fulls[a]
        await_bytes(line.at[a, pl.ds(0, NZ - 1)], line_recv.at[a])
        wide[0 : NZ * TILE, :] = line[a].reshape(NZ * TILE, 128).astype(F32)
        for c in range(ACROSS):
            both = [wide[pl.ds(k * CHUNKS + c, NZ, stride=TILE), :] for k in range(2)]
            full[core, mine, :, c * 128 : (c + 1) * 128] = jnp.concatenate(both, axis=0).astype(
                BF16
            )
        rows = full.at[core, mine, :, pl.ds(0, SPLIT)]
        for (dy, _), target in zip(PLANE_STEPS, on_plane):
            send(rows, rows, rows_send.at[a], rows_recv.at[dy if a == 0 else NY], target)
        await_bytes(plane.at[a, pl.ds(0, STEPS)], plane_recv.at[a])
        wide[...] = plane[a].reshape(PLANE * TILE, 128).astype(F32)
        for c in range(ACROSS, CHUNKS):
            both = [wide[pl.ds(k * CHUNKS + c, PLANE, stride=TILE), :] for k in range(2)]
            cross[a, z, :, (c - ACROSS) * 128 : (c - ACROSS + 1) * 128] = jnp.concatenate(
                both, axis=0
            ).astype(BF16)
        rows = cross.at[a, z]
        for target in on_line:
            send(rows, rows, cross_send.at[a], cross_recv.at[a], target)

    def place_cross(a):
        await_bytes(cross.at[a, pl.ds(0, NZ - 1)], cross_recv.at[a])
        for c in range(CHUNKS - ACROSS):
            wide[...] = cross[a, :, :, c * 128 : (c + 1) * 128].reshape(NZ * 2 * PLANE, 128).astype(F32)
            for p in range(PLANE):
                both = [wide[pl.ds(k * PLANE + p, NZ, stride=2 * PLANE), :] for k in range(2)]
                fulls[a][core, p, :, SPLIT + c * 128 : SPLIT + (c + 1) * 128] = jnp.concatenate(
                    both, axis=0
                ).astype(BF16)

    def core_copy(i, rows):
        return pltpu.make_async_remote_copy(
            src_ref=rows,
            dst_ref=rows,
            send_sem=core_send.at[i],
            recv_sem=core_recv.at[i],
            device_id=partner,
            device_id_type=MESH,
        )

    small[4].wait()
    t_tile = spread(wide.at[pl.ds(0, TILE)], test[...].astype(F32))
    pl.semaphore_wait(barrier, len(targets))
    start_tiles(1, t_tile)

    small[0].wait()
    small[1].wait()
    left = left_pieces(acts[...].reshape(tokens, -1), proj_in[...])
    small[2].wait()
    small[3].wait()
    right = None
    for i in range(PARTS):
        loads_in[i].wait()
        loads_out[i].wait()
        part = slice(i * block, (i + 1) * block)
        preact = mm(acts[...].reshape(tokens, -1), w_in[:, part])
        backprop = mm_t(cot[...].reshape(tokens, -1), w_out[part])
        deltas = (backprop * gelu_slope(preact)).astype(BF16)
        term = mm_t(deltas, proj_out[:, part])
        right = term if right is None else right + term
    outer = outer_tile(left, right, proj_in.shape[0])
    start_tiles(0, (outer * (1.0 / math.sqrt(acts.shape[1]))).astype(BF16))
    start_blocks(0)
    start_blocks(1)

    copies = []

    def forward(i, rows):
        copies.append(core_copy(i, rows))
        copies[-1].start()

    for dy in (0, 1, 3, 2):
        if dy == 2:
            place_cross(0)
            forward(0, v_all.at[core, :, :, pl.ds(SPLIT, (CHUNKS - ACROSS) * 128)])
        first = lax.rem(y + NY - dy, NY) * NX
        count = NX - (dy == 0)
        await_bytes(v_all.at[core, pl.ds(first, count), :, pl.ds(0, SPLIT)], rows_recv.at[dy])
        forward(dy + 1, v_all.at[core, pl.ds(first, NX), :, pl.ds(0, SPLIT)])
    for copy in copies:
        copy.wait_recv()

    small[5].wait()
    v = v_all[...].reshape(2 * HALF, -1)
    top = approximate_inverse(v, split_ref, m_ref)
    place_cross(1)
    await_bytes(t_all.at[core, pl.ds(0, STEPS), :, pl.ds(0, SPLIT)], rows_recv.at[NY])
    forward(NY + 1, t_all.at[core])
    sol, excess = refined(wanted_rows(ids_ref, 2 * HALF), top, split_ref, m_ref)
    copies[-1].wait_recv()
    raw_ref[...] = scores_of(sol, v, t_all[...].reshape(2 * HALF, -1))
    check_ref[...] = jnp.broadcast_to(excess, check_ref.shape)
    for a in range(2):
        await_bytes(line.at[a, pl.ds(0, NZ - 1)], line_send.at[a])
        await_bytes(plane.at[a, pl.ds(0, STEPS)], plane_send.at[a])
        await_bytes(fulls[a].at[core, pl.ds(0, STEPS), :, pl.ds(0, SPLIT)], rows_send.at[a])
        await_bytes(cross.at[a, pl.ds(0, NZ - 1)], cross_send.at[a])
    for copy in copies:
        copy.wait_send()


def finish_kernel(ids_ref, raw_ref, check_ref, v_ref, t_ref, out_ref, split_ref):
    out_ref[...] = raw_ref[0:2]
    excess = check_ref[...]
    fine = jnp.min(jnp.where(excess <= 0.0, 1.0, 0.0))

    @pl.when(fine < 1.0)
    def _():
        count = 2 * HALF
        v, t = v_ref[...].reshape(count, -1), t_ref[...].reshape(count, -1)
        _, _, diagonal, _ = form_system(v, split_ref)
        rhs = wanted_rows(ids_ref, count)
        scale = 1.0 / diagonal

        def ratio(a, b):
            return jnp.where(b > 0.0, a / jnp.where(b > 0.0, b, 1.0), 0.0)

        def unfinished(state):
            step, _, _, _, rz = state
            return (step < MOST_STEPS) & (jnp.max(rz - goal) > 0.0)

        def advance(state):
            step, sol, res, p, rz = state
            q = times_system(p, split_ref)
            alpha = ratio(rz, inner(p, q))
            sol = sol + alpha * p
            res = res - alpha * q
            zed = res * scale
            new = inner(res, zed)
            p = zed + ratio(new, rz) * p
            return step + 1, sol, res, p, new

        zed = rhs * scale
        rz = inner(rhs, zed)
        goal = rz * 1e-12
        state = (jnp.int32(0), jnp.zeros_like(rhs), rhs, zed, rz)
        sol = lax.while_loop(unfinished, advance, state)[1]
        out_ref[...] = scores_of(sol, v, t)[0:2]


def body(
    clip_acts, clip_cotangents, weight_in, weight_out, proj_in, proj_out, test_grads, clip_ids
):
    width = proj_in.shape[1] * proj_out.shape[1]
    proj_in, proj_out = proj_in.T, proj_out.T
    count = 2 * HALF
    full = jax.ShapeDtypeStruct((2, PLANE, ROWS, width), BF16)
    vmem = pl.BlockSpec(memory_space=pltpu.VMEM)
    smem = pl.BlockSpec(memory_space=pltpu.SMEM)
    hbm = pl.BlockSpec(memory_space=pl.ANY)
    dma = pltpu.SemaphoreType.DMA

    def like(array):
        return pltpu.VMEM(array.shape, array.dtype)

    raw, check, v_all, t_all = pl.pallas_call(
        main_kernel,
        out_shape=(
            pltpu.VMEM((8, count), F32),
            pltpu.VMEM((8, 128), F32),
            pltpu.VMEM(full.shape, BF16),
            pltpu.VMEM(full.shape, BF16),
        ),
        in_specs=[hbm] * 8,
        out_specs=(vmem, vmem, vmem, vmem),
        scratch_shapes=[
            pltpu.SMEM(clip_ids.shape, clip_ids.dtype),
            like(clip_acts),
            like(clip_cotangents),
            like(weight_in),
            like(weight_out),
            like(proj_in),
            like(proj_out),
            like(test_grads),
            pltpu.VMEM((2, TILE, 128), BF16),
            pltpu.VMEM((2, NZ, TILE, 128), BF16),
            pltpu.VMEM((2, PLANE, TILE, 128), BF16),
            pltpu.VMEM((2, NZ, 2 * PLANE, (CHUNKS - ACROSS) * 128), BF16),
            pltpu.VMEM((PLANE * TILE, 128), F32),
            pltpu.VMEM((count, 3 * count), BF16),
            pltpu.VMEM((count, count), BF16),
            dma((6,)),
            dma((PARTS,)),
            dma((PARTS,)),
            dma((2,)),
            dma((2,)),
            dma((2,)),
            dma((2,)),
            dma((2,)),
            dma((NY + 1,)),
            dma((2,)),
            dma((2,)),
            dma((NY + 2,)),
            dma((NY + 2,)),
        ],
        compiler_params=pltpu.CompilerParams(
            collective_id=0, has_side_effects=True, vmem_limit_bytes=56 << 20
        ),
    )(
        clip_ids,
        clip_acts,
        clip_cotangents,
        weight_in,
        weight_out,
        proj_in,
        proj_out,
        test_grads,
    )
    return pl.pallas_call(
        finish_kernel,
        out_shape=jax.ShapeDtypeStruct((2, count), F32),
        in_specs=[smem, vmem, vmem, vmem, vmem],
        out_specs=vmem,
        scratch_shapes=[
            pltpu.VMEM((count, 3 * count), BF16),
        ],
        compiler_params=pltpu.CompilerParams(vmem_limit_bytes=32 << 20),
    )(clip_ids, *[pltpu.with_memory_space_constraint(r, pltpu.VMEM) for r in (raw, check, v_all, t_all)])


def solution(mesh):
    in_specs = (
        P(("clip", "proj"), None, None),
        P(("clip", "proj"), None, None),
        P(),
        P(),
        P(),
        P(),
        P(("clip", "proj"), None),
        P(("clip", "proj")),
    )
    out_specs = P(("clip", "proj"), None)
    return jax.shard_map(body, mesh=mesh, in_specs=in_specs, out_specs=out_specs, check_vma=False)
```

```python
import functools
import math

import jax
import jax.numpy as jnp
from jax import lax
from jax.experimental import pallas as pl
from jax.experimental.pallas import tpu as pltpu
from jax.sharding import PartitionSpec as P

MESH = pl.DeviceIdType.MESH
F32, BF16 = jnp.float32, jnp.bfloat16
damp_ratio = 0.1

NY, NX, NZ, XLO = 4, 4, 8, 2
PLANE = NY * NX
TILE = 16
ROWS = 2 * NZ
HALF = PLANE * ROWS
PARTS = 2
DOUBLINGS = 4
REFINEMENTS = 3
MOST_STEPS = 4096
LAST_BITS = 2.0**-22

PLANE_STEPS = sorted(
    ((dy, dx) for dy in range(NY) for dx in range(NX) if (dy, dx) != (0, 0)),
    key=lambda s: -(min(s[0], NY - s[0]) + min(s[1], NX - s[1])),
)
STEPS = len(PLANE_STEPS)
LINE_STEPS = sorted(range(1, NZ), key=lambda d: -min(d, NZ - d))
CHUNKS = 8
BEFORE, NEAR = 2, 5
ACROSS = 6
SPLIT = ACROSS * 128


def gelu_slope(values):
    normal_cdf = 0.5 * (1.0 + lax.erf(values * math.sqrt(0.5)))
    normal_pdf = jnp.exp(-0.5 * values * values) * (1.0 / math.sqrt(2.0 * math.pi))
    return normal_cdf + values * normal_pdf


def my_place():
    clip, proj = lax.axis_index("clip"), lax.axis_index("proj")
    xh = NX // XLO
    y, z = clip // (xh * NZ), lax.rem(clip, NZ)
    x = lax.rem(clip // NZ, xh) * XLO + proj // 2
    return y, x, z, lax.rem(proj, 2)


def device_at(y, x, z, core):
    return {
        "clip": (y * (NX // XLO) + x // XLO) * NZ + z,
        "proj": lax.rem(x, XLO) * 2 + core,
    }


def mm(a, b):
    return jnp.dot(a, b, preferred_element_type=F32)


def mm_t(a, b):
    return lax.dot_general(a, b, (((1,), (1,)), ((), ())), preferred_element_type=F32)


def pieces(values):
    first = values.astype(BF16).astype(F32)
    rest = values - first
    second = rest.astype(BF16).astype(F32)
    return first, second, rest - second


def stacked(values):
    first, second, third = pieces(values)
    return jnp.concatenate([first, second, third, jnp.zeros_like(first)], axis=0).astype(BF16)


def unstacked(product):
    return product[0:8] + product[8:16] + product[16:24]


def iota(shape, axis):
    return lax.broadcasted_iota(jnp.int32, shape, axis)


def inner(a, b):
    return jnp.sum(a * b, axis=1, keepdims=True)


def spread(ref, values):
    chunks = values.shape[1] // 128
    for c in range(chunks):
        ref[pl.ds(c, 2, stride=chunks), :] = values[:, c * 128 : (c + 1) * 128]
    return ref[...].astype(BF16)


def left_pieces(acts, proj_in):
    tokens, width = acts.shape[0], proj_in.shape[0]
    groups = 128 // width
    per = width // groups
    r, c = iota((128, width), 1), iota((128, width), 0)
    chosen = (c < width) & (r == lax.rem(c, per) * groups + c // per)
    ordered = mm(jnp.where(chosen, 1.0, 0.0).astype(BF16), proj_in).astype(BF16)
    left = mm_t(ordered, acts)
    half = tokens // 2
    rows = []
    for k in range(2):
        lane = iota((per, tokens), 1)
        own = (lane >= k * half) & (lane < (k + 1) * half)
        row = [jnp.where(own, left[j * per : (j + 1) * per], 0.0) for j in range(groups)]
        rows.append(jnp.concatenate(row, axis=1))
    return jnp.concatenate(pieces(jnp.concatenate(rows, axis=0)), axis=0).astype(BF16)


def outer_tile(left, right, in_width):
    width = right.shape[1]
    groups = 128 // width
    wide = jnp.concatenate([right] * groups, axis=1)
    lane = iota(wide.shape, 1) // width
    stack = []
    for piece in pieces(wide):
        masked = [jnp.where(lane == j, piece, 0.0) for j in range(groups)]
        stack.append(jnp.concatenate(masked, axis=0).astype(BF16))
    product = mm(left, jnp.concatenate(stack, axis=1))
    total = None
    for i in (2, 1, 0):
        for j in (2, 1, 0):
            term = product[i * TILE : (i + 1) * TILE, j * 128 : (j + 1) * 128]
            total = term if total is None else total + term
    return total


def target_order(shape):
    j = iota((1, shape[1]), 1)
    k, core = lax.rem(j, 2), lax.rem(j // 2, 2)
    x_lo, z = lax.rem(j // 4, XLO), lax.rem(j // (4 * XLO), NZ)
    rest = j // (4 * XLO * NZ)
    x_hi, y = lax.rem(rest, NX // XLO), rest // (NX // XLO)
    source = core * HALF + (y * NX + x_hi * XLO + x_lo) * ROWS + k * NZ + z
    return jnp.where(iota(shape, 0) == source, 1.0, 0.0).astype(BF16)


def wanted_rows(ids_ref, count):
    y, x, _, core = my_place()
    base = core * HALF + (y * NX + x) * ROWS + BEFORE
    lane, sub = iota((8, count), 1), iota((8, count), 0)
    wanted = base + NZ * jnp.where(sub == 0, ids_ref[0], ids_ref[1])
    return jnp.where((lane == wanted) & (sub < 2), 1.0, 0.0)


def form_system(v, split_ref):
    count, width = v.shape
    gram = mm_t(v, v) * (1.0 / count)
    eye = iota((count, count), 0) == iota((count, count), 1)
    diagonal = jnp.sum(jnp.where(eye, gram, 0.0), axis=0, keepdims=True)
    damping = damp_ratio * jnp.sum(diagonal, axis=1, keepdims=True) / width
    system = gram + jnp.where(eye, damping, 0.0)
    for i, piece in enumerate(pieces(system)):
        split_ref[:, i * count : (i + 1) * count] = piece.astype(BF16)
    return system, damping, diagonal + damping, eye


def times_system(p, split_ref):
    count = split_ref.shape[0]
    product = unstacked(mm(stacked(p), split_ref[...]))
    return (
        product[:, 0:count] + product[:, count : 2 * count] + product[:, 2 * count : 3 * count]
    )


def scores_of(sol, v, t):
    mixed = unstacked(mm(stacked(sol), v))
    raw = unstacked(mm_t(stacked(mixed), t)) * (1.0 / math.sqrt(v.shape[1]))
    return unstacked(mm(stacked(raw), target_order((t.shape[0], t.shape[0]))))


def approximate_inverse(v, split_ref, m_ref):
    count = v.shape[0]
    system, low, _, eye = form_system(v, split_ref)
    high = split_ref[:, 0:count]
    square = mm(high, high)
    top = jnp.max(jnp.sum(jnp.abs(square), axis=0, keepdims=True), axis=1, keepdims=True)
    top = jnp.sqrt(top) * 1.02
    centre = 2.0 / (top + low)
    t = (top + low) / (top - low)
    t2 = 2.0 * t * t - 1.0
    c = 2.0 * t * t / t2 * centre
    m = jnp.where(eye, 2.0 * c, 0.0) - (c * centre) * system
    am = (2.0 * c) * system - (c * centre) * square
    for i in range(DOUBLINGS):
        t = t2
        t2 = 2.0 * t * t - 1.0
        c = 2.0 * t * t / t2
        rounded = m.astype(BF16)
        if i > 0:
            am = mm(high, rounded)
        m = c * (2.0 * m - mm(rounded, am.astype(BF16)))
    m_ref[...] = m.astype(BF16)
    return top


def refined(rhs, top, split_ref, m_ref):
    def precondition(r):
        return mm(jnp.concatenate([r, jnp.zeros_like(r)], axis=0).astype(BF16), m_ref[...])[0:8]

    sol = precondition(rhs)
    res = rhs - times_system(sol, split_ref)
    for _ in range(REFINEMENTS):
        sol = sol + precondition(res)
        res = rhs - times_system(sol, split_ref)
    excess = inner(res, res) - (LAST_BITS * top) * (LAST_BITS * top) * inner(sol, sol)
    return sol, excess


def main_kernel(
    ids_hbm, acts_hbm, cot_hbm, w_in_hbm, w_out_hbm, proj_in_hbm, proj_out_hbm, test_hbm,
    raw_ref, check_ref, v_all, t_all,
    ids_ref, acts, cot, w_in, w_out, proj_in, proj_out, test,
    tiles, t_tile, line, plane, cross, wide, split_ref, m_ref,
    load_sem, in_sem, out_sem,
    line_send, line_recv, plane_send, plane_recv, rows_send, rows_recv, cross_send, cross_recv,
    v_send, v_recv, core_send, core_recv,
):
    y, x, z, core = my_place()
    block = w_in.shape[1] // PARTS
    tokens = acts.shape[0] * acts.shape[1]

    small = [
        pltpu.make_async_copy(src, dst, load_sem.at[i])
        for i, (src, dst) in enumerate(
            (
                (acts_hbm, acts),
                (proj_in_hbm, proj_in),
                (cot_hbm, cot),
                (proj_out_hbm, proj_out),
                (test_hbm, test),
                (ids_hbm, ids_ref),
            )
        )
    ]
    loads_in, loads_out = [], []
    for i in range(PARTS):
        part = pl.ds(i * block, block)
        loads_in.append(
            pltpu.make_async_copy(w_in_hbm.at[:, part], w_in.at[:, part], in_sem.at[i])
        )
        loads_out.append(
            pltpu.make_async_copy(w_out_hbm.at[part], w_out.at[part], out_sem.at[i])
        )
    small[4].start()
    small[0].start()
    small[1].start()
    loads_in[0].start()
    small[2].start()
    loads_out[0].start()
    small[3].start()
    for i in range(1, PARTS):
        loads_in[i].start()
        loads_out[i].start()
    small[5].start()

    barrier = pltpu.get_barrier_semaphore()
    on_line = [device_at(y, x, lax.rem(z + d, NZ), core) for d in LINE_STEPS]
    on_plane = [
        device_at(lax.rem(y + dy, NY), lax.rem(x + dx, NX), z, core) for dy, dx in PLANE_STEPS
    ]
    partner = device_at(y, x, z, 1 - core)
    targets = on_line + on_plane + [partner]
    for target in targets:
        pl.semaphore_signal(barrier, inc=1, device_id=target, device_id_type=MESH)

    mine = y * NX + x

    def send(src, dst, send_sem, recv_sem, target):
        pltpu.make_async_remote_copy(
            src_ref=src,
            dst_ref=dst,
            send_sem=send_sem,
            recv_sem=recv_sem,
            device_id=target,
            device_id_type=MESH,
        ).start()

    def await_bytes(ref, sem):
        pltpu.make_async_copy(ref, ref, sem).wait()

    def core_copy(i, rows):
        copy = pltpu.make_async_remote_copy(
            src_ref=rows,
            dst_ref=rows,
            send_sem=core_send.at[i],
            recv_sem=core_recv.at[i],
            device_id=partner,
            device_id_type=MESH,
        )
        copy.start()
        return copy

    def start_test_tiles(tile):
        t_tile[...] = tile
        for target in on_line:
            send(t_tile, line.at[z], line_send, line_recv, target)
        for target in on_plane:
            send(t_tile, plane.at[mine], plane_send, plane_recv, target)
        line[z] = tile
        plane[mine] = tile

    def start_test_blocks():
        await_bytes(line.at[pl.ds(0, NZ - 1)], line_recv)
        wide[0 : NZ * TILE, :] = line[...].reshape(NZ * TILE, 128).astype(F32)
        for c in range(ACROSS):
            both = [wide[pl.ds(k * CHUNKS + c, NZ, stride=TILE), :] for k in range(2)]
            t_all[core, mine, :, c * 128 : (c + 1) * 128] = jnp.concatenate(both, axis=0).astype(
                BF16
            )
        rows = t_all.at[core, mine, :, pl.ds(0, SPLIT)]
        for target in on_plane:
            send(rows, rows, rows_send, rows_recv, target)
        await_bytes(plane.at[pl.ds(0, STEPS)], plane_recv)
        wide[0 : PLANE * TILE, :] = plane[...].reshape(PLANE * TILE, 128).astype(F32)
        for c in range(ACROSS, CHUNKS):
            both = [wide[pl.ds(k * CHUNKS + c, PLANE, stride=TILE), :] for k in range(2)]
            cross[z, :, (c - ACROSS) * 128 : (c - ACROSS + 1) * 128] = jnp.concatenate(
                both, axis=0
            ).astype(BF16)
        rows = cross.at[z]
        for target in on_line:
            send(rows, rows, cross_send, cross_recv, target)

    def place_test_blocks():
        await_bytes(cross.at[pl.ds(0, NZ - 1)], cross_recv)
        for c in range(CHUNKS - ACROSS):
            columns = cross[:, :, c * 128 : (c + 1) * 128]
            wide[0 : NZ * 2 * PLANE, :] = columns.reshape(NZ * 2 * PLANE, 128).astype(F32)
            for p in range(PLANE):
                both = [wide[pl.ds(k * PLANE + p, NZ, stride=2 * PLANE), :] for k in range(2)]
                t_all[core, p, :, SPLIT + c * 128 : SPLIT + (c + 1) * 128] = jnp.concatenate(
                    both, axis=0
                ).astype(BF16)
        await_bytes(t_all.at[core, pl.ds(0, STEPS), :, pl.ds(0, SPLIT)], rows_recv)

    def start_vector_tiles(tile):
        tiles[core, mine, BEFORE] = tile
        own = tiles.at[core, mine, BEFORE]
        for d, target in zip(LINE_STEPS, on_line):
            slot = (BEFORE - d) % NZ
            send(own, tiles.at[core, mine, slot], v_send.at[0], v_recv.at[int(slot >= NEAR)], target)

    def pass_vector_tiles(far):
        slots = pl.ds(NEAR, NZ - NEAR) if far else pl.ds(0, NEAR)
        landed = pl.ds(0, NZ - NEAR if far else NEAR - 1)
        await_bytes(tiles.at[core, mine, landed], v_recv.at[far])
        rows = tiles.at[core, mine, slots]
        for (dy, _), target in zip(PLANE_STEPS, on_plane):
            send(rows, rows, v_send.at[1], v_recv.at[2 + dy], target)

    def group_start(dy):
        return lax.rem(y + NY - dy, NY) * NX

    def lay_out(of_core, dy):
        first = group_start(dy)
        group = tiles[of_core, pl.ds(first, NX)]
        wide[...] = group.reshape(NX * NZ * TILE, 128).astype(F32)
        for p in range(NX):
            for c in range(CHUNKS):
                start = p * NZ * TILE + c
                both = [wide[pl.ds(start + k * CHUNKS, NZ, stride=TILE), :] for k in range(2)]
                v_all[of_core, first + p, :, c * 128 : (c + 1) * 128] = jnp.concatenate(
                    both, axis=0
                ).astype(BF16)

    small[4].wait()
    own_test = spread(wide.at[pl.ds(0, TILE)], test[...].astype(F32))
    pl.semaphore_wait(barrier, len(targets))
    start_test_tiles(own_test)

    small[0].wait()
    small[1].wait()
    left = left_pieces(acts[...].reshape(tokens, -1), proj_in[...])
    small[2].wait()
    small[3].wait()
    right = None
    for i in range(PARTS):
        loads_in[i].wait()
        loads_out[i].wait()
        part = slice(i * block, (i + 1) * block)
        preact = mm(acts[...].reshape(tokens, -1), w_in[:, part])
        backprop = mm_t(cot[...].reshape(tokens, -1), w_out[part])
        deltas = (backprop * gelu_slope(preact)).astype(BF16)
        term = mm_t(deltas, proj_out[:, part])
        right = term if right is None else right + term
    outer = outer_tile(left, right, proj_in.shape[0])
    start_vector_tiles((outer * (1.0 / math.sqrt(acts.shape[1]))).astype(BF16))
    start_test_blocks()
    pass_vector_tiles(0)
    pass_vector_tiles(1)

    other = 1 - core
    copies = []
    for dy in (0, 1, 3, 2):
        first = group_start(dy)
        await_bytes(tiles.at[core, pl.ds(first, NX - (dy == 0))], v_recv.at[2 + dy])
        copies.append(core_copy(dy, tiles.at[core, pl.ds(first, NX)]))
        if dy != 2:
            lay_out(core, dy)
    for copy, dy in zip(copies, (0, 1, 3)):
        copy.wait_recv()
        lay_out(other, dy)
    lay_out(core, 2)
    place_test_blocks()
    copies.append(core_copy(NY, t_all.at[core]))
    copies[NY - 1].wait_recv()
    lay_out(other, 2)

    small[5].wait()
    v = v_all[...].reshape(2 * HALF, -1)
    top = approximate_inverse(v, split_ref, m_ref)
    sol, excess = refined(wanted_rows(ids_ref, 2 * HALF), top, split_ref, m_ref)
    copies[-1].wait_recv()
    raw_ref[...] = scores_of(sol, v, t_all[...].reshape(2 * HALF, -1))
    check_ref[...] = jnp.broadcast_to(excess, check_ref.shape)
    await_bytes(line.at[pl.ds(0, NZ - 1)], line_send)
    await_bytes(plane.at[pl.ds(0, STEPS)], plane_send)
    await_bytes(t_all.at[core, pl.ds(0, STEPS), :, pl.ds(0, SPLIT)], rows_send)
    await_bytes(cross.at[pl.ds(0, NZ - 1)], cross_send)
    await_bytes(tiles.at[core, mine, pl.ds(0, NZ - 1)], v_send.at[0])
    await_bytes(tiles.at[core, pl.ds(0, STEPS)], v_send.at[1])
    for copy in copies:
        copy.wait_send()


def finish_kernel(ids_ref, raw_ref, check_ref, v_ref, t_ref, out_ref, split_ref):
    out_ref[...] = raw_ref[0:2]
    excess = check_ref[...]
    fine = jnp.min(jnp.where(excess <= 0.0, 1.0, 0.0))

    @pl.when(fine < 1.0)
    def _():
        count = 2 * HALF
        v, t = v_ref[...].reshape(count, -1), t_ref[...].reshape(count, -1)
        _, _, diagonal, _ = form_system(v, split_ref)
        rhs = wanted_rows(ids_ref, count)
        scale = 1.0 / diagonal

        def ratio(a, b):
            return jnp.where(b > 0.0, a / jnp.where(b > 0.0, b, 1.0), 0.0)

        def unfinished(state):
            step, _, _, _, rz = state
            return (step < MOST_STEPS) & (jnp.max(rz - goal) > 0.0)

        def advance(state):
            step, sol, res, p, rz = state
            q = times_system(p, split_ref)
            alpha = ratio(rz, inner(p, q))
            sol = sol + alpha * p
            res = res - alpha * q
            zed = res * scale
            new = inner(res, zed)
            p = zed + ratio(new, rz) * p
            return step + 1, sol, res, p, new

        zed = rhs * scale
        rz = inner(rhs, zed)
        goal = rz * 1e-12
        state = (jnp.int32(0), jnp.zeros_like(rhs), rhs, zed, rz)
        sol = lax.while_loop(unfinished, advance, state)[1]
        out_ref[...] = scores_of(sol, v, t)[0:2]


def body(
    clip_acts, clip_cotangents, weight_in, weight_out, proj_in, proj_out, test_grads, clip_ids
):
    width = proj_in.shape[1] * proj_out.shape[1]
    proj_in, proj_out = proj_in.T, proj_out.T
    count = 2 * HALF
    full = jax.ShapeDtypeStruct((2, PLANE, ROWS, width), BF16)
    vmem = pl.BlockSpec(memory_space=pltpu.VMEM)
    smem = pl.BlockSpec(memory_space=pltpu.SMEM)
    hbm = pl.BlockSpec(memory_space=pl.ANY)
    dma = pltpu.SemaphoreType.DMA

    def like(array):
        return pltpu.VMEM(array.shape, array.dtype)

    raw, check, v_all, t_all = pl.pallas_call(
        main_kernel,
        out_shape=(
            pltpu.VMEM((8, count), F32),
            pltpu.VMEM((8, 128), F32),
            pltpu.VMEM(full.shape, BF16),
            pltpu.VMEM(full.shape, BF16),
        ),
        in_specs=[hbm] * 8,
        out_specs=(vmem, vmem, vmem, vmem),
        scratch_shapes=[
            pltpu.SMEM(clip_ids.shape, clip_ids.dtype),
            like(clip_acts),
            like(clip_cotangents),
            like(weight_in),
            like(weight_out),
            like(proj_in),
            like(proj_out),
            like(test_grads),
            pltpu.VMEM((2, PLANE, NZ, TILE, 128), BF16),
            pltpu.VMEM((TILE, 128), BF16),
            pltpu.VMEM((NZ, TILE, 128), BF16),
            pltpu.VMEM((PLANE, TILE, 128), BF16),
            pltpu.VMEM((NZ, 2 * PLANE, (CHUNKS - ACROSS) * 128), BF16),
            pltpu.VMEM((NX * NZ * TILE, 128), F32),
            pltpu.VMEM((count, 3 * count), BF16),
            pltpu.VMEM((count, count), BF16),
            dma((6,)),
            dma((PARTS,)),
            dma((PARTS,)),
        ]
        + [dma] * 8
        + [dma((2,)), dma((2 + NY,)), dma((NY + 1,)), dma((NY + 1,))],
        compiler_params=pltpu.CompilerParams(
            collective_id=0, has_side_effects=True, vmem_limit_bytes=56 << 20
        ),
    )(
        clip_ids,
        clip_acts,
        clip_cotangents,
        weight_in,
        weight_out,
        proj_in,
        proj_out,
        test_grads,
    )
    return pl.pallas_call(
        finish_kernel,
        out_shape=jax.ShapeDtypeStruct((2, count), F32),
        in_specs=[smem, vmem, vmem, vmem, vmem],
        out_specs=vmem,
        scratch_shapes=[
            pltpu.VMEM((count, 3 * count), BF16),
        ],
        compiler_params=pltpu.CompilerParams(vmem_limit_bytes=32 << 20),
    )(clip_ids, *[pltpu.with_memory_space_constraint(r, pltpu.VMEM) for r in (raw, check, v_all, t_all)])


def solution(mesh):
    in_specs = (
        P(("clip", "proj"), None, None),
        P(("clip", "proj"), None, None),
        P(),
        P(),
        P(),
        P(),
        P(("clip", "proj"), None),
        P(("clip", "proj")),
    )
    out_specs = P(("clip", "proj"), None)
    return jax.shard_map(body, mesh=mesh, in_specs=in_specs, out_specs=out_specs, check_vma=False)
```

```python
import functools
import math

import jax
import jax.numpy as jnp
from jax import lax
from jax.experimental import pallas as pl
from jax.experimental.pallas import tpu as pltpu
from jax.sharding import PartitionSpec as P

MESH = pl.DeviceIdType.MESH
F32, BF16 = jnp.float32, jnp.bfloat16
damp_ratio = 0.1

NY, NX, NZ, XLO = 4, 4, 8, 2
PLANE = NY * NX
TILE = 16
ROWS = 2 * NZ
HALF = PLANE * ROWS
PARTS = 2
DOUBLINGS = 4
REFINEMENTS = 3
MOST_STEPS = 4096
LAST_BITS = 2.0**-22

PLANE_STEPS = sorted(
    ((dy, dx) for dy in range(NY) for dx in range(NX) if (dy, dx) != (0, 0)),
    key=lambda s: -(min(s[0], NY - s[0]) + min(s[1], NX - s[1])),
)
STEPS = len(PLANE_STEPS)
LINE_STEPS = sorted(range(1, NZ), key=lambda d: -min(d, NZ - d))
CHUNKS = 8
ACROSS = (6, 6)
SPLIT = (ACROSS[0] * 128, ACROSS[1] * 128)


def gelu_slope(values):
    normal_cdf = 0.5 * (1.0 + lax.erf(values * math.sqrt(0.5)))
    normal_pdf = jnp.exp(-0.5 * values * values) * (1.0 / math.sqrt(2.0 * math.pi))
    return normal_cdf + values * normal_pdf


def my_place():
    clip, proj = lax.axis_index("clip"), lax.axis_index("proj")
    xh = NX // XLO
    y, z = clip // (xh * NZ), lax.rem(clip, NZ)
    x = lax.rem(clip // NZ, xh) * XLO + proj // 2
    return y, x, z, lax.rem(proj, 2)


def device_at(y, x, z, core):
    return {
        "clip": (y * (NX // XLO) + x // XLO) * NZ + z,
        "proj": lax.rem(x, XLO) * 2 + core,
    }


def mm(a, b):
    return jnp.dot(a, b, preferred_element_type=F32)


def mm_t(a, b):
    return lax.dot_general(a, b, (((1,), (1,)), ((), ())), preferred_element_type=F32)


def pieces(values):
    first = values.astype(BF16).astype(F32)
    rest = values - first
    second = rest.astype(BF16).astype(F32)
    return first, second, rest - second


def stacked(values):
    first, second, third = pieces(values)
    return jnp.concatenate([first, second, third, jnp.zeros_like(first)], axis=0).astype(BF16)


def unstacked(product):
    return product[0:8] + product[8:16] + product[16:24]


def iota(shape, axis):
    return lax.broadcasted_iota(jnp.int32, shape, axis)


def inner(a, b):
    return jnp.sum(a * b, axis=1, keepdims=True)


def spread(ref, values):
    chunks = values.shape[1] // 128
    for c in range(chunks):
        ref[pl.ds(c, 2, stride=chunks), :] = values[:, c * 128 : (c + 1) * 128]
    return ref[...].astype(BF16)


def left_pieces(acts, proj_in):
    tokens, width = acts.shape[0], proj_in.shape[0]
    groups = 128 // width
    per = width // groups
    r, c = iota((128, width), 1), iota((128, width), 0)
    chosen = (c < width) & (r == lax.rem(c, per) * groups + c // per)
    ordered = mm(jnp.where(chosen, 1.0, 0.0).astype(BF16), proj_in).astype(BF16)
    left = mm_t(ordered, acts)
    half = tokens // 2
    rows = []
    for k in range(2):
        lane = iota((per, tokens), 1)
        own = (lane >= k * half) & (lane < (k + 1) * half)
        row = [jnp.where(own, left[j * per : (j + 1) * per], 0.0) for j in range(groups)]
        rows.append(jnp.concatenate(row, axis=1))
    return jnp.concatenate(pieces(jnp.concatenate(rows, axis=0)), axis=0).astype(BF16)


def outer_tile(left, right, in_width):
    width = right.shape[1]
    groups = 128 // width
    wide = jnp.concatenate([right] * groups, axis=1)
    lane = iota(wide.shape, 1) // width
    stack = []
    for piece in pieces(wide):
        masked = [jnp.where(lane == j, piece, 0.0) for j in range(groups)]
        stack.append(jnp.concatenate(masked, axis=0).astype(BF16))
    product = mm(left, jnp.concatenate(stack, axis=1))
    total = None
    for i in (2, 1, 0):
        for j in (2, 1, 0):
            term = product[i * TILE : (i + 1) * TILE, j * 128 : (j + 1) * 128]
            total = term if total is None else total + term
    return total


def target_order(shape):
    j = iota((1, shape[1]), 1)
    k, core = lax.rem(j, 2), lax.rem(j // 2, 2)
    x_lo, z = lax.rem(j // 4, XLO), lax.rem(j // (4 * XLO), NZ)
    rest = j // (4 * XLO * NZ)
    x_hi, y = lax.rem(rest, NX // XLO), rest // (NX // XLO)
    source = core * HALF + (y * NX + x_hi * XLO + x_lo) * ROWS + k * NZ + z
    return jnp.where(iota(shape, 0) == source, 1.0, 0.0).astype(BF16)


def wanted_rows(ids_ref, count):
    y, x, z, core = my_place()
    base = core * HALF + (y * NX + x) * ROWS + z
    lane, sub = iota((8, count), 1), iota((8, count), 0)
    wanted = base + NZ * jnp.where(sub == 0, ids_ref[0], ids_ref[1])
    return jnp.where((lane == wanted) & (sub < 2), 1.0, 0.0)


def form_system(v, split_ref):
    count, width = v.shape
    gram = mm_t(v, v) * (1.0 / count)
    eye = iota((count, count), 0) == iota((count, count), 1)
    diagonal = jnp.sum(jnp.where(eye, gram, 0.0), axis=0, keepdims=True)
    damping = damp_ratio * jnp.sum(diagonal, axis=1, keepdims=True) / width
    system = gram + jnp.where(eye, damping, 0.0)
    for i, piece in enumerate(pieces(system)):
        split_ref[:, i * count : (i + 1) * count] = piece.astype(BF16)
    return system, damping, diagonal + damping, eye


def times_system(p, split_ref, used=3):
    count = split_ref.shape[0]
    product = unstacked(mm(stacked(p), split_ref[:, 0 : used * count]))
    total = product[:, 0:count]
    for i in range(1, used):
        total = total + product[:, i * count : (i + 1) * count]
    return total


def scores_of(sol, v, t, order):
    mixed = unstacked(mm(stacked(sol), v))
    raw = unstacked(mm_t(stacked(mixed), t)) * (1.0 / math.sqrt(v.shape[1]))
    return unstacked(mm(stacked(raw), order))


def approximate_inverse(v, split_ref, m_ref):
    count = v.shape[0]
    system, low, _, eye = form_system(v, split_ref)
    high = split_ref[:, 0:count]
    square = mm(high, high)
    top = jnp.max(jnp.sum(jnp.abs(square), axis=0, keepdims=True), axis=1, keepdims=True)
    top = jnp.sqrt(top) * 1.02
    centre = 2.0 / (top + low)
    t = (top + low) / (top - low)
    t2 = 2.0 * t * t - 1.0
    c = 2.0 * t * t / t2 * centre
    m = jnp.where(eye, 2.0 * c, 0.0) - (c * centre) * system
    am = (2.0 * c) * system - (c * centre) * square
    for i in range(DOUBLINGS):
        t = t2
        t2 = 2.0 * t * t - 1.0
        c = 2.0 * t * t / t2
        rounded = m.astype(BF16)
        if i > 0:
            am = mm(high, rounded)
        m = c * (2.0 * m - mm(rounded, am.astype(BF16)))
    m_ref[...] = m.astype(BF16)
    return top


def refined(rhs, top, split_ref, m_ref):
    def precondition(r):
        return mm(jnp.concatenate([r, jnp.zeros_like(r)], axis=0).astype(BF16), m_ref[...])[0:8]

    sol = precondition(rhs)
    res = rhs - times_system(sol, split_ref, 2)
    for i in range(REFINEMENTS):
        sol = sol + precondition(res)
        res = rhs - times_system(sol, split_ref, 2 if i == 0 else 3)
    excess = inner(res, res) - (LAST_BITS * top) * (LAST_BITS * top) * inner(sol, sol)
    return sol, excess


def main_kernel(
    ids_hbm, acts_hbm, cot_hbm, w_in_hbm, w_out_hbm, proj_in_hbm, proj_out_hbm, test_hbm,
    raw_ref, check_ref, v_all, t_all,
    ids_ref, acts, cot, w_in, w_out, proj_in, proj_out, test,
    tiles, line, plane, v_cross, t_cross, wide, split_ref, m_ref, order_ref,
    load_sem, in_sem, out_sem,
    line_send, line_recv, plane_send, plane_recv,
    rows_send, rows_recv, cross_send, cross_recv, core_send, core_recv,
):
    y, x, z, core = my_place()
    block = w_in.shape[1] // PARTS
    tokens = acts.shape[0] * acts.shape[1]

    small = [
        pltpu.make_async_copy(src, dst, load_sem.at[i])
        for i, (src, dst) in enumerate(
            (
                (acts_hbm, acts),
                (proj_in_hbm, proj_in),
                (cot_hbm, cot),
                (proj_out_hbm, proj_out),
                (test_hbm, test),
                (ids_hbm, ids_ref),
            )
        )
    ]
    loads_in, loads_out = [], []
    for i in range(PARTS):
        part = pl.ds(i * block, block)
        loads_in.append(
            pltpu.make_async_copy(w_in_hbm.at[:, part], w_in.at[:, part], in_sem.at[i])
        )
        loads_out.append(
            pltpu.make_async_copy(w_out_hbm.at[part], w_out.at[part], out_sem.at[i])
        )
    small[4].start()
    small[0].start()
    small[1].start()
    loads_in[0].start()
    small[2].start()
    loads_out[0].start()
    small[3].start()
    for i in range(1, PARTS):
        loads_in[i].start()
        loads_out[i].start()
    small[5].start()

    barrier = pltpu.get_barrier_semaphore()
    on_line = [device_at(y, x, lax.rem(z + d, NZ), core) for d in LINE_STEPS]
    on_plane = [
        device_at(lax.rem(y + dy, NY), lax.rem(x + dx, NX), z, core) for dy, dx in PLANE_STEPS
    ]
    partner = device_at(y, x, z, 1 - core)
    targets = on_line + on_plane + [partner]
    for target in targets:
        pl.semaphore_signal(barrier, inc=1, device_id=target, device_id_type=MESH)

    fulls, crosses = (v_all, t_all), (v_cross, t_cross)
    mine = y * NX + x

    def send(src, dst, send_sem, recv_sem, target):
        pltpu.make_async_remote_copy(
            src_ref=src,
            dst_ref=dst,
            send_sem=send_sem,
            recv_sem=recv_sem,
            device_id=target,
            device_id_type=MESH,
        ).start()

    def await_bytes(ref, sem):
        pltpu.make_async_copy(ref, ref, sem).wait()

    def start_tiles(a, tile):
        tiles[a] = tile
        for target in on_line:
            send(tiles.at[a], line.at[a, z], line_send.at[a], line_recv.at[a], target)
        for target in on_plane:
            send(tiles.at[a], plane.at[a, mine], plane_send.at[a], plane_recv.at[a], target)
        line[a, z] = tile
        plane[a, mine] = tile

    def start_blocks(a):
        full = fulls[a]
        await_bytes(line.at[a, pl.ds(0, NZ - 1)], line_recv.at[a])
        wide[0 : NZ * TILE, :] = line[a].reshape(NZ * TILE, 128).astype(F32)
        for c in range(ACROSS[a]):
            both = [wide[pl.ds(k * CHUNKS + c, NZ, stride=TILE), :] for k in range(2)]
            full[core, mine, :, c * 128 : (c + 1) * 128] = jnp.concatenate(both, axis=0).astype(
                BF16
            )
        rows = full.at[core, mine, :, pl.ds(0, SPLIT[a])]
        for (dy, _), target in zip(PLANE_STEPS, on_plane):
            send(rows, rows, rows_send.at[a], rows_recv.at[dy if a == 0 else NY], target)
        await_bytes(plane.at[a, pl.ds(0, STEPS)], plane_recv.at[a])
        wide[...] = plane[a].reshape(PLANE * TILE, 128).astype(F32)
        for c in range(ACROSS[a], CHUNKS):
            both = [wide[pl.ds(k * CHUNKS + c, PLANE, stride=TILE), :] for k in range(2)]
            at = c - ACROSS[a]
            crosses[a][z, :, at * 128 : (at + 1) * 128] = jnp.concatenate(both, axis=0).astype(BF16)
        rows = crosses[a].at[z]
        for target in on_line:
            send(rows, rows, cross_send.at[a], cross_recv.at[a], target)

    def place_cross(a):
        await_bytes(crosses[a].at[pl.ds(0, NZ - 1)], cross_recv.at[a])
        for c in range(ACROSS[a], CHUNKS):
            at = c - ACROSS[a]
            columns = crosses[a][:, :, at * 128 : (at + 1) * 128]
            wide[...] = columns.reshape(NZ * 2 * PLANE, 128).astype(F32)
            for p in range(PLANE):
                both = [wide[pl.ds(k * PLANE + p, NZ, stride=2 * PLANE), :] for k in range(2)]
                fulls[a][core, p, :, c * 128 : (c + 1) * 128] = jnp.concatenate(
                    both, axis=0
                ).astype(BF16)

    def core_copy(i, rows):
        return pltpu.make_async_remote_copy(
            src_ref=rows,
            dst_ref=rows,
            send_sem=core_send.at[i],
            recv_sem=core_recv.at[i],
            device_id=partner,
            device_id_type=MESH,
        )

    small[4].wait()
    t_tile = spread(wide.at[pl.ds(0, TILE)], test[...].astype(F32))
    pl.semaphore_wait(barrier, len(targets))
    start_tiles(1, t_tile)

    small[0].wait()
    small[1].wait()
    left = left_pieces(acts[...].reshape(tokens, -1), proj_in[...])
    small[2].wait()
    small[3].wait()
    right = None
    for i in range(PARTS):
        loads_in[i].wait()
        loads_out[i].wait()
        part = slice(i * block, (i + 1) * block)
        preact = mm(acts[...].reshape(tokens, -1), w_in[:, part])
        backprop = mm_t(cot[...].reshape(tokens, -1), w_out[part])
        deltas = (backprop * gelu_slope(preact)).astype(BF16)
        term = mm_t(deltas, proj_out[:, part])
        right = term if right is None else right + term
    outer = outer_tile(left, right, proj_in.shape[0])
    start_tiles(0, (outer * (1.0 / math.sqrt(acts.shape[1]))).astype(BF16))
    start_blocks(1)
    start_blocks(0)
    order_ref[...] = target_order(order_ref.shape)

    copies = []

    def forward(i, rows):
        copies.append(core_copy(i, rows))
        copies[-1].start()

    for dy in (0, 1, 3, 2):
        if dy == 2:
            place_cross(0)
            forward(0, v_all.at[core, :, :, pl.ds(SPLIT[0], (CHUNKS - ACROSS[0]) * 128)])
        first = lax.rem(y + NY - dy, NY) * NX
        count = NX - (dy == 0)
        await_bytes(v_all.at[core, pl.ds(first, count), :, pl.ds(0, SPLIT[0])], rows_recv.at[dy])
        forward(dy + 1, v_all.at[core, pl.ds(first, NX), :, pl.ds(0, SPLIT[0])])
    place_cross(1)
    await_bytes(t_all.at[core, pl.ds(0, STEPS), :, pl.ds(0, SPLIT[1])], rows_recv.at[NY])
    forward(NY + 1, t_all.at[core])
    for copy in copies[:-1]:
        copy.wait_recv()

    small[5].wait()
    v = v_all[...].reshape(2 * HALF, -1)
    top = approximate_inverse(v, split_ref, m_ref)
    sol, excess = refined(wanted_rows(ids_ref, 2 * HALF), top, split_ref, m_ref)
    copies[-1].wait_recv()
    raw = scores_of(sol, v, t_all[...].reshape(2 * HALF, -1), order_ref[...])
    raw_ref[...] = raw[0:2]
    check_ref[...] = jnp.broadcast_to(excess, check_ref.shape)
    for a in range(2):
        await_bytes(line.at[a, pl.ds(0, NZ - 1)], line_send.at[a])
        await_bytes(plane.at[a, pl.ds(0, STEPS)], plane_send.at[a])
        await_bytes(fulls[a].at[core, pl.ds(0, STEPS), :, pl.ds(0, SPLIT[a])], rows_send.at[a])
        await_bytes(crosses[a].at[pl.ds(0, NZ - 1)], cross_send.at[a])
    for copy in copies:
        copy.wait_send()


def finish_kernel(ids_ref, raw_ref, check_ref, v_ref, t_ref, out_hbm, late_ref, split_ref, sem):
    copy = pltpu.make_async_copy(raw_ref, out_hbm, sem)
    copy.start()
    excess = check_ref[...]
    fine = jnp.min(jnp.where(excess <= 0.0, 1.0, 0.0))
    copy.wait()

    @pl.when(fine < 1.0)
    def _():
        count = 2 * HALF
        v, t = v_ref[...].reshape(count, -1), t_ref[...].reshape(count, -1)
        _, _, diagonal, _ = form_system(v, split_ref)
        rhs = wanted_rows(ids_ref, count)
        scale = 1.0 / diagonal

        def ratio(a, b):
            return jnp.where(b > 0.0, a / jnp.where(b > 0.0, b, 1.0), 0.0)

        def unfinished(state):
            step, _, _, _, rz = state
            return (step < MOST_STEPS) & (jnp.max(rz - goal) > 0.0)

        def advance(state):
            step, sol, res, p, rz = state
            q = times_system(p, split_ref)
            alpha = ratio(rz, inner(p, q))
            sol = sol + alpha * p
            res = res - alpha * q
            zed = res * scale
            new = inner(res, zed)
            p = zed + ratio(new, rz) * p
            return step + 1, sol, res, p, new

        zed = rhs * scale
        rz = inner(rhs, zed)
        goal = rz * 1e-12
        state = (jnp.int32(0), jnp.zeros_like(rhs), rhs, zed, rz)
        sol = lax.while_loop(unfinished, advance, state)[1]
        late_ref[...] = scores_of(sol, v, t, target_order((count, count)))[0:2]
        again = pltpu.make_async_copy(late_ref, out_hbm, sem)
        again.start()
        again.wait()


def body(
    clip_acts, clip_cotangents, weight_in, weight_out, proj_in, proj_out, test_grads, clip_ids
):
    width = proj_in.shape[1] * proj_out.shape[1]
    proj_in, proj_out = proj_in.T, proj_out.T
    count = 2 * HALF
    full = jax.ShapeDtypeStruct((2, PLANE, ROWS, width), BF16)
    vmem = pl.BlockSpec(memory_space=pltpu.VMEM)
    smem = pl.BlockSpec(memory_space=pltpu.SMEM)
    hbm = pl.BlockSpec(memory_space=pl.ANY)
    dma = pltpu.SemaphoreType.DMA

    def like(array):
        return pltpu.VMEM(array.shape, array.dtype)

    raw, check, v_all, t_all = pl.pallas_call(
        main_kernel,
        out_shape=(
            pltpu.VMEM((2, count), F32),
            pltpu.VMEM((8, 128), F32),
            pltpu.VMEM(full.shape, BF16),
            pltpu.VMEM(full.shape, BF16),
        ),
        in_specs=[hbm] * 8,
        out_specs=(vmem, vmem, vmem, vmem),
        scratch_shapes=[
            pltpu.SMEM(clip_ids.shape, clip_ids.dtype),
            like(clip_acts),
            like(clip_cotangents),
            like(weight_in),
            like(weight_out),
            like(proj_in),
            like(proj_out),
            like(test_grads),
            pltpu.VMEM((2, TILE, 128), BF16),
            pltpu.VMEM((2, NZ, TILE, 128), BF16),
            pltpu.VMEM((2, PLANE, TILE, 128), BF16),
            pltpu.VMEM((NZ, 2 * PLANE, (CHUNKS - ACROSS[0]) * 128), BF16),
            pltpu.VMEM((NZ, 2 * PLANE, (CHUNKS - ACROSS[1]) * 128), BF16),
            pltpu.VMEM((PLANE * TILE, 128), F32),
            pltpu.VMEM((count, 3 * count), BF16),
            pltpu.VMEM((count, count), BF16),
            pltpu.VMEM((count, count), BF16),
            dma((6,)),
            dma((PARTS,)),
            dma((PARTS,)),
            dma((2,)),
            dma((2,)),
            dma((2,)),
            dma((2,)),
            dma((2,)),
            dma((NY + 1,)),
            dma((2,)),
            dma((2,)),
            dma((NY + 2,)),
            dma((NY + 2,)),
        ],
        compiler_params=pltpu.CompilerParams(
            collective_id=0, has_side_effects=True, vmem_limit_bytes=56 << 20
        ),
    )(
        clip_ids,
        clip_acts,
        clip_cotangents,
        weight_in,
        weight_out,
        proj_in,
        proj_out,
        test_grads,
    )
    return pl.pallas_call(
        finish_kernel,
        out_shape=jax.ShapeDtypeStruct((2, count), F32),
        in_specs=[smem, vmem, vmem, vmem, vmem],
        out_specs=hbm,
        scratch_shapes=[
            pltpu.VMEM((2, count), F32),
            pltpu.VMEM((count, 3 * count), BF16),
            dma,
        ],
        compiler_params=pltpu.CompilerParams(vmem_limit_bytes=32 << 20),
    )(clip_ids, *[pltpu.with_memory_space_constraint(r, pltpu.VMEM) for r in (raw, check, v_all, t_all)])


def solution(mesh):
    in_specs = (
        P(("clip", "proj"), None, None),
        P(("clip", "proj"), None, None),
        P(),
        P(),
        P(),
        P(),
        P(("clip", "proj"), None),
        P(("clip", "proj")),
    )
    out_specs = P(("clip", "proj"), None)
    return jax.shard_map(body, mesh=mesh, in_specs=in_specs, out_specs=out_specs, check_vma=False)
```

```python
import functools
import math

import jax
import jax.numpy as jnp
from jax import lax
from jax.experimental import pallas as pl
from jax.experimental.pallas import tpu as pltpu
from jax.sharding import PartitionSpec as P

MESH = pl.DeviceIdType.MESH
F32, BF16 = jnp.float32, jnp.bfloat16
damp_ratio = 0.1

NY, NX, NZ, XLO = 4, 4, 8, 2
PLANE = NY * NX
TILE = 16
ROWS = 2 * NZ
HALF = PLANE * ROWS
PARTS = 2
DOUBLINGS = 4
REFINEMENTS = 3
MOST_STEPS = 4096
LAST_BITS = 2.0**-22

PLANE_STEPS = sorted(
    ((dy, dx) for dy in range(NY) for dx in range(NX) if (dy, dx) != (0, 0)),
    key=lambda s: -(min(s[0], NY - s[0]) + min(s[1], NX - s[1])),
)
STEPS = len(PLANE_STEPS)
LINE_STEPS = sorted(range(1, NZ), key=lambda d: -min(d, NZ - d))
CHUNKS = 8
ACROSS = (6, 6)
SPLIT = (ACROSS[0] * 128, ACROSS[1] * 128)


def gelu_slope(values):
    normal_cdf = 0.5 * (1.0 + lax.erf(values * math.sqrt(0.5)))
    normal_pdf = jnp.exp(-0.5 * values * values) * (1.0 / math.sqrt(2.0 * math.pi))
    return normal_cdf + values * normal_pdf


def my_place():
    clip, proj = lax.axis_index("clip"), lax.axis_index("proj")
    xh = NX // XLO
    y, z = clip // (xh * NZ), lax.rem(clip, NZ)
    x = lax.rem(clip // NZ, xh) * XLO + proj // 2
    return y, x, z, lax.rem(proj, 2)


def device_at(y, x, z, core):
    return {
        "clip": (y * (NX // XLO) + x // XLO) * NZ + z,
        "proj": lax.rem(x, XLO) * 2 + core,
    }


def mm(a, b):
    return jnp.dot(a, b, preferred_element_type=F32)


def mm_t(a, b):
    return lax.dot_general(a, b, (((1,), (1,)), ((), ())), preferred_element_type=F32)


def pieces(values):
    first = values.astype(BF16).astype(F32)
    rest = values - first
    second = rest.astype(BF16).astype(F32)
    return first, second, rest - second


def stacked(values):
    first, second, third = pieces(values)
    return jnp.concatenate([first, second, third, jnp.zeros_like(first)], axis=0).astype(BF16)


def unstacked(product):
    return product[0:8] + product[8:16] + product[16:24]


def iota(shape, axis):
    return lax.broadcasted_iota(jnp.int32, shape, axis)


def inner(a, b):
    return jnp.sum(a * b, axis=1, keepdims=True)


def spread(ref, values):
    chunks = values.shape[1] // 128
    for c in range(chunks):
        ref[pl.ds(c, 2, stride=chunks), :] = values[:, c * 128 : (c + 1) * 128]
    return ref[...].astype(BF16)


def left_pieces(acts, proj_in):
    tokens, width = acts.shape[0], proj_in.shape[0]
    groups = 128 // width
    per = width // groups
    r, c = iota((128, width), 1), iota((128, width), 0)
    chosen = (c < width) & (r == lax.rem(c, per) * groups + c // per)
    ordered = mm(jnp.where(chosen, 1.0, 0.0).astype(BF16), proj_in).astype(BF16)
    left = mm_t(ordered, acts)
    half = tokens // 2
    rows = []
    for k in range(2):
        lane = iota((per, tokens), 1)
        own = (lane >= k * half) & (lane < (k + 1) * half)
        row = [jnp.where(own, left[j * per : (j + 1) * per], 0.0) for j in range(groups)]
        rows.append(jnp.concatenate(row, axis=1))
    return jnp.concatenate(pieces(jnp.concatenate(rows, axis=0)), axis=0).astype(BF16)


def outer_tile(left, right, in_width):
    width = right.shape[1]
    groups = 128 // width
    wide = jnp.concatenate([right] * groups, axis=1)
    lane = iota(wide.shape, 1) // width
    stack = []
    for piece in pieces(wide):
        masked = [jnp.where(lane == j, piece, 0.0) for j in range(groups)]
        stack.append(jnp.concatenate(masked, axis=0).astype(BF16))
    product = mm(left, jnp.concatenate(stack, axis=1))
    total = None
    for i in (2, 1, 0):
        for j in (2, 1, 0):
            term = product[i * TILE : (i + 1) * TILE, j * 128 : (j + 1) * 128]
            total = term if total is None else total + term
    return total


def target_order(shape):
    j = iota((1, shape[1]), 1)
    k, core = lax.rem(j, 2), lax.rem(j // 2, 2)
    x_lo, z = lax.rem(j // 4, XLO), lax.rem(j // (4 * XLO), NZ)
    rest = j // (4 * XLO * NZ)
    x_hi, y = lax.rem(rest, NX // XLO), rest // (NX // XLO)
    source = core * HALF + (y * NX + x_hi * XLO + x_lo) * ROWS + k * NZ + z
    return jnp.where(iota(shape, 0) == source, 1.0, 0.0).astype(BF16)


def wanted_rows(ids_ref, count):
    y, x, z, core = my_place()
    base = core * HALF + (y * NX + x) * ROWS + z
    lane, sub = iota((8, count), 1), iota((8, count), 0)
    wanted = base + NZ * jnp.where(sub == 0, ids_ref[0], ids_ref[1])
    return jnp.where((lane == wanted) & (sub < 2), 1.0, 0.0)


def form_system(v, split_ref):
    count, width = v.shape
    gram = mm_t(v, v) * (1.0 / count)
    eye = iota((count, count), 0) == iota((count, count), 1)
    diagonal = jnp.sum(jnp.where(eye, gram, 0.0), axis=0, keepdims=True)
    damping = damp_ratio * jnp.sum(diagonal, axis=1, keepdims=True) / width
    system = gram + jnp.where(eye, damping, 0.0)
    for i, piece in enumerate(pieces(system)):
        split_ref[:, i * count : (i + 1) * count] = piece.astype(BF16)
    return system, damping, diagonal + damping, eye


def times_system(p, split_ref, used=3):
    count = split_ref.shape[0]
    product = unstacked(mm(stacked(p), split_ref[:, 0 : used * count]))
    total = product[:, 0:count]
    for i in range(1, used):
        total = total + product[:, i * count : (i + 1) * count]
    return total


def scores_of(sol, v, t, order):
    mixed = unstacked(mm(stacked(sol), v))
    raw = unstacked(mm_t(stacked(mixed), t)) * (1.0 / math.sqrt(v.shape[1]))
    return unstacked(mm(stacked(raw), order))


def approximate_inverse(v, split_ref, m_ref):
    count = v.shape[0]
    system, low, _, eye = form_system(v, split_ref)
    high = split_ref[:, 0:count]
    square = mm(high, high)
    top = jnp.max(jnp.sum(jnp.abs(square), axis=0, keepdims=True), axis=1, keepdims=True)
    top = jnp.sqrt(top) * 1.02
    centre = 2.0 / (top + low)
    t = (top + low) / (top - low)
    t2 = 2.0 * t * t - 1.0
    c = 2.0 * t * t / t2 * centre
    m = jnp.where(eye, 2.0 * c, 0.0) - (c * centre) * system
    am = (2.0 * c) * system - (c * centre) * square
    for i in range(DOUBLINGS):
        t = t2
        t2 = 2.0 * t * t - 1.0
        c = 2.0 * t * t / t2
        rounded = m.astype(BF16)
        if i > 0:
            am = mm(high, rounded)
        m = c * (2.0 * m - mm(rounded, am.astype(BF16)))
    m_ref[...] = m.astype(BF16)
    return top


def refined(rhs, top, split_ref, m_ref):
    def precondition(r):
        return mm(jnp.concatenate([r, jnp.zeros_like(r)], axis=0).astype(BF16), m_ref[...])[0:8]

    sol = precondition(rhs)
    res = rhs - times_system(sol, split_ref, 2)
    for i in range(REFINEMENTS):
        sol = sol + precondition(res)
        res = rhs - times_system(sol, split_ref, 2 if i == 0 else 3)
    excess = inner(res, res) - (LAST_BITS * top) * (LAST_BITS * top) * inner(sol, sol)
    return sol, excess


def main_kernel(
    ids_hbm, acts_hbm, cot_hbm, w_in_hbm, w_out_hbm, proj_in_hbm, proj_out_hbm, test_hbm,
    raw_ref, check_ref, v_all, t_all,
    ids_ref, acts, cot, w_in, w_out, proj_in, proj_out, test,
    tiles, line, plane, v_cross, t_cross, wide, split_ref, m_ref, order_ref,
    load_sem, in_sem, out_sem,
    line_send, line_recv, plane_send, plane_recv,
    rows_send, rows_recv, cross_send, cross_recv, core_send, core_recv,
):
    y, x, z, core = my_place()
    block = w_in.shape[1] // PARTS
    tokens = acts.shape[0] * acts.shape[1]

    small = [
        pltpu.make_async_copy(src, dst, load_sem.at[i])
        for i, (src, dst) in enumerate(
            (
                (acts_hbm, acts),
                (proj_in_hbm, proj_in),
                (cot_hbm, cot),
                (proj_out_hbm, proj_out),
                (test_hbm, test),
                (ids_hbm, ids_ref),
            )
        )
    ]
    loads_in, loads_out = [], []
    for i in range(PARTS):
        part = pl.ds(i * block, block)
        loads_in.append(
            pltpu.make_async_copy(w_in_hbm.at[:, part], w_in.at[:, part], in_sem.at[i])
        )
        loads_out.append(
            pltpu.make_async_copy(w_out_hbm.at[part], w_out.at[part], out_sem.at[i])
        )
    small[4].start()
    small[0].start()
    small[1].start()
    loads_in[0].start()
    small[2].start()
    loads_out[0].start()
    small[3].start()
    for i in range(1, PARTS):
        loads_in[i].start()
        loads_out[i].start()
    small[5].start()

    barrier = pltpu.get_barrier_semaphore()
    on_line = [device_at(y, x, lax.rem(z + d, NZ), core) for d in LINE_STEPS]
    on_plane = [
        device_at(lax.rem(y + dy, NY), lax.rem(x + dx, NX), z, core) for dy, dx in PLANE_STEPS
    ]
    partner = device_at(y, x, z, 1 - core)
    targets = on_line + on_plane + [partner]
    for target in targets:
        pl.semaphore_signal(barrier, inc=1, device_id=target, device_id_type=MESH)

    fulls, crosses = (v_all, t_all), (v_cross, t_cross)
    mine = y * NX + x

    def send(src, dst, send_sem, recv_sem, target):
        pltpu.make_async_remote_copy(
            src_ref=src,
            dst_ref=dst,
            send_sem=send_sem,
            recv_sem=recv_sem,
            device_id=target,
            device_id_type=MESH,
        ).start()

    def await_bytes(ref, sem):
        pltpu.make_async_copy(ref, ref, sem).wait()

    def start_tiles(a, tile):
        tiles[a] = tile
        for target in on_line:
            send(tiles.at[a], line.at[a, z], line_send.at[a], line_recv.at[a], target)
        for target in on_plane:
            send(tiles.at[a], plane.at[a, mine], plane_send.at[a], plane_recv.at[a], target)
        line[a, z] = tile
        plane[a, mine] = tile

    def start_blocks(a):
        full = fulls[a]
        await_bytes(line.at[a, pl.ds(0, NZ - 1)], line_recv.at[a])
        wide[0 : NZ * TILE, :] = line[a].reshape(NZ * TILE, 128).astype(F32)
        for c in range(ACROSS[a]):
            both = [wide[pl.ds(k * CHUNKS + c, NZ, stride=TILE), :] for k in range(2)]
            full[core, mine, :, c * 128 : (c + 1) * 128] = jnp.concatenate(both, axis=0).astype(
                BF16
            )
        rows = full.at[core, mine, :, pl.ds(0, SPLIT[a])]
        for (dy, _), target in zip(PLANE_STEPS, on_plane):
            send(rows, rows, rows_send.at[a], rows_recv.at[dy if a == 0 else NY], target)
        await_bytes(plane.at[a, pl.ds(0, STEPS)], plane_recv.at[a])
        wide[...] = plane[a].reshape(PLANE * TILE, 128).astype(F32)
        for c in range(ACROSS[a], CHUNKS):
            both = [wide[pl.ds(k * CHUNKS + c, PLANE, stride=TILE), :] for k in range(2)]
            at = c - ACROSS[a]
            crosses[a][z, :, at * 128 : (at + 1) * 128] = jnp.concatenate(both, axis=0).astype(BF16)
        rows = crosses[a].at[z]
        for target in on_line:
            send(rows, rows, cross_send.at[a], cross_recv.at[a], target)

    def place_cross(a):
        await_bytes(crosses[a].at[pl.ds(0, NZ - 1)], cross_recv.at[a])
        for c in range(ACROSS[a], CHUNKS):
            at = c - ACROSS[a]
            columns = crosses[a][:, :, at * 128 : (at + 1) * 128]
            wide[...] = columns.reshape(NZ * 2 * PLANE, 128).astype(F32)
            for p in range(PLANE):
                both = [wide[pl.ds(k * PLANE + p, NZ, stride=2 * PLANE), :] for k in range(2)]
                fulls[a][core, p, :, c * 128 : (c + 1) * 128] = jnp.concatenate(
                    both, axis=0
                ).astype(BF16)

    def core_copy(i, rows):
        return pltpu.make_async_remote_copy(
            src_ref=rows,
            dst_ref=rows,
            send_sem=core_send.at[i],
            recv_sem=core_recv.at[i],
            device_id=partner,
            device_id_type=MESH,
        )

    small[4].wait()
    t_tile = spread(wide.at[pl.ds(0, TILE)], test[...].astype(F32))
    pl.semaphore_wait(barrier, len(targets))
    start_tiles(1, t_tile)

    small[0].wait()
    small[1].wait()
    left = left_pieces(acts[...].reshape(tokens, -1), proj_in[...])
    small[2].wait()
    small[3].wait()
    right = None
    for i in range(PARTS):
        loads_in[i].wait()
        loads_out[i].wait()
        part = slice(i * block, (i + 1) * block)
        preact = mm(acts[...].reshape(tokens, -1), w_in[:, part])
        backprop = mm_t(cot[...].reshape(tokens, -1), w_out[part])
        deltas = (backprop * gelu_slope(preact)).astype(BF16)
        term = mm_t(deltas, proj_out[:, part])
        right = term if right is None else right + term
    outer = outer_tile(left, right, proj_in.shape[0])
    start_tiles(0, (outer * (1.0 / math.sqrt(acts.shape[1]))).astype(BF16))
    start_blocks(0)
    order_ref[...] = target_order(order_ref.shape)

    copies = []

    def forward(i, rows):
        copies.append(core_copy(i, rows))
        copies[-1].start()

    for dy in (0, 1, 3, 2):
        if dy == 2:
            place_cross(0)
            forward(0, v_all.at[core, :, :, pl.ds(SPLIT[0], (CHUNKS - ACROSS[0]) * 128)])
        first = lax.rem(y + NY - dy, NY) * NX
        count = NX - (dy == 0)
        await_bytes(v_all.at[core, pl.ds(first, count), :, pl.ds(0, SPLIT[0])], rows_recv.at[dy])
        forward(dy + 1, v_all.at[core, pl.ds(first, NX), :, pl.ds(0, SPLIT[0])])
        if dy == 0:
            start_blocks(1)
    for copy in copies:
        copy.wait_recv()

    small[5].wait()
    v = v_all[...].reshape(2 * HALF, -1)
    top = approximate_inverse(v, split_ref, m_ref)
    place_cross(1)
    await_bytes(t_all.at[core, pl.ds(0, STEPS), :, pl.ds(0, SPLIT[1])], rows_recv.at[NY])
    forward(NY + 1, t_all.at[core])
    sol, excess = refined(wanted_rows(ids_ref, 2 * HALF), top, split_ref, m_ref)
    copies[-1].wait_recv()
    raw = scores_of(sol, v, t_all[...].reshape(2 * HALF, -1), order_ref[...])
    raw_ref[...] = raw[0:2]
    check_ref[...] = jnp.broadcast_to(excess, check_ref.shape)
    for a in range(2):
        await_bytes(line.at[a, pl.ds(0, NZ - 1)], line_send.at[a])
        await_bytes(plane.at[a, pl.ds(0, STEPS)], plane_send.at[a])
        await_bytes(fulls[a].at[core, pl.ds(0, STEPS), :, pl.ds(0, SPLIT[a])], rows_send.at[a])
        await_bytes(crosses[a].at[pl.ds(0, NZ - 1)], cross_send.at[a])
    for copy in copies:
        copy.wait_send()


def finish_kernel(ids_ref, raw_ref, check_ref, v_ref, t_ref, out_hbm, late_ref, split_ref, sem):
    copy = pltpu.make_async_copy(raw_ref, out_hbm, sem)
    copy.start()
    excess = check_ref[...]
    fine = jnp.min(jnp.where(excess <= 0.0, 1.0, 0.0))
    copy.wait()

    @pl.when(fine < 1.0)
    def _():
        count = 2 * HALF
        v, t = v_ref[...].reshape(count, -1), t_ref[...].reshape(count, -1)
        _, _, diagonal, _ = form_system(v, split_ref)
        rhs = wanted_rows(ids_ref, count)
        scale = 1.0 / diagonal

        def ratio(a, b):
            return jnp.where(b > 0.0, a / jnp.where(b > 0.0, b, 1.0), 0.0)

        def unfinished(state):
            step, _, _, _, rz = state
            return (step < MOST_STEPS) & (jnp.max(rz - goal) > 0.0)

        def advance(state):
            step, sol, res, p, rz = state
            q = times_system(p, split_ref)
            alpha = ratio(rz, inner(p, q))
            sol = sol + alpha * p
            res = res - alpha * q
            zed = res * scale
            new = inner(res, zed)
            p = zed + ratio(new, rz) * p
            return step + 1, sol, res, p, new

        zed = rhs * scale
        rz = inner(rhs, zed)
        goal = rz * 1e-12
        state = (jnp.int32(0), jnp.zeros_like(rhs), rhs, zed, rz)
        sol = lax.while_loop(unfinished, advance, state)[1]
        late_ref[...] = scores_of(sol, v, t, target_order((count, count)))[0:2]
        again = pltpu.make_async_copy(late_ref, out_hbm, sem)
        again.start()
        again.wait()


def body(
    clip_acts, clip_cotangents, weight_in, weight_out, proj_in, proj_out, test_grads, clip_ids
):
    width = proj_in.shape[1] * proj_out.shape[1]
    proj_in, proj_out = proj_in.T, proj_out.T
    count = 2 * HALF
    full = jax.ShapeDtypeStruct((2, PLANE, ROWS, width), BF16)
    vmem = pl.BlockSpec(memory_space=pltpu.VMEM)
    smem = pl.BlockSpec(memory_space=pltpu.SMEM)
    hbm = pl.BlockSpec(memory_space=pl.ANY)
    dma = pltpu.SemaphoreType.DMA

    def like(array):
        return pltpu.VMEM(array.shape, array.dtype)

    raw, check, v_all, t_all = pl.pallas_call(
        main_kernel,
        out_shape=(
            pltpu.VMEM((2, count), F32),
            pltpu.VMEM((8, 128), F32),
            pltpu.VMEM(full.shape, BF16),
            pltpu.VMEM(full.shape, BF16),
        ),
        in_specs=[hbm] * 8,
        out_specs=(vmem, vmem, vmem, vmem),
        scratch_shapes=[
            pltpu.SMEM(clip_ids.shape, clip_ids.dtype),
            like(clip_acts),
            like(clip_cotangents),
            like(weight_in),
            like(weight_out),
            like(proj_in),
            like(proj_out),
            like(test_grads),
            pltpu.VMEM((2, TILE, 128), BF16),
            pltpu.VMEM((2, NZ, TILE, 128), BF16),
            pltpu.VMEM((2, PLANE, TILE, 128), BF16),
            pltpu.VMEM((NZ, 2 * PLANE, (CHUNKS - ACROSS[0]) * 128), BF16),
            pltpu.VMEM((NZ, 2 * PLANE, (CHUNKS - ACROSS[1]) * 128), BF16),
            pltpu.VMEM((PLANE * TILE, 128), F32),
            pltpu.VMEM((count, 3 * count), BF16),
            pltpu.VMEM((count, count), BF16),
            pltpu.VMEM((count, count), BF16),
            dma((6,)),
            dma((PARTS,)),
            dma((PARTS,)),
            dma((2,)),
            dma((2,)),
            dma((2,)),
            dma((2,)),
            dma((2,)),
            dma((NY + 1,)),
            dma((2,)),
            dma((2,)),
            dma((NY + 2,)),
            dma((NY + 2,)),
        ],
        compiler_params=pltpu.CompilerParams(
            collective_id=0, has_side_effects=True, vmem_limit_bytes=56 << 20
        ),
    )(
        clip_ids,
        clip_acts,
        clip_cotangents,
        weight_in,
        weight_out,
        proj_in,
        proj_out,
        test_grads,
    )
    return pl.pallas_call(
        finish_kernel,
        out_shape=jax.ShapeDtypeStruct((2, count), F32),
        in_specs=[smem, vmem, vmem, vmem, vmem],
        out_specs=hbm,
        scratch_shapes=[
            pltpu.VMEM((2, count), F32),
            pltpu.VMEM((count, 3 * count), BF16),
            dma,
        ],
        compiler_params=pltpu.CompilerParams(vmem_limit_bytes=32 << 20),
    )(clip_ids, *[pltpu.with_memory_space_constraint(r, pltpu.VMEM) for r in (raw, check, v_all, t_all)])


def solution(mesh):
    in_specs = (
        P(("clip", "proj"), None, None),
        P(("clip", "proj"), None, None),
        P(),
        P(),
        P(),
        P(),
        P(("clip", "proj"), None),
        P(("clip", "proj")),
    )
    out_specs = P(("clip", "proj"), None)
    return jax.shard_map(body, mesh=mesh, in_specs=in_specs, out_specs=out_specs, check_vma=False)
```

```python
import functools
import math

import jax
import jax.numpy as jnp
from jax import lax
from jax.experimental import pallas as pl
from jax.experimental.pallas import tpu as pltpu
from jax.sharding import PartitionSpec as P

MESH = pl.DeviceIdType.MESH
F32, BF16 = jnp.float32, jnp.bfloat16
damp_ratio = 0.1

NY, NX, NZ, XLO = 4, 4, 8, 2
PLANE = NY * NX
TILE = 16
ROWS = 2 * NZ
HALF = PLANE * ROWS
PARTS = 2
DOUBLINGS = 4
REFINEMENTS = 3
MOST_STEPS = 4096
LAST_BITS = 2.0**-22

PLANE_STEPS = sorted(
    ((dy, dx) for dy in range(NY) for dx in range(NX) if (dy, dx) != (0, 0)),
    key=lambda s: -(min(s[0], NY - s[0]) + min(s[1], NX - s[1])),
)
STEPS = len(PLANE_STEPS)
LINE_STEPS = sorted(range(1, NZ), key=lambda d: -min(d, NZ - d))
CHUNKS = 8
ACROSS = (6, 6)
SPLIT = (ACROSS[0] * 128, ACROSS[1] * 128)


def gelu_slope(values):
    normal_cdf = 0.5 * (1.0 + lax.erf(values * math.sqrt(0.5)))
    normal_pdf = jnp.exp(-0.5 * values * values) * (1.0 / math.sqrt(2.0 * math.pi))
    return normal_cdf + values * normal_pdf


def my_place():
    clip, proj = lax.axis_index("clip"), lax.axis_index("proj")
    xh = NX // XLO
    y, z = clip // (xh * NZ), lax.rem(clip, NZ)
    x = lax.rem(clip // NZ, xh) * XLO + proj // 2
    return y, x, z, lax.rem(proj, 2)


def device_at(y, x, z, core):
    return {
        "clip": (y * (NX // XLO) + x // XLO) * NZ + z,
        "proj": lax.rem(x, XLO) * 2 + core,
    }


def mm(a, b):
    return jnp.dot(a, b, preferred_element_type=F32)


def mm_t(a, b):
    return lax.dot_general(a, b, (((1,), (1,)), ((), ())), preferred_element_type=F32)


def pieces(values):
    first = values.astype(BF16).astype(F32)
    rest = values - first
    second = rest.astype(BF16).astype(F32)
    return first, second, rest - second


def stacked(values):
    first, second, third = pieces(values)
    return jnp.concatenate([first, second, third, jnp.zeros_like(first)], axis=0).astype(BF16)


def unstacked(product):
    return product[0:8] + product[8:16] + product[16:24]


def iota(shape, axis):
    return lax.broadcasted_iota(jnp.int32, shape, axis)


def inner(a, b):
    return jnp.sum(a * b, axis=1, keepdims=True)


def spread(ref, values):
    chunks = values.shape[1] // 128
    for c in range(chunks):
        ref[pl.ds(c, 2, stride=chunks), :] = values[:, c * 128 : (c + 1) * 128]
    return ref[...].astype(BF16)


def left_pieces(acts, proj_in):
    tokens, width = acts.shape[0], proj_in.shape[0]
    groups = 128 // width
    per = width // groups
    r, c = iota((128, width), 1), iota((128, width), 0)
    chosen = (c < width) & (r == lax.rem(c, per) * groups + c // per)
    ordered = mm(jnp.where(chosen, 1.0, 0.0).astype(BF16), proj_in).astype(BF16)
    left = mm_t(ordered, acts)
    half = tokens // 2
    rows = []
    for k in range(2):
        lane = iota((per, tokens), 1)
        own = (lane >= k * half) & (lane < (k + 1) * half)
        row = [jnp.where(own, left[j * per : (j + 1) * per], 0.0) for j in range(groups)]
        rows.append(jnp.concatenate(row, axis=1))
    return jnp.concatenate(pieces(jnp.concatenate(rows, axis=0)), axis=0).astype(BF16)


def outer_tile(left, right, in_width):
    width = right.shape[1]
    groups = 128 // width
    wide = jnp.concatenate([right] * groups, axis=1)
    lane = iota(wide.shape, 1) // width
    stack = []
    for piece in pieces(wide):
        masked = [jnp.where(lane == j, piece, 0.0) for j in range(groups)]
        stack.append(jnp.concatenate(masked, axis=0).astype(BF16))
    product = mm(left, jnp.concatenate(stack, axis=1))
    total = None
    for i in (2, 1, 0):
        for j in (2, 1, 0):
            term = product[i * TILE : (i + 1) * TILE, j * 128 : (j + 1) * 128]
            total = term if total is None else total + term
    return total


def target_order(shape):
    j = iota((1, shape[1]), 1)
    k, core = lax.rem(j, 2), lax.rem(j // 2, 2)
    x_lo, z = lax.rem(j // 4, XLO), lax.rem(j // (4 * XLO), NZ)
    rest = j // (4 * XLO * NZ)
    x_hi, y = lax.rem(rest, NX // XLO), rest // (NX // XLO)
    source = core * HALF + (y * NX + x_hi * XLO + x_lo) * ROWS + k * NZ + z
    return jnp.where(iota(shape, 0) == source, 1.0, 0.0).astype(BF16)


def wanted_rows(ids_ref, count):
    y, x, z, core = my_place()
    base = core * HALF + (y * NX + x) * ROWS + z
    lane, sub = iota((8, count), 1), iota((8, count), 0)
    wanted = base + NZ * jnp.where(sub == 0, ids_ref[0], ids_ref[1])
    return jnp.where((lane == wanted) & (sub < 2), 1.0, 0.0)


def form_system(v, split_ref, gram=None):
    count, width = v.shape
    gram = (mm_t(v, v) if gram is None else gram) * (1.0 / count)
    eye = iota((count, count), 0) == iota((count, count), 1)
    diagonal = jnp.sum(jnp.where(eye, gram, 0.0), axis=0, keepdims=True)
    damping = damp_ratio * jnp.sum(diagonal, axis=1, keepdims=True) / width
    system = gram + jnp.where(eye, damping, 0.0)
    for i, piece in enumerate(pieces(system)):
        split_ref[:, i * count : (i + 1) * count] = piece.astype(BF16)
    return system, damping, diagonal + damping, eye


def times_system(p, split_ref, used=3):
    count = split_ref.shape[0]
    product = unstacked(mm(stacked(p), split_ref[:, 0 : used * count]))
    total = product[:, 0:count]
    for i in range(1, used):
        total = total + product[:, i * count : (i + 1) * count]
    return total


def scores_of(sol, v, t, order):
    mixed = unstacked(mm(stacked(sol), v))
    raw = unstacked(mm_t(stacked(mixed), t)) * (1.0 / math.sqrt(v.shape[1]))
    return unstacked(mm(stacked(raw), order))


def approximate_inverse(v, split_ref, m_ref, gram):
    count = v.shape[0]
    system, low, _, eye = form_system(v, split_ref, gram)
    high = split_ref[:, 0:count]
    square = mm(high, high)
    top = jnp.max(jnp.sum(jnp.abs(square), axis=0, keepdims=True), axis=1, keepdims=True)
    top = jnp.sqrt(top) * 1.02
    centre = 2.0 / (top + low)
    t = (top + low) / (top - low)
    t2 = 2.0 * t * t - 1.0
    c = 2.0 * t * t / t2 * centre
    m = jnp.where(eye, 2.0 * c, 0.0) - (c * centre) * system
    am = (2.0 * c) * system - (c * centre) * square
    for i in range(DOUBLINGS):
        t = t2
        t2 = 2.0 * t * t - 1.0
        c = 2.0 * t * t / t2
        rounded = m.astype(BF16)
        if i > 0:
            am = mm(high, rounded)
        m = c * (2.0 * m - mm(rounded, am.astype(BF16)))
    m_ref[...] = m.astype(BF16)
    return top


def refined(rhs, top, split_ref, m_ref):
    def precondition(r):
        return mm(jnp.concatenate([r, jnp.zeros_like(r)], axis=0).astype(BF16), m_ref[...])[0:8]

    sol = precondition(rhs)
    res = rhs - times_system(sol, split_ref, 2)
    for i in range(REFINEMENTS):
        sol = sol + precondition(res)
        res = rhs - times_system(sol, split_ref, 2 if i == 0 else 3)
    excess = inner(res, res) - (LAST_BITS * top) * (LAST_BITS * top) * inner(sol, sol)
    return sol, excess


def main_kernel(
    ids_hbm, acts_hbm, cot_hbm, w_in_hbm, w_out_hbm, proj_in_hbm, proj_out_hbm, test_hbm,
    raw_ref, check_ref, v_all, t_all,
    ids_ref, acts, cot, w_in, w_out, proj_in, proj_out, test,
    tiles, line, plane, v_cross, t_cross, wide, split_ref, m_ref, order_ref, gram_ref,
    load_sem, in_sem, out_sem,
    line_send, line_recv, plane_send, plane_recv,
    rows_send, rows_recv, cross_send, cross_recv, core_send, core_recv,
):
    y, x, z, core = my_place()
    block = w_in.shape[1] // PARTS
    tokens = acts.shape[0] * acts.shape[1]

    small = [
        pltpu.make_async_copy(src, dst, load_sem.at[i])
        for i, (src, dst) in enumerate(
            (
                (acts_hbm, acts),
                (proj_in_hbm, proj_in),
                (cot_hbm, cot),
                (proj_out_hbm, proj_out),
                (test_hbm, test),
                (ids_hbm, ids_ref),
            )
        )
    ]
    loads_in, loads_out = [], []
    for i in range(PARTS):
        part = pl.ds(i * block, block)
        loads_in.append(
            pltpu.make_async_copy(w_in_hbm.at[:, part], w_in.at[:, part], in_sem.at[i])
        )
        loads_out.append(
            pltpu.make_async_copy(w_out_hbm.at[part], w_out.at[part], out_sem.at[i])
        )
    small[4].start()
    small[0].start()
    small[1].start()
    loads_in[0].start()
    small[2].start()
    loads_out[0].start()
    small[3].start()
    for i in range(1, PARTS):
        loads_in[i].start()
        loads_out[i].start()
    small[5].start()

    barrier = pltpu.get_barrier_semaphore()
    on_line = [device_at(y, x, lax.rem(z + d, NZ), core) for d in LINE_STEPS]
    on_plane = [
        device_at(lax.rem(y + dy, NY), lax.rem(x + dx, NX), z, core) for dy, dx in PLANE_STEPS
    ]
    partner = device_at(y, x, z, 1 - core)
    targets = on_line + on_plane + [partner]
    for target in targets:
        pl.semaphore_signal(barrier, inc=1, device_id=target, device_id_type=MESH)

    fulls, crosses = (v_all, t_all), (v_cross, t_cross)
    mine = y * NX + x

    def send(src, dst, send_sem, recv_sem, target):
        pltpu.make_async_remote_copy(
            src_ref=src,
            dst_ref=dst,
            send_sem=send_sem,
            recv_sem=recv_sem,
            device_id=target,
            device_id_type=MESH,
        ).start()

    def await_bytes(ref, sem):
        pltpu.make_async_copy(ref, ref, sem).wait()

    def start_tiles(a, tile):
        tiles[a] = tile
        for target in on_line:
            send(tiles.at[a], line.at[a, z], line_send.at[a], line_recv.at[a], target)
        for target in on_plane:
            send(tiles.at[a], plane.at[a, mine], plane_send.at[a], plane_recv.at[a], target)
        line[a, z] = tile
        plane[a, mine] = tile

    def start_blocks(a):
        full = fulls[a]
        await_bytes(line.at[a, pl.ds(0, NZ - 1)], line_recv.at[a])
        wide[0 : NZ * TILE, :] = line[a].reshape(NZ * TILE, 128).astype(F32)
        for c in range(ACROSS[a]):
            both = [wide[pl.ds(k * CHUNKS + c, NZ, stride=TILE), :] for k in range(2)]
            full[core, mine, :, c * 128 : (c + 1) * 128] = jnp.concatenate(both, axis=0).astype(
                BF16
            )
        rows = full.at[core, mine, :, pl.ds(0, SPLIT[a])]
        for (dy, _), target in zip(PLANE_STEPS, on_plane):
            send(rows, rows, rows_send.at[a], rows_recv.at[dy if a == 0 else NY], target)
        await_bytes(plane.at[a, pl.ds(0, STEPS)], plane_recv.at[a])
        wide[...] = plane[a].reshape(PLANE * TILE, 128).astype(F32)
        for c in range(ACROSS[a], CHUNKS):
            both = [wide[pl.ds(k * CHUNKS + c, PLANE, stride=TILE), :] for k in range(2)]
            at = c - ACROSS[a]
            crosses[a][z, :, at * 128 : (at + 1) * 128] = jnp.concatenate(both, axis=0).astype(BF16)
        rows = crosses[a].at[z]
        for target in on_line:
            send(rows, rows, cross_send.at[a], cross_recv.at[a], target)

    def place_cross(a):
        await_bytes(crosses[a].at[pl.ds(0, NZ - 1)], cross_recv.at[a])
        for c in range(ACROSS[a], CHUNKS):
            at = c - ACROSS[a]
            columns = crosses[a][:, :, at * 128 : (at + 1) * 128]
            wide[...] = columns.reshape(NZ * 2 * PLANE, 128).astype(F32)
            for p in range(PLANE):
                both = [wide[pl.ds(k * PLANE + p, NZ, stride=2 * PLANE), :] for k in range(2)]
                fulls[a][core, p, :, c * 128 : (c + 1) * 128] = jnp.concatenate(
                    both, axis=0
                ).astype(BF16)

    def core_copy(i, rows):
        return pltpu.make_async_remote_copy(
            src_ref=rows,
            dst_ref=rows,
            send_sem=core_send.at[i],
            recv_sem=core_recv.at[i],
            device_id=partner,
            device_id_type=MESH,
        )

    small[4].wait()
    t_tile = spread(wide.at[pl.ds(0, TILE)], test[...].astype(F32))
    pl.semaphore_wait(barrier, len(targets))
    start_tiles(1, t_tile)

    small[0].wait()
    small[1].wait()
    left = left_pieces(acts[...].reshape(tokens, -1), proj_in[...])
    small[2].wait()
    small[3].wait()
    right = None
    for i in range(PARTS):
        loads_in[i].wait()
        loads_out[i].wait()
        part = slice(i * block, (i + 1) * block)
        preact = mm(acts[...].reshape(tokens, -1), w_in[:, part])
        backprop = mm_t(cot[...].reshape(tokens, -1), w_out[part])
        deltas = (backprop * gelu_slope(preact)).astype(BF16)
        term = mm_t(deltas, proj_out[:, part])
        right = term if right is None else right + term
    outer = outer_tile(left, right, proj_in.shape[0])
    start_tiles(0, (outer * (1.0 / math.sqrt(acts.shape[1]))).astype(BF16))
    start_blocks(0)
    order_ref[...] = target_order(order_ref.shape)

    copies = []

    def forward(i, rows):
        copies.append(core_copy(i, rows))
        copies[-1].start()

    for dy in (0, 1, 3, 2):
        if dy == 2:
            place_cross(0)
            forward(0, v_all.at[core, :, :, pl.ds(SPLIT[0], (CHUNKS - ACROSS[0]) * 128)])
        first = lax.rem(y + NY - dy, NY) * NX
        count = NX - (dy == 0)
        await_bytes(v_all.at[core, pl.ds(first, count), :, pl.ds(0, SPLIT[0])], rows_recv.at[dy])
        forward(dy + 1, v_all.at[core, pl.ds(first, NX), :, pl.ds(0, SPLIT[0])])
        if dy == 0:
            start_blocks(1)
    own_rows = pl.ds(pl.multiple_of(core * HALF, HALF), HALF)
    other_rows = pl.ds(pl.multiple_of((1 - core) * HALF, HALF), HALF)
    own = v_all[core].reshape(HALF, -1)
    gram_ref[own_rows, own_rows] = mm_t(own, own)
    for copy in copies:
        copy.wait_recv()

    small[5].wait()
    v = v_all[...].reshape(2 * HALF, -1)
    gram_ref[other_rows, :] = mm_t(v_all[1 - core].reshape(HALF, -1), v)
    gram_ref[own_rows, other_rows] = mm_t(
        v_all[core].reshape(HALF, -1), v_all[1 - core].reshape(HALF, -1)
    )
    top = approximate_inverse(v, split_ref, m_ref, gram_ref[...])
    place_cross(1)
    await_bytes(t_all.at[core, pl.ds(0, STEPS), :, pl.ds(0, SPLIT[1])], rows_recv.at[NY])
    forward(NY + 1, t_all.at[core])
    sol, excess = refined(wanted_rows(ids_ref, 2 * HALF), top, split_ref, m_ref)
    copies[-1].wait_recv()
    raw = scores_of(sol, v, t_all[...].reshape(2 * HALF, -1), order_ref[...])
    raw_ref[...] = raw[0:2]
    check_ref[...] = jnp.broadcast_to(excess, check_ref.shape)
    for a in range(2):
        await_bytes(line.at[a, pl.ds(0, NZ - 1)], line_send.at[a])
        await_bytes(plane.at[a, pl.ds(0, STEPS)], plane_send.at[a])
        await_bytes(fulls[a].at[core, pl.ds(0, STEPS), :, pl.ds(0, SPLIT[a])], rows_send.at[a])
        await_bytes(crosses[a].at[pl.ds(0, NZ - 1)], cross_send.at[a])
    for copy in copies:
        copy.wait_send()


def finish_kernel(ids_ref, raw_ref, check_ref, v_ref, t_ref, out_hbm, late_ref, split_ref, sem):
    copy = pltpu.make_async_copy(raw_ref, out_hbm, sem)
    copy.start()
    excess = check_ref[...]
    fine = jnp.min(jnp.where(excess <= 0.0, 1.0, 0.0))
    copy.wait()

    @pl.when(fine < 1.0)
    def _():
        count = 2 * HALF
        v, t = v_ref[...].reshape(count, -1), t_ref[...].reshape(count, -1)
        _, _, diagonal, _ = form_system(v, split_ref)
        rhs = wanted_rows(ids_ref, count)
        scale = 1.0 / diagonal

        def ratio(a, b):
            return jnp.where(b > 0.0, a / jnp.where(b > 0.0, b, 1.0), 0.0)

        def unfinished(state):
            step, _, _, _, rz = state
            return (step < MOST_STEPS) & (jnp.max(rz - goal) > 0.0)

        def advance(state):
            step, sol, res, p, rz = state
            q = times_system(p, split_ref)
            alpha = ratio(rz, inner(p, q))
            sol = sol + alpha * p
            res = res - alpha * q
            zed = res * scale
            new = inner(res, zed)
            p = zed + ratio(new, rz) * p
            return step + 1, sol, res, p, new

        zed = rhs * scale
        rz = inner(rhs, zed)
        goal = rz * 1e-12
        state = (jnp.int32(0), jnp.zeros_like(rhs), rhs, zed, rz)
        sol = lax.while_loop(unfinished, advance, state)[1]
        late_ref[...] = scores_of(sol, v, t, target_order((count, count)))[0:2]
        again = pltpu.make_async_copy(late_ref, out_hbm, sem)
        again.start()
        again.wait()


def body(
    clip_acts, clip_cotangents, weight_in, weight_out, proj_in, proj_out, test_grads, clip_ids
):
    width = proj_in.shape[1] * proj_out.shape[1]
    proj_in, proj_out = proj_in.T, proj_out.T
    count = 2 * HALF
    full = jax.ShapeDtypeStruct((2, PLANE, ROWS, width), BF16)
    vmem = pl.BlockSpec(memory_space=pltpu.VMEM)
    smem = pl.BlockSpec(memory_space=pltpu.SMEM)
    hbm = pl.BlockSpec(memory_space=pl.ANY)
    dma = pltpu.SemaphoreType.DMA

    def like(array):
        return pltpu.VMEM(array.shape, array.dtype)

    raw, check, v_all, t_all = pl.pallas_call(
        main_kernel,
        out_shape=(
            pltpu.VMEM((2, count), F32),
            pltpu.VMEM((8, 128), F32),
            pltpu.VMEM(full.shape, BF16),
            pltpu.VMEM(full.shape, BF16),
        ),
        in_specs=[hbm] * 8,
        out_specs=(vmem, vmem, vmem, vmem),
        scratch_shapes=[
            pltpu.SMEM(clip_ids.shape, clip_ids.dtype),
            like(clip_acts),
            like(clip_cotangents),
            like(weight_in),
            like(weight_out),
            like(proj_in),
            like(proj_out),
            like(test_grads),
            pltpu.VMEM((2, TILE, 128), BF16),
            pltpu.VMEM((2, NZ, TILE, 128), BF16),
            pltpu.VMEM((2, PLANE, TILE, 128), BF16),
            pltpu.VMEM((NZ, 2 * PLANE, (CHUNKS - ACROSS[0]) * 128), BF16),
            pltpu.VMEM((NZ, 2 * PLANE, (CHUNKS - ACROSS[1]) * 128), BF16),
            pltpu.VMEM((PLANE * TILE, 128), F32),
            pltpu.VMEM((count, 3 * count), BF16),
            pltpu.VMEM((count, count), BF16),
            pltpu.VMEM((count, count), BF16),
            pltpu.VMEM((count, count), F32),
            dma((6,)),
            dma((PARTS,)),
            dma((PARTS,)),
            dma((2,)),
            dma((2,)),
            dma((2,)),
            dma((2,)),
            dma((2,)),
            dma((NY + 1,)),
            dma((2,)),
            dma((2,)),
            dma((NY + 2,)),
            dma((NY + 2,)),
        ],
        compiler_params=pltpu.CompilerParams(
            collective_id=0, has_side_effects=True, vmem_limit_bytes=56 << 20
        ),
    )(
        clip_ids,
        clip_acts,
        clip_cotangents,
        weight_in,
        weight_out,
        proj_in,
        proj_out,
        test_grads,
    )
    return pl.pallas_call(
        finish_kernel,
        out_shape=jax.ShapeDtypeStruct((2, count), F32),
        in_specs=[smem, vmem, vmem, vmem, vmem],
        out_specs=hbm,
        scratch_shapes=[
            pltpu.VMEM((2, count), F32),
            pltpu.VMEM((count, 3 * count), BF16),
            dma,
        ],
        compiler_params=pltpu.CompilerParams(vmem_limit_bytes=32 << 20),
    )(clip_ids, *[pltpu.with_memory_space_constraint(r, pltpu.VMEM) for r in (raw, check, v_all, t_all)])


def solution(mesh):
    in_specs = (
        P(("clip", "proj"), None, None),
        P(("clip", "proj"), None, None),
        P(),
        P(),
        P(),
        P(),
        P(("clip", "proj"), None),
        P(("clip", "proj")),
    )
    out_specs = P(("clip", "proj"), None)
    return jax.shard_map(body, mesh=mesh, in_specs=in_specs, out_specs=out_specs, check_vma=False)
```

```python
import functools
import math

import jax
import jax.numpy as jnp
from jax import lax
from jax.experimental import pallas as pl
from jax.experimental.pallas import tpu as pltpu
from jax.sharding import PartitionSpec as P

MESH = pl.DeviceIdType.MESH
F32, BF16 = jnp.float32, jnp.bfloat16
damp_ratio = 0.1

NY, NX, NZ, XLO = 4, 4, 8, 2
PLANE = NY * NX
TILE = 16
ROWS = 2 * NZ
HALF = PLANE * ROWS
PARTS = 2
DOUBLINGS = 4
REFINEMENTS = 3
MOST_STEPS = 4096
LAST_BITS = 2.0**-22

PLANE_STEPS = sorted(
    ((dy, dx) for dy in range(NY) for dx in range(NX) if (dy, dx) != (0, 0)),
    key=lambda s: -(min(s[0], NY - s[0]) + min(s[1], NX - s[1])),
)
STEPS = len(PLANE_STEPS)
LINE_STEPS = sorted(range(1, NZ), key=lambda d: -min(d, NZ - d))
CHUNKS = 8
ACROSS = (6, 6)
SPLIT = (ACROSS[0] * 128, ACROSS[1] * 128)


def gelu_slope(values):
    normal_cdf = 0.5 * (1.0 + lax.erf(values * math.sqrt(0.5)))
    normal_pdf = jnp.exp(-0.5 * values * values) * (1.0 / math.sqrt(2.0 * math.pi))
    return normal_cdf + values * normal_pdf


def my_place():
    clip, proj = lax.axis_index("clip"), lax.axis_index("proj")
    xh = NX // XLO
    y, z = clip // (xh * NZ), lax.rem(clip, NZ)
    x = lax.rem(clip // NZ, xh) * XLO + proj // 2
    return y, x, z, lax.rem(proj, 2)


def device_at(y, x, z, core):
    return {
        "clip": (y * (NX // XLO) + x // XLO) * NZ + z,
        "proj": lax.rem(x, XLO) * 2 + core,
    }


def mm(a, b):
    return jnp.dot(a, b, preferred_element_type=F32)


def mm_t(a, b):
    return lax.dot_general(a, b, (((1,), (1,)), ((), ())), preferred_element_type=F32)


def pieces(values):
    first = values.astype(BF16).astype(F32)
    rest = values - first
    second = rest.astype(BF16).astype(F32)
    return first, second, rest - second


def stacked(values):
    first, second, third = pieces(values)
    return jnp.concatenate([first, second, third, jnp.zeros_like(first)], axis=0).astype(BF16)


def unstacked(product):
    return product[0:8] + product[8:16] + product[16:24]


def iota(shape, axis):
    return lax.broadcasted_iota(jnp.int32, shape, axis)


def inner(a, b):
    return jnp.sum(a * b, axis=1, keepdims=True)


def spread(ref, values):
    chunks = values.shape[1] // 128
    for c in range(chunks):
        ref[pl.ds(c, 2, stride=chunks), :] = values[:, c * 128 : (c + 1) * 128]
    return ref[...].astype(BF16)


def left_pieces(acts, proj_in):
    tokens, width = acts.shape[0], proj_in.shape[0]
    groups = 128 // width
    per = width // groups
    r, c = iota((128, width), 1), iota((128, width), 0)
    chosen = (c < width) & (r == lax.rem(c, per) * groups + c // per)
    ordered = mm(jnp.where(chosen, 1.0, 0.0).astype(BF16), proj_in).astype(BF16)
    left = mm_t(ordered, acts)
    half = tokens // 2
    rows = []
    for k in range(2):
        lane = iota((per, tokens), 1)
        own = (lane >= k * half) & (lane < (k + 1) * half)
        row = [jnp.where(own, left[j * per : (j + 1) * per], 0.0) for j in range(groups)]
        rows.append(jnp.concatenate(row, axis=1))
    return jnp.concatenate(pieces(jnp.concatenate(rows, axis=0)), axis=0).astype(BF16)


def outer_tile(left, right, in_width):
    width = right.shape[1]
    groups = 128 // width
    wide = jnp.concatenate([right] * groups, axis=1)
    lane = iota(wide.shape, 1) // width
    stack = []
    for piece in pieces(wide):
        masked = [jnp.where(lane == j, piece, 0.0) for j in range(groups)]
        stack.append(jnp.concatenate(masked, axis=0).astype(BF16))
    product = mm(left, jnp.concatenate(stack, axis=1))
    total = None
    for i in (2, 1, 0):
        for j in (2, 1, 0):
            term = product[i * TILE : (i + 1) * TILE, j * 128 : (j + 1) * 128]
            total = term if total is None else total + term
    return total


def target_order(shape):
    j = iota((1, shape[1]), 1)
    k, core = lax.rem(j, 2), lax.rem(j // 2, 2)
    x_lo, z = lax.rem(j // 4, XLO), lax.rem(j // (4 * XLO), NZ)
    rest = j // (4 * XLO * NZ)
    x_hi, y = lax.rem(rest, NX // XLO), rest // (NX // XLO)
    source = core * HALF + (y * NX + x_hi * XLO + x_lo) * ROWS + k * NZ + z
    return jnp.where(iota(shape, 0) == source, 1.0, 0.0).astype(BF16)


def wanted_rows(ids_ref, count):
    y, x, z, core = my_place()
    base = core * HALF + (y * NX + x) * ROWS + z
    lane, sub = iota((8, count), 1), iota((8, count), 0)
    wanted = base + NZ * jnp.where(sub == 0, ids_ref[0], ids_ref[1])
    return jnp.where((lane == wanted) & (sub < 2), 1.0, 0.0)


def form_system(v, split_ref):
    count, width = v.shape
    gram = mm_t(v, v) * (1.0 / count)
    eye = iota((count, count), 0) == iota((count, count), 1)
    diagonal = jnp.sum(jnp.where(eye, gram, 0.0), axis=0, keepdims=True)
    damping = damp_ratio * jnp.sum(diagonal, axis=1, keepdims=True) / width
    system = gram + jnp.where(eye, damping, 0.0)
    for i, piece in enumerate(pieces(system)):
        split_ref[:, i * count : (i + 1) * count] = piece.astype(BF16)
    return system, damping, diagonal + damping, eye


def times_system(p, split_ref, used=3):
    count = split_ref.shape[0]
    product = unstacked(mm(stacked(p), split_ref[:, 0 : used * count]))
    total = product[:, 0:count]
    for i in range(1, used):
        total = total + product[:, i * count : (i + 1) * count]
    return total


def scores_of(sol, v, t, order):
    mixed = unstacked(mm(stacked(sol), v))
    raw = unstacked(mm_t(stacked(mixed), t)) * (1.0 / math.sqrt(v.shape[1]))
    return unstacked(mm(stacked(raw), order))


def approximate_inverse(v, split_ref, m_ref, before_last):
    count = v.shape[0]
    system, low, _, eye = form_system(v, split_ref)
    high = split_ref[:, 0:count]
    square = mm(high, high)
    top = jnp.max(jnp.sum(jnp.abs(square), axis=0, keepdims=True), axis=1, keepdims=True)
    top = jnp.sqrt(top) * 1.02
    centre = 2.0 / (top + low)
    t = (top + low) / (top - low)
    t2 = 2.0 * t * t - 1.0
    c = 2.0 * t * t / t2 * centre
    m = jnp.where(eye, 2.0 * c, 0.0) - (c * centre) * system
    am = (2.0 * c) * system - (c * centre) * square
    for i in range(DOUBLINGS):
        t = t2
        t2 = 2.0 * t * t - 1.0
        c = 2.0 * t * t / t2
        if i == DOUBLINGS - 1:
            before_last()
        rounded = m.astype(BF16)
        if i > 0:
            am = mm(high, rounded)
        m = c * (2.0 * m - mm(rounded, am.astype(BF16)))
    m_ref[...] = m.astype(BF16)
    return top


def refined(rhs, top, split_ref, m_ref):
    def precondition(r):
        return mm(jnp.concatenate([r, jnp.zeros_like(r)], axis=0).astype(BF16), m_ref[...])[0:8]

    sol = precondition(rhs)
    for i in range(REFINEMENTS):
        sol = sol + precondition(rhs - times_system(sol, split_ref, 2 if i < 2 else 3))
    return sol


def excess_of(sol, rhs, top, split_ref):
    res = rhs - times_system(sol, split_ref)
    return inner(res, res) - (LAST_BITS * top) * (LAST_BITS * top) * inner(sol, sol)


def main_kernel(
    ids_hbm, acts_hbm, cot_hbm, w_in_hbm, w_out_hbm, proj_in_hbm, proj_out_hbm, test_hbm,
    raw_ref, check_ref, v_all, t_all,
    ids_ref, acts, cot, w_in, w_out, proj_in, proj_out, test,
    tiles, line, plane, v_cross, t_cross, wide, split_ref, m_ref, order_ref,
    load_sem, in_sem, out_sem,
    line_send, line_recv, plane_send, plane_recv,
    rows_send, rows_recv, cross_send, cross_recv, core_send, core_recv,
):
    y, x, z, core = my_place()
    block = w_in.shape[1] // PARTS
    tokens = acts.shape[0] * acts.shape[1]

    small = [
        pltpu.make_async_copy(src, dst, load_sem.at[i])
        for i, (src, dst) in enumerate(
            (
                (acts_hbm, acts),
                (proj_in_hbm, proj_in),
                (cot_hbm, cot),
                (proj_out_hbm, proj_out),
                (test_hbm, test),
                (ids_hbm, ids_ref),
            )
        )
    ]
    loads_in, loads_out = [], []
    for i in range(PARTS):
        part = pl.ds(i * block, block)
        loads_in.append(
            pltpu.make_async_copy(w_in_hbm.at[:, part], w_in.at[:, part], in_sem.at[i])
        )
        loads_out.append(
            pltpu.make_async_copy(w_out_hbm.at[part], w_out.at[part], out_sem.at[i])
        )
    small[4].start()
    small[0].start()
    small[1].start()
    loads_in[0].start()
    small[2].start()
    loads_out[0].start()
    small[3].start()
    for i in range(1, PARTS):
        loads_in[i].start()
        loads_out[i].start()
    small[5].start()

    barrier = pltpu.get_barrier_semaphore()
    on_line = [device_at(y, x, lax.rem(z + d, NZ), core) for d in LINE_STEPS]
    on_plane = [
        device_at(lax.rem(y + dy, NY), lax.rem(x + dx, NX), z, core) for dy, dx in PLANE_STEPS
    ]
    partner = device_at(y, x, z, 1 - core)
    targets = on_line + on_plane + [partner]
    for target in targets:
        pl.semaphore_signal(barrier, inc=1, device_id=target, device_id_type=MESH)

    fulls, crosses = (v_all, t_all), (v_cross, t_cross)
    mine = y * NX + x

    def send(src, dst, send_sem, recv_sem, target):
        pltpu.make_async_remote_copy(
            src_ref=src,
            dst_ref=dst,
            send_sem=send_sem,
            recv_sem=recv_sem,
            device_id=target,
            device_id_type=MESH,
        ).start()

    def await_bytes(ref, sem):
        pltpu.make_async_copy(ref, ref, sem).wait()

    def start_tiles(a, tile):
        tiles[a] = tile
        for target in on_line:
            send(tiles.at[a], line.at[a, z], line_send.at[a], line_recv.at[a], target)
        for target in on_plane:
            send(tiles.at[a], plane.at[a, mine], plane_send.at[a], plane_recv.at[a], target)
        line[a, z] = tile
        plane[a, mine] = tile

    def start_blocks(a):
        full = fulls[a]
        await_bytes(line.at[a, pl.ds(0, NZ - 1)], line_recv.at[a])
        wide[0 : NZ * TILE, :] = line[a].reshape(NZ * TILE, 128).astype(F32)
        for c in range(ACROSS[a]):
            both = [wide[pl.ds(k * CHUNKS + c, NZ, stride=TILE), :] for k in range(2)]
            full[core, mine, :, c * 128 : (c + 1) * 128] = jnp.concatenate(both, axis=0).astype(
                BF16
            )
        rows = full.at[core, mine, :, pl.ds(0, SPLIT[a])]
        for (dy, _), target in zip(PLANE_STEPS, on_plane):
            send(rows, rows, rows_send.at[a], rows_recv.at[dy if a == 0 else NY], target)
        await_bytes(plane.at[a, pl.ds(0, STEPS)], plane_recv.at[a])
        wide[...] = plane[a].reshape(PLANE * TILE, 128).astype(F32)
        for c in range(ACROSS[a], CHUNKS):
            both = [wide[pl.ds(k * CHUNKS + c, PLANE, stride=TILE), :] for k in range(2)]
            at = c - ACROSS[a]
            crosses[a][z, :, at * 128 : (at + 1) * 128] = jnp.concatenate(both, axis=0).astype(BF16)
        rows = crosses[a].at[z]
        for target in on_line:
            send(rows, rows, cross_send.at[a], cross_recv.at[a], target)

    def place_cross(a):
        await_bytes(crosses[a].at[pl.ds(0, NZ - 1)], cross_recv.at[a])
        for c in range(ACROSS[a], CHUNKS):
            at = c - ACROSS[a]
            columns = crosses[a][:, :, at * 128 : (at + 1) * 128]
            wide[...] = columns.reshape(NZ * 2 * PLANE, 128).astype(F32)
            for p in range(PLANE):
                both = [wide[pl.ds(k * PLANE + p, NZ, stride=2 * PLANE), :] for k in range(2)]
                fulls[a][core, p, :, c * 128 : (c + 1) * 128] = jnp.concatenate(
                    both, axis=0
                ).astype(BF16)

    def core_copy(i, rows):
        return pltpu.make_async_remote_copy(
            src_ref=rows,
            dst_ref=rows,
            send_sem=core_send.at[i],
            recv_sem=core_recv.at[i],
            device_id=partner,
            device_id_type=MESH,
        )

    small[4].wait()
    t_tile = spread(wide.at[pl.ds(0, TILE)], test[...].astype(F32))
    pl.semaphore_wait(barrier, len(targets))
    start_tiles(1, t_tile)

    small[0].wait()
    small[1].wait()
    left = left_pieces(acts[...].reshape(tokens, -1), proj_in[...])
    small[2].wait()
    small[3].wait()
    right = None
    for i in range(PARTS):
        loads_in[i].wait()
        loads_out[i].wait()
        part = slice(i * block, (i + 1) * block)
        preact = mm(acts[...].reshape(tokens, -1), w_in[:, part])
        backprop = mm_t(cot[...].reshape(tokens, -1), w_out[part])
        deltas = (backprop * gelu_slope(preact)).astype(BF16)
        term = mm_t(deltas, proj_out[:, part])
        right = term if right is None else right + term
    outer = outer_tile(left, right, proj_in.shape[0])
    start_tiles(0, (outer * (1.0 / math.sqrt(acts.shape[1]))).astype(BF16))
    start_blocks(0)
    order_ref[...] = target_order(order_ref.shape)

    copies = []

    def forward(i, rows):
        copies.append(core_copy(i, rows))
        copies[-1].start()

    for dy in (0, 1, 3, 2):
        if dy == 2:
            place_cross(0)
            forward(0, v_all.at[core, :, :, pl.ds(SPLIT[0], (CHUNKS - ACROSS[0]) * 128)])
        first = lax.rem(y + NY - dy, NY) * NX
        count = NX - (dy == 0)
        await_bytes(v_all.at[core, pl.ds(first, count), :, pl.ds(0, SPLIT[0])], rows_recv.at[dy])
        forward(dy + 1, v_all.at[core, pl.ds(first, NX), :, pl.ds(0, SPLIT[0])])
        if dy == 0:
            start_blocks(1)
    for copy in copies:
        copy.wait_recv()

    small[5].wait()
    v = v_all[...].reshape(2 * HALF, -1)

    def complete_tests():
        place_cross(1)
        await_bytes(t_all.at[core, pl.ds(0, STEPS), :, pl.ds(0, SPLIT[1])], rows_recv.at[NY])
        forward(NY + 1, t_all.at[core])

    top = approximate_inverse(v, split_ref, m_ref, complete_tests)
    rhs = wanted_rows(ids_ref, 2 * HALF)
    sol = refined(rhs, top, split_ref, m_ref)
    copies[-1].wait_recv()
    raw = scores_of(sol, v, t_all[...].reshape(2 * HALF, -1), order_ref[...])
    excess = excess_of(sol, rhs, top, split_ref)
    raw_ref[...] = raw[0:2]
    check_ref[...] = jnp.broadcast_to(excess, check_ref.shape)
    for a in range(2):
        await_bytes(line.at[a, pl.ds(0, NZ - 1)], line_send.at[a])
        await_bytes(plane.at[a, pl.ds(0, STEPS)], plane_send.at[a])
        await_bytes(fulls[a].at[core, pl.ds(0, STEPS), :, pl.ds(0, SPLIT[a])], rows_send.at[a])
        await_bytes(crosses[a].at[pl.ds(0, NZ - 1)], cross_send.at[a])
    for copy in copies:
        copy.wait_send()


def finish_kernel(ids_ref, raw_ref, check_ref, v_ref, t_ref, out_hbm, late_ref, split_ref, sem):
    copy = pltpu.make_async_copy(raw_ref, out_hbm, sem)
    copy.start()
    excess = check_ref[...]
    fine = jnp.min(jnp.where(excess <= 0.0, 1.0, 0.0))
    copy.wait()

    @pl.when(fine < 1.0)
    def _():
        count = 2 * HALF
        v, t = v_ref[...].reshape(count, -1), t_ref[...].reshape(count, -1)
        _, _, diagonal, _ = form_system(v, split_ref)
        rhs = wanted_rows(ids_ref, count)
        scale = 1.0 / diagonal

        def ratio(a, b):
            return jnp.where(b > 0.0, a / jnp.where(b > 0.0, b, 1.0), 0.0)

        def unfinished(state):
            step, _, _, _, rz = state
            return (step < MOST_STEPS) & (jnp.max(rz - goal) > 0.0)

        def advance(state):
            step, sol, res, p, rz = state
            q = times_system(p, split_ref)
            alpha = ratio(rz, inner(p, q))
            sol = sol + alpha * p
            res = res - alpha * q
            zed = res * scale
            new = inner(res, zed)
            p = zed + ratio(new, rz) * p
            return step + 1, sol, res, p, new

        zed = rhs * scale
        rz = inner(rhs, zed)
        goal = rz * 1e-12
        state = (jnp.int32(0), jnp.zeros_like(rhs), rhs, zed, rz)
        sol = lax.while_loop(unfinished, advance, state)[1]
        late_ref[...] = scores_of(sol, v, t, target_order((count, count)))[0:2]
        again = pltpu.make_async_copy(late_ref, out_hbm, sem)
        again.start()
        again.wait()


def body(
    clip_acts, clip_cotangents, weight_in, weight_out, proj_in, proj_out, test_grads, clip_ids
):
    width = proj_in.shape[1] * proj_out.shape[1]
    proj_in, proj_out = proj_in.T, proj_out.T
    count = 2 * HALF
    full = jax.ShapeDtypeStruct((2, PLANE, ROWS, width), BF16)
    vmem = pl.BlockSpec(memory_space=pltpu.VMEM)
    smem = pl.BlockSpec(memory_space=pltpu.SMEM)
    hbm = pl.BlockSpec(memory_space=pl.ANY)
    dma = pltpu.SemaphoreType.DMA

    def like(array):
        return pltpu.VMEM(array.shape, array.dtype)

    raw, check, v_all, t_all = pl.pallas_call(
        main_kernel,
        out_shape=(
            pltpu.VMEM((2, count), F32),
            pltpu.VMEM((8, 128), F32),
            pltpu.VMEM(full.shape, BF16),
            pltpu.VMEM(full.shape, BF16),
        ),
        in_specs=[hbm] * 8,
        out_specs=(vmem, vmem, vmem, vmem),
        scratch_shapes=[
            pltpu.SMEM(clip_ids.shape, clip_ids.dtype),
            like(clip_acts),
            like(clip_cotangents),
            like(weight_in),
            like(weight_out),
            like(proj_in),
            like(proj_out),
            like(test_grads),
            pltpu.VMEM((2, TILE, 128), BF16),
            pltpu.VMEM((2, NZ, TILE, 128), BF16),
            pltpu.VMEM((2, PLANE, TILE, 128), BF16),
            pltpu.VMEM((NZ, 2 * PLANE, (CHUNKS - ACROSS[0]) * 128), BF16),
            pltpu.VMEM((NZ, 2 * PLANE, (CHUNKS - ACROSS[1]) * 128), BF16),
            pltpu.VMEM((PLANE * TILE, 128), F32),
            pltpu.VMEM((count, 3 * count), BF16),
            pltpu.VMEM((count, count), BF16),
            pltpu.VMEM((count, count), BF16),
            dma((6,)),
            dma((PARTS,)),
            dma((PARTS,)),
            dma((2,)),
            dma((2,)),
            dma((2,)),
            dma((2,)),
            dma((2,)),
            dma((NY + 1,)),
            dma((2,)),
            dma((2,)),
            dma((NY + 2,)),
            dma((NY + 2,)),
        ],
        compiler_params=pltpu.CompilerParams(
            collective_id=0, has_side_effects=True, vmem_limit_bytes=56 << 20
        ),
    )(
        clip_ids,
        clip_acts,
        clip_cotangents,
        weight_in,
        weight_out,
        proj_in,
        proj_out,
        test_grads,
    )
    return pl.pallas_call(
        finish_kernel,
        out_shape=jax.ShapeDtypeStruct((2, count), F32),
        in_specs=[smem, vmem, vmem, vmem, vmem],
        out_specs=hbm,
        scratch_shapes=[
            pltpu.VMEM((2, count), F32),
            pltpu.VMEM((count, 3 * count), BF16),
            dma,
        ],
        compiler_params=pltpu.CompilerParams(vmem_limit_bytes=32 << 20),
    )(clip_ids, *[pltpu.with_memory_space_constraint(r, pltpu.VMEM) for r in (raw, check, v_all, t_all)])


def solution(mesh):
    in_specs = (
        P(("clip", "proj"), None, None),
        P(("clip", "proj"), None, None),
        P(),
        P(),
        P(),
        P(),
        P(("clip", "proj"), None),
        P(("clip", "proj")),
    )
    out_specs = P(("clip", "proj"), None)
    return jax.shard_map(body, mesh=mesh, in_specs=in_specs, out_specs=out_specs, check_vma=False)
```
